32 devices in a mesh: grp: 4 (over x, core), dev: 8 (over z, y).
Axes of the slice: x: 2, y: 2, z: 4, core: 2. Of those that a mesh axis runs over, the one named last changes fastest.
Arguments:
- amplitudes: float32 [2, 2048, 128], P(None, ('grp', 'dev')), may hold values from -6 to 6
- couplings: float32 [2, 12, 128, 128], replicated, may hold values from -1 to 1, as said below
- block_index: int32 [128], P(('grp', 'dev')), may hold values from 0 to 11
- bond_map: int32 [5], replicated, may hold values from 0 to 6
- bond_strength: float32 [5], replicated, may hold values from 0.05 to 0.5
- drive_amplitude: float32 [4, 5], replicated, may hold values from 0.05 to 0.5
Outputs:
- new_amplitudes: float32 [2, 2048, 128], P(None, ('grp', 'dev'))
The draws below stay inside these ranges and needn't reach their ends.
Inputs may be any that keep to these rules, and one draw needn't show every extreme that they name: couplings[0][k] is symmetric and couplings[1][k] antisymmetric, so each listed coupling is Hermitian.
All inputs are finite; a program needn't handle non-finite values.
Results may differ from the reference program's by a relative error of at most 0.00007.
Values sent between devices are 32-bit elements; how exact they have to be, the bound alone decides.
A program may use at most 64 MiB of HBM per device.

```python
import math
import jax
import jax.numpy as jnp
from jax import lax

COLS = 128
KINDS = 12
BROWS = 16
SECTIONS = 4
ROWS = 64
COL_SPINS = 7
LEAD = 5
NBLK = 4
TOTAL_ROWS = 2048
TOTAL_BLOCKS = 128


def draw_couplings(key, part):
    first_key, second_key = jax.random.split(jax.random.fold_in(key, 7))
    shape = (KINDS, COLS, COLS)
    sym_base = jax.random.uniform(first_key, shape, jnp.float32, -1.0, 1.0)
    anti_base = jax.random.uniform(second_key, shape, jnp.float32, -1.0, 1.0)
    scale = 1.2 / COLS ** 0.5
    real_block = 0.5 * scale * (sym_base + jnp.swapaxes(sym_base, 1, 2))
    imag_block = 0.5 * scale * (anti_base - jnp.swapaxes(anti_base, 1, 2))
    return jnp.stack([real_block, imag_block]).astype(jnp.float32)


def plant(entries, own_key, low, top_value):
    shape = entries.shape
    spot = [jax.random.randint(jax.random.fold_in(own_key, axis), (), 0, shape[axis]) for axis in range(len(shape))]
    entries = entries.at[tuple(spot)].set(low)
    longest = shape.index(max(shape))
    spot[longest] = (spot[longest] + 1) % shape[longest]
    return entries.at[tuple(spot)].set(top_value)


def block_levels(rng, shape, cuts, low, top_value):
    loudness = 1.0
    for axis_at, parts in cuts:
        steps = jax.random.uniform(jax.random.fold_in(jax.random.fold_in(rng, 6), axis_at), (parts,), jnp.float32, low / len(cuts), top_value / len(cuts))
        loudness = loudness * jnp.repeat(jnp.exp(steps), shape[axis_at] // parts).reshape((-1,) + (1,) * (len(shape) - 1 - axis_at))
    return loudness


def normal_values(stream_key, extent, width, reach, shards=(), held_as=jnp.bfloat16):
    values = width * jax.random.normal(stream_key, extent, jnp.float32)
    if shards:
        values = values * block_levels(stream_key, extent, shards, -0.22, 0.18)
    return jnp.clip(values, -reach, reach).astype(held_as)


def setup_inputs(seed: int = 0) -> dict:
    keys = jax.random.split(jax.random.key(seed), 7)
    amplitudes = normal_values(keys[0], (2, TOTAL_ROWS, COLS), 1.0, 6.0, ((1, 32),), jnp.float32)
    couplings = draw_couplings(jax.random.fold_in(keys[6], 71), 0)
    block_index = plant(jax.random.randint(keys[2], (TOTAL_BLOCKS,), 0, KINDS), jax.random.fold_in(keys[2], 1), 0, KINDS - 1).astype(jnp.int32)
    bond_map = plant(jax.random.randint(keys[3], (LEAD,), 0, COL_SPINS), jax.random.fold_in(keys[3], 1), 0, COL_SPINS - 1).astype(jnp.int32)
    bond_strength = jnp.clip(jnp.exp(jax.random.uniform(keys[4], (LEAD,), jnp.float32, math.log(0.05), math.log(0.5))), 0.05, 0.5)
    drive_amplitude = jnp.clip(jnp.exp(jax.random.uniform(keys[5], (SECTIONS, LEAD), jnp.float32, math.log(0.05), math.log(0.5))), 0.05, 0.5)
    return {"amplitudes": amplitudes, "couplings": couplings, "block_index": block_index, "bond_map": bond_map, "bond_strength": bond_strength, "drive_amplitude": drive_amplitude}


STEP_SIZE = 0.5
HIGHEST = lax.Precision.HIGHEST


def coupled(real_part, imag_part, couplings, block_index):
    dev_total = TOTAL_ROWS // ROWS
    real_four = real_part.reshape(dev_total, NBLK, BROWS, COLS)
    imag_four = imag_part.reshape(dev_total, NBLK, BROWS, COLS)
    kind_rows = block_index.reshape(dev_total, NBLK)

    def one_device(items):
        block_real, block_imag, kind_now = items
        mat_real = jnp.take(couplings[0], kind_now, axis=0)
        mat_imag = jnp.take(couplings[1], kind_now, axis=0)

        def apply_mat(field, matrix):
            return jnp.einsum("brj,bcj->brc", field, matrix, precision=HIGHEST)

        out_real = apply_mat(block_real, mat_real) - apply_mat(block_imag, mat_imag)
        out_imag = apply_mat(block_imag, mat_real) + apply_mat(block_real, mat_imag)
        return out_real, out_imag

    out_real, out_imag = lax.map(one_device, (real_four, imag_four, kind_rows))
    return out_real.reshape(TOTAL_ROWS, COLS), out_imag.reshape(TOTAL_ROWS, COLS)


def flip_leading(field, lead_spin):
    outer_count = TOTAL_ROWS // (ROWS * 2 ** (lead_spin + 1))
    folded = field.reshape(outer_count, 2, ROWS * 2 ** lead_spin, COLS)
    return folded[:, ::-1].reshape(TOTAL_ROWS, COLS)


def evaluate_field(real_part, imag_part, couplings, block_index, bond_map, bond_strength, drive_row):
    out_real, out_imag = coupled(real_part, imag_part, couplings, block_index)
    columns = jnp.arange(COLS, dtype=jnp.int32)
    devices = jnp.arange(TOTAL_ROWS, dtype=jnp.int32) // ROWS
    for lead_spin in range(LEAD):
        target = bond_map[lead_spin]
        shuffle = jnp.bitwise_xor(columns, jnp.left_shift(jnp.int32(1), target)).astype(jnp.int32)
        sign_col = (1 - 2 * jnp.bitwise_and(jnp.right_shift(columns, target), 1)).astype(jnp.float32)[None, :]
        sign_lead = (1 - 2 * jnp.bitwise_and(jnp.right_shift(devices, lead_spin), 1)).astype(jnp.float32)[:, None]
        part_real = flip_leading(real_part, lead_spin)
        part_imag = flip_leading(imag_part, lead_spin)
        strength = bond_strength[lead_spin]
        drive_now = drive_row[lead_spin]
        out_real = out_real + strength * (sign_lead * sign_col * real_part + jnp.take(part_real, shuffle, axis=1)) + drive_now * part_real
        out_imag = out_imag + strength * (sign_lead * sign_col * imag_part + jnp.take(part_imag, shuffle, axis=1)) + drive_now * part_imag
    return out_imag, -out_real


def runge_kutta(real_part, imag_part, evaluate):
    half_step = 0.5 * STEP_SIZE
    slope_one = evaluate(0, real_part, imag_part)
    slope_two = evaluate(1, real_part + half_step * slope_one[0], imag_part + half_step * slope_one[1])
    slope_three = evaluate(2, real_part + half_step * slope_two[0], imag_part + half_step * slope_two[1])
    slope_four = evaluate(3, real_part + STEP_SIZE * slope_three[0], imag_part + STEP_SIZE * slope_three[1])
    factor = STEP_SIZE / 6.0
    new_real = real_part + factor * (slope_one[0] + 2.0 * slope_two[0] + 2.0 * slope_three[0] + slope_four[0])
    new_imag = imag_part + factor * (slope_one[1] + 2.0 * slope_two[1] + 2.0 * slope_three[1] + slope_four[1])
    return new_real, new_imag


def reference(amplitudes, couplings, block_index, bond_map, bond_strength, drive_amplitude):
    def evaluate(section, first, second):
        return evaluate_field(first, second, couplings, block_index, bond_map, bond_strength, drive_amplitude[section])

    new_real, new_imag = runge_kutta(amplitudes[0], amplitudes[1], evaluate)
    return jnp.stack([new_real, new_imag])
```

```python
import functools

import jax
import jax.numpy as jnp
from jax import lax
from jax.experimental import pallas as pl
from jax.experimental.pallas import tpu as pltpu
from jax.sharding import PartitionSpec as P

BROWS = 16


STEP_SIZE = 0.5
HIGHEST = lax.Precision.HIGHEST


def swapped(shard, axis, distance):
    return lax.ppermute(shard, axis, [(i, i ^ 1 << distance) for i in range(lax.axis_size(axis))])


def spin_count(number):
    return number.bit_length() - 1


def flip_group(real_part, imag_part, bit_now):
    return swapped((real_part, imag_part), "grp", bit_now)


def coupled(real_part, imag_part, table, row_kind, kinds):
    row_count, col_count = real_part.shape
    product = jnp.dot(
        jnp.concatenate([real_part, imag_part], 0),
        table,
        precision=HIGHEST,
        preferred_element_type=jnp.float32,
    )
    extent = kinds * col_count
    left_part = product[:, :extent]
    right_part = product[:, extent:]
    all_real = left_part[:row_count] - right_part[row_count:]
    all_imag = left_part[row_count:] + right_part[:row_count]
    select = (row_kind[:, None] == jnp.arange(kinds, dtype=jnp.int32)[None, :]).astype(jnp.float32)[
        :, :, None
    ]
    out_real = jnp.sum(all_real.reshape(row_count, kinds, col_count) * select, axis=1)
    out_imag = jnp.sum(all_imag.reshape(row_count, kinds, col_count) * select, axis=1)
    return (out_real, out_imag)


def evaluate_field(
    real_part, imag_part, table, row_kind, kinds, bond_map, bond_strength, drive_row
):
    out_real, out_imag = coupled(real_part, imag_part, table, row_kind, kinds)
    row_count, col_count = real_part.shape
    dev_bits = spin_count(lax.axis_size("dev"))
    grp_bits = spin_count(lax.axis_size("grp"))
    columns = jnp.arange(col_count, dtype=jnp.int32)
    for lead_spin in range(dev_bits + grp_bits):
        target = bond_map[lead_spin]
        shuffle = jnp.bitwise_xor(columns, jnp.left_shift(jnp.int32(1), target))
        sign_col = (1 - 2 * jnp.bitwise_and(jnp.right_shift(columns, target), 1)).astype(
            jnp.float32
        )[None, :]
        if lead_spin < dev_bits:
            part_real, part_imag = swapped((real_part, imag_part), "dev", lead_spin)
            sign_lead = (
                1 - 2 * jnp.bitwise_and(jnp.right_shift(lax.axis_index("dev"), lead_spin), 1)
            ).astype(jnp.float32)
        else:
            part_real, part_imag = flip_group(real_part, imag_part, lead_spin - dev_bits)
            sign_lead = (
                1
                - 2
                * jnp.bitwise_and(jnp.right_shift(lax.axis_index("grp"), lead_spin - dev_bits), 1)
            ).astype(jnp.float32)
        strength = bond_strength[lead_spin]
        drive_now = drive_row[lead_spin]
        out_real = (
            out_real
            + strength * (sign_lead * sign_col * real_part + jnp.take(part_real, shuffle, axis=1))
            + drive_now * part_real
        )
        out_imag = (
            out_imag
            + strength * (sign_lead * sign_col * imag_part + jnp.take(part_imag, shuffle, axis=1))
            + drive_now * part_imag
        )
    return (out_imag, -out_real)


def runge_kutta(real_part, imag_part, evaluate):
    half_step = 0.5 * STEP_SIZE
    slope_one = evaluate(0, real_part, imag_part)
    slope_two = evaluate(
        1, real_part + half_step * slope_one[0], imag_part + half_step * slope_one[1]
    )
    slope_three = evaluate(
        2, real_part + half_step * slope_two[0], imag_part + half_step * slope_two[1]
    )
    slope_four = evaluate(
        3, real_part + STEP_SIZE * slope_three[0], imag_part + STEP_SIZE * slope_three[1]
    )
    factor = STEP_SIZE / 6.0
    new_real = real_part + factor * (
        slope_one[0] + 2.0 * slope_two[0] + 2.0 * slope_three[0] + slope_four[0]
    )
    new_imag = imag_part + factor * (
        slope_one[1] + 2.0 * slope_two[1] + 2.0 * slope_three[1] + slope_four[1]
    )
    return (new_real, new_imag)


def body(amplitudes, couplings, block_index, bond_map, bond_strength, drive_amplitude):
    kinds = couplings.shape[1]
    col_count = couplings.shape[2]
    table_real = jnp.transpose(couplings[0], (2, 0, 1)).reshape(col_count, kinds * col_count)
    table_imag = jnp.transpose(couplings[1], (2, 0, 1)).reshape(col_count, kinds * col_count)
    table = jnp.concatenate([table_real, table_imag], 1)
    real_part = amplitudes[0]
    imag_part = amplitudes[1]
    row_count = real_part.shape[0]
    row_kind = jnp.repeat(block_index, BROWS, total_repeat_length=row_count)

    def evaluate(section, first, second):
        return evaluate_field(
            first, second, table, row_kind, kinds, bond_map, bond_strength, drive_amplitude[section]
        )

    new_real, new_imag = runge_kutta(real_part, imag_part, evaluate)
    return jnp.stack([new_real, new_imag])


SUBLANES = 8
MESH = pl.DeviceIdType.MESH


def flipped(field, stride):
    row_count, col_count = field.shape
    if stride >= SUBLANES:
        folded = field.reshape(row_count // (2 * stride), 2, stride, col_count)
        return jnp.concatenate([folded[:, 1:], folded[:, :1]], 1).reshape(row_count, col_count)
    tiles = field.reshape(row_count // SUBLANES, SUBLANES, col_count)
    down = pltpu.roll(tiles, stride, 1)
    if 2 * stride < SUBLANES:
        row = lax.broadcasted_iota(jnp.int32, tiles.shape, 1)
        up = pltpu.roll(tiles, SUBLANES - stride, 1)
        down = jnp.where(row // stride % 2 == 1, down, up)
    return down.reshape(row_count, col_count)


def step_kernel(
    sizes,
    kind_ref,
    bond_ref,
    strength_ref,
    drive_ref,
    amp_ref,
    coup_ref,
    out_ref,
    stage,
    held,
    table,
    weight_high,
    weight_low,
    masks,
    diagonal,
    field,
    total,
    final,
    local_sem,
    send_sem,
    recv_sem,
):
    grp_size, dev_size, block_rows = sizes
    devices = grp_size * dev_size
    lead = spin_count(devices)
    row_count, col_count = amp_ref.shape[1:]
    kinds = coup_ref.shape[1]
    sections = drive_ref.shape[0]
    share = row_count // devices
    others = (devices - 1) * share
    me = lax.axis_index("grp") * dev_size + lax.axis_index("dev")

    def place(hop):
        other = lax.rem(me + hop, devices)
        return other, (other // dev_size, lax.rem(other, dev_size))

    load_table = pltpu.make_async_copy(coup_ref, table, local_sem.at[0])
    load_table.start()
    barrier = pltpu.get_barrier_semaphore()

    def greet(hop, carry):
        pl.semaphore_signal(barrier, inc=1, device_id=place(hop)[1], device_id_type=MESH)
        return carry

    lax.fori_loop(1, devices, greet, 0)
    stage[0] = amp_ref[0]
    stage[1] = amp_ref[1]
    for block in range(row_count // block_rows):
        kind = kind_ref[block].astype(jnp.float32)
        stage[2, block * block_rows : (block + 1) * block_rows] = jnp.full(
            (block_rows, col_count), kind, jnp.float32
        )
    pl.semaphore_wait(barrier, devices - 1)

    mine = pl.ds(me * share, share)

    def exchange(source, target, phase):
        def send(hop, carry):
            other, where = place(hop)
            pltpu.make_async_remote_copy(
                src_ref=source.at[:, pl.ds(other * share, share)],
                dst_ref=target.at[:, mine],
                send_sem=send_sem.at[phase],
                recv_sem=recv_sem.at[phase],
                device_id=where,
                device_id_type=MESH,
            ).start()
            return carry

        lax.fori_loop(1, devices, send, 0)
        own = pltpu.make_async_copy(
            source.at[:, mine], target.at[:, mine], local_sem.at[1 + phase]
        )
        own.start()
        return own

    def finish(source, target, phase, own):
        own.wait()
        sent = source.at[:, pl.ds(0, others)]
        pltpu.make_async_copy(sent, sent, send_sem.at[phase]).wait()
        came = target.at[:, pl.ds(0, others)]
        pltpu.make_async_copy(came, came, recv_sem.at[phase]).wait()

    own = exchange(stage, held, 0)
    load_table.wait()

    def split(kind, carry):
        real = table[0, kind]
        imag = table[1, kind]
        real_high = real.astype(jnp.bfloat16)
        imag_high = imag.astype(jnp.bfloat16)
        real_low = (real - real_high.astype(jnp.float32)).astype(jnp.bfloat16)
        imag_low = (imag - imag_high.astype(jnp.float32)).astype(jnp.bfloat16)
        first = pl.ds(pl.multiple_of(kind * 2 * col_count, 2 * col_count), col_count)
        second = pl.ds(pl.multiple_of(kind * 2 * col_count, col_count) + col_count, col_count)
        for weight, real_now, imag_now in (
            (weight_high, real_high, imag_high),
            (weight_low, real_low, imag_low),
        ):
            weight[first, :col_count] = -imag_now
            weight[first, col_count:] = -real_now
            weight[second, :col_count] = real_now
            weight[second, col_count:] = -imag_now
        return carry

    lax.fori_loop(0, kinds, split, 0)

    row = lax.broadcasted_iota(jnp.int32, (row_count, col_count), 0)
    column = lax.broadcasted_iota(jnp.int32, (row_count, col_count), 1)
    diag = jnp.zeros((row_count, col_count), jnp.float32)
    shuffles = []
    for spin in range(lead):
        target = bond_ref[spin]
        shuffles.append(jnp.bitwise_xor(column, jnp.left_shift(jnp.int32(1), target)))
        parity = jnp.bitwise_xor(
            jnp.right_shift(row // share, spin), jnp.right_shift(column, target)
        )
        sign = (1 - 2 * jnp.bitwise_and(parity, 1)).astype(jnp.float32)
        diag = diag + strength_ref[spin] * sign
    diagonal[...] = diag

    finish(stage, held, 0, own)
    kind_rows = held[2]
    for kind in range(kinds):
        masks[kind] = (kind_rows == float(kind)).astype(jnp.float32).astype(jnp.bfloat16)
    field[...] = held[:2]
    total[...] = jnp.zeros_like(total)

    def section(now, carry):
        both = jnp.concatenate([field[0], field[1]], 1)
        high = both.astype(jnp.bfloat16)
        low = (both - high.astype(jnp.float32)).astype(jnp.bfloat16)
        high_parts = []
        low_parts = []
        for kind in range(kinds):
            mask = jnp.concatenate([masks[kind], masks[kind]], 1)
            high_parts.append(high * mask)
            low_parts.append(low * mask)
        high_all = jnp.concatenate(high_parts, 1)
        low_all = jnp.concatenate(low_parts, 1)
        main = jnp.dot(
            jnp.concatenate([high_all, low_all], 0),
            weight_high[...],
            preferred_element_type=jnp.float32,
        )
        rest = jnp.dot(high_all, weight_low[...], preferred_element_type=jnp.float32)
        product = main[:row_count] + (main[row_count:] + rest)
        leads = []
        for part in range(2):
            here = field[part]
            other = diagonal[...] * here
            for spin in range(lead):
                there = flipped(here, share << spin)
                moved = jnp.take_along_axis(
                    there, shuffles[spin], axis=1, mode="promise_in_bounds"
                )
                other = other + strength_ref[spin] * moved + drive_ref[now, spin] * there
            leads.append(other)
        slope = (product[:, :col_count] + leads[1], product[:, col_count:] - leads[0])
        edge = (now == 0) | (now == sections - 1)
        weight = jnp.where(edge, 1.0, 2.0)
        step = jnp.where(now == sections - 2, STEP_SIZE, 0.5 * STEP_SIZE)
        for part in range(2):
            total[part] = total[part] + weight * slope[part]
            field[part] = held[part] + step * slope[part]
        return carry

    lax.fori_loop(0, sections, section, 0)
    final[...] = held[:2] + (STEP_SIZE / 6.0) * total[...]
    own = exchange(final, out_ref, 1)
    finish(final, out_ref, 1, own)


def body_by_rows(
    sizes, amplitudes, couplings, block_index, bond_map, bond_strength, drive_amplitude
):
    parts, row_count, col_count = amplitudes.shape
    kinds = couplings.shape[1]
    block_rows = row_count // block_index.shape[0]
    half = (parts, row_count, col_count)
    smem = pl.BlockSpec(memory_space=pltpu.SMEM)
    vmem = pl.BlockSpec(memory_space=pltpu.VMEM)
    weight = pltpu.VMEM((kinds * 2 * col_count, 2 * col_count), jnp.bfloat16)
    return pl.pallas_call(
        functools.partial(step_kernel, (*sizes, block_rows)),
        out_shape=jax.ShapeDtypeStruct(half, jnp.float32),
        in_specs=[smem, smem, smem, smem, vmem, pl.BlockSpec(memory_space=pl.ANY)],
        out_specs=vmem,
        scratch_shapes=[
            pltpu.VMEM((parts + 1, row_count, col_count), jnp.float32),
            pltpu.VMEM((parts + 1, row_count, col_count), jnp.float32),
            pltpu.VMEM(couplings.shape, jnp.float32),
            weight,
            weight,
            pltpu.VMEM((kinds, row_count, col_count), jnp.bfloat16),
            pltpu.VMEM((row_count, col_count), jnp.float32),
            pltpu.VMEM(half, jnp.float32),
            pltpu.VMEM(half, jnp.float32),
            pltpu.VMEM(half, jnp.float32),
            pltpu.SemaphoreType.DMA((3,)),
            pltpu.SemaphoreType.DMA((2,)),
            pltpu.SemaphoreType.DMA((2,)),
        ],
        compiler_params=pltpu.CompilerParams(
            collective_id=0, has_side_effects=True, vmem_limit_bytes=32 * 2**20
        ),
    )(block_index, bond_map, bond_strength, drive_amplitude, amplitudes, couplings)


def chosen_body(sizes, amplitudes, couplings, block_index, *rest):
    row_count = amplitudes.shape[1]
    devices = sizes[0] * sizes[1]
    block_rows = row_count // block_index.shape[0]
    if row_count % devices == 0 and block_rows % (row_count // devices) == 0:
        return body_by_rows(sizes, amplitudes, couplings, block_index, *rest)
    return body(amplitudes, couplings, block_index, *rest)


def solution(mesh):
    in_specs = (P(None, ("grp", "dev"), None), P(), P(("grp", "dev")), P(), P(), P())
    out_specs = P(None, ("grp", "dev"), None)
    sizes = (mesh.shape["grp"], mesh.shape["dev"])
    return jax.shard_map(
        functools.partial(chosen_body, sizes),
        mesh=mesh,
        in_specs=in_specs,
        out_specs=out_specs,
        check_vma=False,
    )
```

```python
import functools

import jax
import jax.numpy as jnp
from jax import lax
from jax.experimental import pallas as pl
from jax.experimental.pallas import tpu as pltpu
from jax.sharding import PartitionSpec as P

BROWS = 16


STEP_SIZE = 0.5
HIGHEST = lax.Precision.HIGHEST


def swapped(shard, axis, distance):
    return lax.ppermute(shard, axis, [(i, i ^ 1 << distance) for i in range(lax.axis_size(axis))])


def spin_count(number):
    return number.bit_length() - 1


def flip_group(real_part, imag_part, bit_now):
    return swapped((real_part, imag_part), "grp", bit_now)


def coupled(real_part, imag_part, table, row_kind, kinds):
    row_count, col_count = real_part.shape
    product = jnp.dot(
        jnp.concatenate([real_part, imag_part], 0),
        table,
        precision=HIGHEST,
        preferred_element_type=jnp.float32,
    )
    extent = kinds * col_count
    left_part = product[:, :extent]
    right_part = product[:, extent:]
    all_real = left_part[:row_count] - right_part[row_count:]
    all_imag = left_part[row_count:] + right_part[:row_count]
    select = (row_kind[:, None] == jnp.arange(kinds, dtype=jnp.int32)[None, :]).astype(jnp.float32)[
        :, :, None
    ]
    out_real = jnp.sum(all_real.reshape(row_count, kinds, col_count) * select, axis=1)
    out_imag = jnp.sum(all_imag.reshape(row_count, kinds, col_count) * select, axis=1)
    return (out_real, out_imag)


def evaluate_field(
    real_part, imag_part, table, row_kind, kinds, bond_map, bond_strength, drive_row
):
    out_real, out_imag = coupled(real_part, imag_part, table, row_kind, kinds)
    row_count, col_count = real_part.shape
    dev_bits = spin_count(lax.axis_size("dev"))
    grp_bits = spin_count(lax.axis_size("grp"))
    columns = jnp.arange(col_count, dtype=jnp.int32)
    for lead_spin in range(dev_bits + grp_bits):
        target = bond_map[lead_spin]
        shuffle = jnp.bitwise_xor(columns, jnp.left_shift(jnp.int32(1), target))
        sign_col = (1 - 2 * jnp.bitwise_and(jnp.right_shift(columns, target), 1)).astype(
            jnp.float32
        )[None, :]
        if lead_spin < dev_bits:
            part_real, part_imag = swapped((real_part, imag_part), "dev", lead_spin)
            sign_lead = (
                1 - 2 * jnp.bitwise_and(jnp.right_shift(lax.axis_index("dev"), lead_spin), 1)
            ).astype(jnp.float32)
        else:
            part_real, part_imag = flip_group(real_part, imag_part, lead_spin - dev_bits)
            sign_lead = (
                1
                - 2
                * jnp.bitwise_and(jnp.right_shift(lax.axis_index("grp"), lead_spin - dev_bits), 1)
            ).astype(jnp.float32)
        strength = bond_strength[lead_spin]
        drive_now = drive_row[lead_spin]
        out_real = (
            out_real
            + strength * (sign_lead * sign_col * real_part + jnp.take(part_real, shuffle, axis=1))
            + drive_now * part_real
        )
        out_imag = (
            out_imag
            + strength * (sign_lead * sign_col * imag_part + jnp.take(part_imag, shuffle, axis=1))
            + drive_now * part_imag
        )
    return (out_imag, -out_real)


def runge_kutta(real_part, imag_part, evaluate):
    half_step = 0.5 * STEP_SIZE
    slope_one = evaluate(0, real_part, imag_part)
    slope_two = evaluate(
        1, real_part + half_step * slope_one[0], imag_part + half_step * slope_one[1]
    )
    slope_three = evaluate(
        2, real_part + half_step * slope_two[0], imag_part + half_step * slope_two[1]
    )
    slope_four = evaluate(
        3, real_part + STEP_SIZE * slope_three[0], imag_part + STEP_SIZE * slope_three[1]
    )
    factor = STEP_SIZE / 6.0
    new_real = real_part + factor * (
        slope_one[0] + 2.0 * slope_two[0] + 2.0 * slope_three[0] + slope_four[0]
    )
    new_imag = imag_part + factor * (
        slope_one[1] + 2.0 * slope_two[1] + 2.0 * slope_three[1] + slope_four[1]
    )
    return (new_real, new_imag)


def body(amplitudes, couplings, block_index, bond_map, bond_strength, drive_amplitude):
    kinds = couplings.shape[1]
    col_count = couplings.shape[2]
    table_real = jnp.transpose(couplings[0], (2, 0, 1)).reshape(col_count, kinds * col_count)
    table_imag = jnp.transpose(couplings[1], (2, 0, 1)).reshape(col_count, kinds * col_count)
    table = jnp.concatenate([table_real, table_imag], 1)
    real_part = amplitudes[0]
    imag_part = amplitudes[1]
    row_count = real_part.shape[0]
    row_kind = jnp.repeat(block_index, BROWS, total_repeat_length=row_count)

    def evaluate(section, first, second):
        return evaluate_field(
            first, second, table, row_kind, kinds, bond_map, bond_strength, drive_amplitude[section]
        )

    new_real, new_imag = runge_kutta(real_part, imag_part, evaluate)
    return jnp.stack([new_real, new_imag])


SUBLANES = 8
MESH = pl.DeviceIdType.MESH


def flipped(field, stride):
    row_count, col_count = field.shape
    if stride >= SUBLANES:
        folded = field.reshape(row_count // (2 * stride), 2, stride, col_count)
        return jnp.concatenate([folded[:, 1:], folded[:, :1]], 1).reshape(row_count, col_count)
    tiles = field.reshape(row_count // SUBLANES, SUBLANES, col_count)
    down = pltpu.roll(tiles, stride, 1)
    if 2 * stride < SUBLANES:
        row = lax.broadcasted_iota(jnp.int32, tiles.shape, 1)
        up = pltpu.roll(tiles, SUBLANES - stride, 1)
        down = jnp.where(row // stride % 2 == 1, down, up)
    return down.reshape(row_count, col_count)


def step_kernel(
    sizes,
    kind_hbm,
    bond_hbm,
    strength_hbm,
    drive_hbm,
    amp_ref,
    coup_ref,
    out_ref,
    kind_ref,
    bond_ref,
    strength_ref,
    drive_ref,
    stage,
    held,
    table,
    weight_high,
    weight_low,
    masks,
    diagonal,
    field,
    total,
    final,
    local_sem,
    send_sem,
    recv_sem,
):
    grp_size, dev_size, block_rows = sizes
    devices = grp_size * dev_size
    lead = spin_count(devices)
    row_count, col_count = amp_ref.shape[1:]
    kinds = coup_ref.shape[1]
    sections = drive_ref.shape[0]
    share = row_count // devices
    others = (devices - 1) * share
    me = lax.axis_index("grp") * dev_size + lax.axis_index("dev")

    def place(hop):
        other = lax.rem(me + hop, devices)
        return other, (other // dev_size, lax.rem(other, dev_size))

    barrier = pltpu.get_barrier_semaphore()

    def greet(hop, carry):
        pl.semaphore_signal(barrier, inc=1, device_id=place(hop)[1], device_id_type=MESH)
        return carry

    lax.fori_loop(1, devices, greet, 0)
    loads = [
        pltpu.make_async_copy(source, target, local_sem.at[3 + index])
        for index, (source, target) in enumerate(
            (
                (kind_hbm, kind_ref),
                (amp_ref, stage.at[pl.ds(0, 2)]),
                (coup_ref, table),
                (bond_hbm, bond_ref),
                (strength_hbm, strength_ref),
                (drive_hbm, drive_ref),
            )
        )
    ]
    for load in loads:
        load.start()
    loads[0].wait()
    for block in range(row_count // block_rows):
        kind = kind_ref[block].astype(jnp.float32)
        stage[2, block * block_rows : (block + 1) * block_rows] = jnp.full(
            (block_rows, col_count), kind, jnp.float32
        )
    loads[1].wait()
    pl.semaphore_wait(barrier, devices - 1)

    mine = pl.ds(me * share, share)

    def exchange(source, target, phase):
        def send(hop, carry):
            other, where = place(hop)
            pltpu.make_async_remote_copy(
                src_ref=source.at[:, pl.ds(other * share, share)],
                dst_ref=target.at[:, mine],
                send_sem=send_sem.at[phase],
                recv_sem=recv_sem.at[phase],
                device_id=where,
                device_id_type=MESH,
            ).start()
            return carry

        lax.fori_loop(1, devices, send, 0)
        own = pltpu.make_async_copy(
            source.at[:, mine], target.at[:, mine], local_sem.at[phase]
        )
        own.start()
        return own

    def finish(source, target, phase, own):
        own.wait()
        sent = source.at[:, pl.ds(0, others)]
        pltpu.make_async_copy(sent, sent, send_sem.at[phase]).wait()
        came = target.at[:, pl.ds(0, others)]
        pltpu.make_async_copy(came, came, recv_sem.at[phase]).wait()

    own = exchange(stage, held, 0)
    for load in loads[2:]:
        load.wait()

    def split(kind, carry):
        real = table[0, kind]
        imag = table[1, kind]
        real_high = real.astype(jnp.bfloat16)
        imag_high = imag.astype(jnp.bfloat16)
        real_low = (real - real_high.astype(jnp.float32)).astype(jnp.bfloat16)
        imag_low = (imag - imag_high.astype(jnp.float32)).astype(jnp.bfloat16)
        first = pl.ds(pl.multiple_of(kind * 2 * col_count, 2 * col_count), col_count)
        second = pl.ds(pl.multiple_of(kind * 2 * col_count, col_count) + col_count, col_count)
        for weight, real_now, imag_now in (
            (weight_high, real_high, imag_high),
            (weight_low, real_low, imag_low),
        ):
            weight[first, :col_count] = -imag_now
            weight[first, col_count:] = -real_now
            weight[second, :col_count] = real_now
            weight[second, col_count:] = -imag_now
        return carry

    lax.fori_loop(0, kinds, split, 0)

    row = lax.broadcasted_iota(jnp.int32, (row_count, col_count), 0)
    column = lax.broadcasted_iota(jnp.int32, (row_count, col_count), 1)
    diag = jnp.zeros((row_count, col_count), jnp.float32)
    shuffles = []
    for spin in range(lead):
        target = bond_ref[spin]
        shuffles.append(jnp.bitwise_xor(column, jnp.left_shift(jnp.int32(1), target)))
        parity = jnp.bitwise_xor(
            jnp.right_shift(row // share, spin), jnp.right_shift(column, target)
        )
        sign = (1 - 2 * jnp.bitwise_and(parity, 1)).astype(jnp.float32)
        diag = diag + strength_ref[spin] * sign
    diagonal[...] = diag

    finish(stage, held, 0, own)
    kind_rows = held[2]
    for kind in range(kinds):
        masks[kind] = (kind_rows == float(kind)).astype(jnp.float32).astype(jnp.bfloat16)
    field[...] = held[:2]
    total[...] = jnp.zeros_like(total)

    def section(now, carry):
        both = jnp.concatenate([field[0], field[1]], 1)
        high = both.astype(jnp.bfloat16)
        low = (both - high.astype(jnp.float32)).astype(jnp.bfloat16)
        high_parts = []
        low_parts = []
        for kind in range(kinds):
            mask = jnp.concatenate([masks[kind], masks[kind]], 1)
            high_parts.append(high * mask)
            low_parts.append(low * mask)
        high_all = jnp.concatenate(high_parts, 1)
        low_all = jnp.concatenate(low_parts, 1)
        main = jnp.dot(
            jnp.concatenate([high_all, low_all], 0),
            weight_high[...],
            preferred_element_type=jnp.float32,
        )
        rest = jnp.dot(high_all, weight_low[...], preferred_element_type=jnp.float32)
        product = main[:row_count] + (main[row_count:] + rest)
        leads = []
        for part in range(2):
            here = field[part]
            other = diagonal[...] * here
            for spin in range(lead):
                there = flipped(here, share << spin)
                moved = jnp.take_along_axis(
                    there, shuffles[spin], axis=1, mode="promise_in_bounds"
                )
                other = other + strength_ref[spin] * moved + drive_ref[now, spin] * there
            leads.append(other)
        slope = (product[:, :col_count] + leads[1], product[:, col_count:] - leads[0])
        edge = (now == 0) | (now == sections - 1)
        weight = jnp.where(edge, 1.0, 2.0)
        step = jnp.where(now == sections - 2, STEP_SIZE, 0.5 * STEP_SIZE)
        for part in range(2):
            total[part] = total[part] + weight * slope[part]
            field[part] = held[part] + step * slope[part]
        return carry

    lax.fori_loop(0, sections, section, 0)
    final[...] = held[:2] + (STEP_SIZE / 6.0) * total[...]
    own = exchange(final, out_ref, 1)
    finish(final, out_ref, 1, own)


def body_by_rows(
    sizes, amplitudes, couplings, block_index, bond_map, bond_strength, drive_amplitude
):
    parts, row_count, col_count = amplitudes.shape
    kinds = couplings.shape[1]
    block_rows = row_count // block_index.shape[0]
    half = (parts, row_count, col_count)
    weight = pltpu.VMEM((kinds * 2 * col_count, 2 * col_count), jnp.bfloat16)
    return pl.pallas_call(
        functools.partial(step_kernel, (*sizes, block_rows)),
        out_shape=jax.ShapeDtypeStruct(half, jnp.float32),
        in_specs=[pl.BlockSpec(memory_space=pl.ANY)] * 6,
        out_specs=pl.BlockSpec(memory_space=pltpu.VMEM),
        scratch_shapes=[
            pltpu.SMEM(block_index.shape, jnp.int32),
            pltpu.SMEM(bond_map.shape, jnp.int32),
            pltpu.SMEM(bond_strength.shape, jnp.float32),
            pltpu.SMEM(drive_amplitude.shape, jnp.float32),
            pltpu.VMEM((parts + 1, row_count, col_count), jnp.float32),
            pltpu.VMEM((parts + 1, row_count, col_count), jnp.float32),
            pltpu.VMEM(couplings.shape, jnp.float32),
            weight,
            weight,
            pltpu.VMEM((kinds, row_count, col_count), jnp.bfloat16),
            pltpu.VMEM((row_count, col_count), jnp.float32),
            pltpu.VMEM(half, jnp.float32),
            pltpu.VMEM(half, jnp.float32),
            pltpu.VMEM(half, jnp.float32),
            pltpu.SemaphoreType.DMA((9,)),
            pltpu.SemaphoreType.DMA((2,)),
            pltpu.SemaphoreType.DMA((2,)),
        ],
        compiler_params=pltpu.CompilerParams(collective_id=0, has_side_effects=True),
    )(block_index, bond_map, bond_strength, drive_amplitude, amplitudes, couplings)


def chosen_body(sizes, amplitudes, couplings, block_index, *rest):
    row_count = amplitudes.shape[1]
    devices = sizes[0] * sizes[1]
    block_rows = row_count // block_index.shape[0]
    if row_count % devices == 0 and block_rows % (row_count // devices) == 0:
        return body_by_rows(sizes, amplitudes, couplings, block_index, *rest)
    return body(amplitudes, couplings, block_index, *rest)


def solution(mesh):
    in_specs = (P(None, ("grp", "dev"), None), P(), P(("grp", "dev")), P(), P(), P())
    out_specs = P(None, ("grp", "dev"), None)
    sizes = (mesh.shape["grp"], mesh.shape["dev"])
    return jax.shard_map(
        functools.partial(chosen_body, sizes),
        mesh=mesh,
        in_specs=in_specs,
        out_specs=out_specs,
        check_vma=False,
    )
```

```python
import functools

import jax
import jax.numpy as jnp
from jax import lax
from jax.experimental import pallas as pl
from jax.experimental.pallas import tpu as pltpu
from jax.sharding import PartitionSpec as P

BROWS = 16


STEP_SIZE = 0.5
HIGHEST = lax.Precision.HIGHEST


def swapped(shard, axis, distance):
    return lax.ppermute(shard, axis, [(i, i ^ 1 << distance) for i in range(lax.axis_size(axis))])


def spin_count(number):
    return number.bit_length() - 1


def flip_group(real_part, imag_part, bit_now):
    return swapped((real_part, imag_part), "grp", bit_now)


def coupled(real_part, imag_part, table, row_kind, kinds):
    row_count, col_count = real_part.shape
    product = jnp.dot(
        jnp.concatenate([real_part, imag_part], 0),
        table,
        precision=HIGHEST,
        preferred_element_type=jnp.float32,
    )
    extent = kinds * col_count
    left_part = product[:, :extent]
    right_part = product[:, extent:]
    all_real = left_part[:row_count] - right_part[row_count:]
    all_imag = left_part[row_count:] + right_part[:row_count]
    select = (row_kind[:, None] == jnp.arange(kinds, dtype=jnp.int32)[None, :]).astype(jnp.float32)[
        :, :, None
    ]
    out_real = jnp.sum(all_real.reshape(row_count, kinds, col_count) * select, axis=1)
    out_imag = jnp.sum(all_imag.reshape(row_count, kinds, col_count) * select, axis=1)
    return (out_real, out_imag)


def evaluate_field(
    real_part, imag_part, table, row_kind, kinds, bond_map, bond_strength, drive_row
):
    out_real, out_imag = coupled(real_part, imag_part, table, row_kind, kinds)
    row_count, col_count = real_part.shape
    dev_bits = spin_count(lax.axis_size("dev"))
    grp_bits = spin_count(lax.axis_size("grp"))
    columns = jnp.arange(col_count, dtype=jnp.int32)
    for lead_spin in range(dev_bits + grp_bits):
        target = bond_map[lead_spin]
        shuffle = jnp.bitwise_xor(columns, jnp.left_shift(jnp.int32(1), target))
        sign_col = (1 - 2 * jnp.bitwise_and(jnp.right_shift(columns, target), 1)).astype(
            jnp.float32
        )[None, :]
        if lead_spin < dev_bits:
            part_real, part_imag = swapped((real_part, imag_part), "dev", lead_spin)
            sign_lead = (
                1 - 2 * jnp.bitwise_and(jnp.right_shift(lax.axis_index("dev"), lead_spin), 1)
            ).astype(jnp.float32)
        else:
            part_real, part_imag = flip_group(real_part, imag_part, lead_spin - dev_bits)
            sign_lead = (
                1
                - 2
                * jnp.bitwise_and(jnp.right_shift(lax.axis_index("grp"), lead_spin - dev_bits), 1)
            ).astype(jnp.float32)
        strength = bond_strength[lead_spin]
        drive_now = drive_row[lead_spin]
        out_real = (
            out_real
            + strength * (sign_lead * sign_col * real_part + jnp.take(part_real, shuffle, axis=1))
            + drive_now * part_real
        )
        out_imag = (
            out_imag
            + strength * (sign_lead * sign_col * imag_part + jnp.take(part_imag, shuffle, axis=1))
            + drive_now * part_imag
        )
    return (out_imag, -out_real)


def runge_kutta(real_part, imag_part, evaluate):
    half_step = 0.5 * STEP_SIZE
    slope_one = evaluate(0, real_part, imag_part)
    slope_two = evaluate(
        1, real_part + half_step * slope_one[0], imag_part + half_step * slope_one[1]
    )
    slope_three = evaluate(
        2, real_part + half_step * slope_two[0], imag_part + half_step * slope_two[1]
    )
    slope_four = evaluate(
        3, real_part + STEP_SIZE * slope_three[0], imag_part + STEP_SIZE * slope_three[1]
    )
    factor = STEP_SIZE / 6.0
    new_real = real_part + factor * (
        slope_one[0] + 2.0 * slope_two[0] + 2.0 * slope_three[0] + slope_four[0]
    )
    new_imag = imag_part + factor * (
        slope_one[1] + 2.0 * slope_two[1] + 2.0 * slope_three[1] + slope_four[1]
    )
    return (new_real, new_imag)


def body(amplitudes, couplings, block_index, bond_map, bond_strength, drive_amplitude):
    kinds = couplings.shape[1]
    col_count = couplings.shape[2]
    table_real = jnp.transpose(couplings[0], (2, 0, 1)).reshape(col_count, kinds * col_count)
    table_imag = jnp.transpose(couplings[1], (2, 0, 1)).reshape(col_count, kinds * col_count)
    table = jnp.concatenate([table_real, table_imag], 1)
    real_part = amplitudes[0]
    imag_part = amplitudes[1]
    row_count = real_part.shape[0]
    row_kind = jnp.repeat(block_index, BROWS, total_repeat_length=row_count)

    def evaluate(section, first, second):
        return evaluate_field(
            first, second, table, row_kind, kinds, bond_map, bond_strength, drive_amplitude[section]
        )

    new_real, new_imag = runge_kutta(real_part, imag_part, evaluate)
    return jnp.stack([new_real, new_imag])


SUBLANES = 8
VMEM_GRANT = 64 * 2**20 - 2**18
MESH = pl.DeviceIdType.MESH


def flipped(field, stride):
    row_count, col_count = field.shape
    if stride >= SUBLANES:
        folded = field.reshape(row_count // (2 * stride), 2, stride, col_count)
        return jnp.concatenate([folded[:, 1:], folded[:, :1]], 1).reshape(row_count, col_count)
    tiles = field.reshape(row_count // SUBLANES, SUBLANES, col_count)
    down = pltpu.roll(tiles, stride, 1)
    if 2 * stride < SUBLANES:
        row = lax.broadcasted_iota(jnp.int32, tiles.shape, 1)
        up = pltpu.roll(tiles, SUBLANES - stride, 1)
        down = jnp.where(row // stride % 2 == 1, down, up)
    return down.reshape(row_count, col_count)


def step_kernel(
    sizes,
    kind_hbm,
    bond_hbm,
    strength_hbm,
    drive_hbm,
    amp_ref,
    coup_ref,
    out_ref,
    kind_ref,
    bond_ref,
    strength_ref,
    drive_ref,
    stage,
    held,
    table,
    weight_high,
    weight_low,
    masks,
    diagonal,
    field,
    total,
    final,
    local_sem,
    send_sem,
    recv_sem,
):
    grp_size, dev_size, block_rows = sizes
    devices = grp_size * dev_size
    lead = spin_count(devices)
    row_count, col_count = amp_ref.shape[1:]
    kinds = coup_ref.shape[1]
    sections = drive_ref.shape[0]
    share = row_count // devices
    others = (devices - 1) * share
    me = lax.axis_index("grp") * dev_size + lax.axis_index("dev")

    def place(hop):
        other = lax.rem(me + hop, devices)
        return other, (other // dev_size, lax.rem(other, dev_size))

    barrier = pltpu.get_barrier_semaphore()

    for hop in range(1, devices):
        pl.semaphore_signal(barrier, inc=1, device_id=place(hop)[1], device_id_type=MESH)
    loads = [
        pltpu.make_async_copy(source, target, local_sem.at[3 + index])
        for index, (source, target) in enumerate(
            (
                (kind_hbm, kind_ref),
                (amp_ref, stage.at[pl.ds(0, 2)]),
                (coup_ref, table),
                (bond_hbm, bond_ref),
                (strength_hbm, strength_ref),
                (drive_hbm, drive_ref),
            )
        )
    ]
    for load in loads:
        load.start()
    loads[0].wait()
    for block in range(row_count // block_rows):
        kind = kind_ref[block].astype(jnp.float32)
        stage[2, block * block_rows : (block + 1) * block_rows] = jnp.full(
            (block_rows, col_count), kind, jnp.float32
        )
    loads[1].wait()
    pl.semaphore_wait(barrier, devices - 1)

    mine = pl.ds(me * share, share)

    def exchange(source, target, phase):
        for hop in range(1, devices):
            other, where = place(hop)
            pltpu.make_async_remote_copy(
                src_ref=source.at[:, pl.ds(other * share, share)],
                dst_ref=target.at[:, mine],
                send_sem=send_sem.at[phase],
                recv_sem=recv_sem.at[phase],
                device_id=where,
                device_id_type=MESH,
            ).start()
        own = pltpu.make_async_copy(
            source.at[:, mine], target.at[:, mine], local_sem.at[phase]
        )
        own.start()
        return own

    def finish(source, target, phase, own):
        own.wait()
        sent = source.at[:, pl.ds(0, others)]
        pltpu.make_async_copy(sent, sent, send_sem.at[phase]).wait()
        came = target.at[:, pl.ds(0, others)]
        pltpu.make_async_copy(came, came, recv_sem.at[phase]).wait()

    own = exchange(stage, held, 0)
    for load in loads[2:]:
        load.wait()

    def split(kind, carry):
        rows = pl.ds(pl.multiple_of(kind * col_count, col_count), col_count)
        for part in range(2):
            columns = slice(part * col_count, (part + 1) * col_count)
            full = table[part, kind]
            high = full.astype(jnp.bfloat16)
            weight_high[rows, columns] = high
            weight_low[rows, columns] = (full - high.astype(jnp.float32)).astype(jnp.bfloat16)
        return carry

    lax.fori_loop(0, kinds, split, 0)

    row = lax.broadcasted_iota(jnp.int32, (row_count, col_count), 0)
    column = lax.broadcasted_iota(jnp.int32, (row_count, col_count), 1)
    diag = jnp.zeros((row_count, col_count), jnp.float32)
    shuffles = []
    for spin in range(lead):
        target = bond_ref[spin]
        shuffles.append(jnp.bitwise_xor(column, jnp.left_shift(jnp.int32(1), target)))
        parity = jnp.bitwise_xor(
            jnp.right_shift(row // share, spin), jnp.right_shift(column, target)
        )
        sign = (1 - 2 * jnp.bitwise_and(parity, 1)).astype(jnp.float32)
        diag = diag + strength_ref[spin] * sign
    diagonal[...] = diag

    finish(stage, held, 0, own)
    kind_rows = held[2]
    for kind in range(kinds):
        masks[kind] = (kind_rows == float(kind)).astype(jnp.float32).astype(jnp.bfloat16)
    field[...] = held[:2]
    total[...] = jnp.zeros_like(total)

    def section(now, carry):
        both = jnp.concatenate([field[0], field[1]], 0)
        high = both.astype(jnp.bfloat16)
        low = (both - high.astype(jnp.float32)).astype(jnp.bfloat16)
        high_parts = []
        low_parts = []
        for kind in range(kinds):
            mask = jnp.concatenate([masks[kind], masks[kind]], 0)
            high_parts.append(high * mask)
            low_parts.append(low * mask)
        high_all = jnp.concatenate(high_parts, 1)
        low_all = jnp.concatenate(low_parts, 1)
        main = jnp.dot(
            jnp.concatenate([high_all, low_all], 0),
            weight_high[...],
            preferred_element_type=jnp.float32,
        )
        rest = jnp.dot(high_all, weight_low[...], preferred_element_type=jnp.float32)
        product = main[: 2 * row_count] + (main[2 * row_count :] + rest)
        from_real, from_imag = product[:row_count], product[row_count:]
        column_real = from_imag[:, :col_count] - from_real[:, col_count:]
        column_imag = -from_real[:, :col_count] - from_imag[:, col_count:]
        leads = []
        for part in range(2):
            here = field[part]
            other = diagonal[...] * here
            for spin in range(lead):
                there = flipped(here, share << spin)
                moved = jnp.take_along_axis(
                    there, shuffles[spin], axis=1, mode="promise_in_bounds"
                )
                other = other + strength_ref[spin] * moved + drive_ref[now, spin] * there
            leads.append(other)
        slope = (column_real + leads[1], column_imag - leads[0])
        edge = (now == 0) | (now == sections - 1)
        weight = jnp.where(edge, 1.0, 2.0)
        step = jnp.where(now == sections - 2, STEP_SIZE, 0.5 * STEP_SIZE)
        for part in range(2):
            total[part] = total[part] + weight * slope[part]
            field[part] = held[part] + step * slope[part]
        return carry

    lax.fori_loop(0, sections, section, 0)
    final[...] = held[:2] + (STEP_SIZE / 6.0) * total[...]
    own = exchange(final, out_ref, 1)
    finish(final, out_ref, 1, own)


def body_by_rows(
    sizes, amplitudes, couplings, block_index, bond_map, bond_strength, drive_amplitude
):
    parts, row_count, col_count = amplitudes.shape
    kinds = couplings.shape[1]
    block_rows = row_count // block_index.shape[0]
    half = (parts, row_count, col_count)
    weight = pltpu.VMEM((kinds * col_count, 2 * col_count), jnp.bfloat16)
    return pl.pallas_call(
        functools.partial(step_kernel, (*sizes, block_rows)),
        out_shape=pltpu.VMEM(half, jnp.float32),
        in_specs=[pl.BlockSpec(memory_space=pltpu.HBM)] * 6,
        out_specs=pl.BlockSpec(memory_space=pltpu.VMEM),
        scratch_shapes=[
            pltpu.SMEM(block_index.shape, jnp.int32),
            pltpu.SMEM(bond_map.shape, jnp.int32),
            pltpu.SMEM(bond_strength.shape, jnp.float32),
            pltpu.SMEM(drive_amplitude.shape, jnp.float32),
            pltpu.VMEM((parts + 1, row_count, col_count), jnp.float32),
            pltpu.VMEM((parts + 1, row_count, col_count), jnp.float32),
            pltpu.VMEM(couplings.shape, jnp.float32),
            weight,
            weight,
            pltpu.VMEM((kinds, row_count, col_count), jnp.bfloat16),
            pltpu.VMEM((row_count, col_count), jnp.float32),
            pltpu.VMEM(half, jnp.float32),
            pltpu.VMEM(half, jnp.float32),
            pltpu.VMEM(half, jnp.float32),
            pltpu.SemaphoreType.DMA((9,)),
            pltpu.SemaphoreType.DMA((2,)),
            pltpu.SemaphoreType.DMA((2,)),
        ],
        compiler_params=pltpu.CompilerParams(
            collective_id=0, has_side_effects=True, vmem_limit_bytes=VMEM_GRANT
        ),
    )(block_index, bond_map, bond_strength, drive_amplitude, amplitudes, couplings)


def chosen_body(sizes, amplitudes, couplings, block_index, *rest):
    row_count = amplitudes.shape[1]
    devices = sizes[0] * sizes[1]
    block_rows = row_count // block_index.shape[0]
    if row_count % devices == 0 and block_rows % (row_count // devices) == 0:
        return body_by_rows(sizes, amplitudes, couplings, block_index, *rest)
    return body(amplitudes, couplings, block_index, *rest)


def solution(mesh):
    in_specs = (P(None, ("grp", "dev"), None), P(), P(("grp", "dev")), P(), P(), P())
    out_specs = P(None, ("grp", "dev"), None)
    sizes = (mesh.shape["grp"], mesh.shape["dev"])
    return jax.shard_map(
        functools.partial(chosen_body, sizes),
        mesh=mesh,
        in_specs=in_specs,
        out_specs=out_specs,
        check_vma=False,
    )
```

```python
import functools

import jax
import jax.numpy as jnp
from jax import lax
from jax.experimental import pallas as pl
from jax.experimental.pallas import tpu as pltpu
from jax.sharding import PartitionSpec as P

BROWS = 16


STEP_SIZE = 0.5
HIGHEST = lax.Precision.HIGHEST


def swapped(shard, axis, distance):
    return lax.ppermute(shard, axis, [(i, i ^ 1 << distance) for i in range(lax.axis_size(axis))])


def spin_count(number):
    return number.bit_length() - 1


def flip_group(real_part, imag_part, bit_now):
    return swapped((real_part, imag_part), "grp", bit_now)


def coupled(real_part, imag_part, table, row_kind, kinds):
    row_count, col_count = real_part.shape
    product = jnp.dot(
        jnp.concatenate([real_part, imag_part], 0),
        table,
        precision=HIGHEST,
        preferred_element_type=jnp.float32,
    )
    extent = kinds * col_count
    left_part = product[:, :extent]
    right_part = product[:, extent:]
    all_real = left_part[:row_count] - right_part[row_count:]
    all_imag = left_part[row_count:] + right_part[:row_count]
    select = (row_kind[:, None] == jnp.arange(kinds, dtype=jnp.int32)[None, :]).astype(jnp.float32)[
        :, :, None
    ]
    out_real = jnp.sum(all_real.reshape(row_count, kinds, col_count) * select, axis=1)
    out_imag = jnp.sum(all_imag.reshape(row_count, kinds, col_count) * select, axis=1)
    return (out_real, out_imag)


def evaluate_field(
    real_part, imag_part, table, row_kind, kinds, bond_map, bond_strength, drive_row
):
    out_real, out_imag = coupled(real_part, imag_part, table, row_kind, kinds)
    row_count, col_count = real_part.shape
    dev_bits = spin_count(lax.axis_size("dev"))
    grp_bits = spin_count(lax.axis_size("grp"))
    columns = jnp.arange(col_count, dtype=jnp.int32)
    for lead_spin in range(dev_bits + grp_bits):
        target = bond_map[lead_spin]
        shuffle = jnp.bitwise_xor(columns, jnp.left_shift(jnp.int32(1), target))
        sign_col = (1 - 2 * jnp.bitwise_and(jnp.right_shift(columns, target), 1)).astype(
            jnp.float32
        )[None, :]
        if lead_spin < dev_bits:
            part_real, part_imag = swapped((real_part, imag_part), "dev", lead_spin)
            sign_lead = (
                1 - 2 * jnp.bitwise_and(jnp.right_shift(lax.axis_index("dev"), lead_spin), 1)
            ).astype(jnp.float32)
        else:
            part_real, part_imag = flip_group(real_part, imag_part, lead_spin - dev_bits)
            sign_lead = (
                1
                - 2
                * jnp.bitwise_and(jnp.right_shift(lax.axis_index("grp"), lead_spin - dev_bits), 1)
            ).astype(jnp.float32)
        strength = bond_strength[lead_spin]
        drive_now = drive_row[lead_spin]
        out_real = (
            out_real
            + strength * (sign_lead * sign_col * real_part + jnp.take(part_real, shuffle, axis=1))
            + drive_now * part_real
        )
        out_imag = (
            out_imag
            + strength * (sign_lead * sign_col * imag_part + jnp.take(part_imag, shuffle, axis=1))
            + drive_now * part_imag
        )
    return (out_imag, -out_real)


def runge_kutta(real_part, imag_part, evaluate):
    half_step = 0.5 * STEP_SIZE
    slope_one = evaluate(0, real_part, imag_part)
    slope_two = evaluate(
        1, real_part + half_step * slope_one[0], imag_part + half_step * slope_one[1]
    )
    slope_three = evaluate(
        2, real_part + half_step * slope_two[0], imag_part + half_step * slope_two[1]
    )
    slope_four = evaluate(
        3, real_part + STEP_SIZE * slope_three[0], imag_part + STEP_SIZE * slope_three[1]
    )
    factor = STEP_SIZE / 6.0
    new_real = real_part + factor * (
        slope_one[0] + 2.0 * slope_two[0] + 2.0 * slope_three[0] + slope_four[0]
    )
    new_imag = imag_part + factor * (
        slope_one[1] + 2.0 * slope_two[1] + 2.0 * slope_three[1] + slope_four[1]
    )
    return (new_real, new_imag)


def body(amplitudes, couplings, block_index, bond_map, bond_strength, drive_amplitude):
    kinds = couplings.shape[1]
    col_count = couplings.shape[2]
    table_real = jnp.transpose(couplings[0], (2, 0, 1)).reshape(col_count, kinds * col_count)
    table_imag = jnp.transpose(couplings[1], (2, 0, 1)).reshape(col_count, kinds * col_count)
    table = jnp.concatenate([table_real, table_imag], 1)
    real_part = amplitudes[0]
    imag_part = amplitudes[1]
    row_count = real_part.shape[0]
    row_kind = jnp.repeat(block_index, BROWS, total_repeat_length=row_count)

    def evaluate(section, first, second):
        return evaluate_field(
            first, second, table, row_kind, kinds, bond_map, bond_strength, drive_amplitude[section]
        )

    new_real, new_imag = runge_kutta(real_part, imag_part, evaluate)
    return jnp.stack([new_real, new_imag])


SUBLANES = 8
VMEM_GRANT = 64 * 2**20 - 2**18
MESH = pl.DeviceIdType.MESH


def flipped(field, stride):
    row_count, col_count = field.shape
    if stride >= SUBLANES:
        folded = field.reshape(row_count // (2 * stride), 2, stride, col_count)
        return jnp.concatenate([folded[:, 1:], folded[:, :1]], 1).reshape(row_count, col_count)
    tiles = field.reshape(row_count // SUBLANES, SUBLANES, col_count)
    down = pltpu.roll(tiles, stride, 1)
    if 2 * stride < SUBLANES:
        row = lax.broadcasted_iota(jnp.int32, tiles.shape, 1)
        up = pltpu.roll(tiles, SUBLANES - stride, 1)
        down = jnp.where(row // stride % 2 == 1, down, up)
    return down.reshape(row_count, col_count)


def step_kernel(
    sizes,
    kind_hbm,
    bond_hbm,
    strength_hbm,
    drive_hbm,
    amp_ref,
    coup_ref,
    out_ref,
    kind_ref,
    bond_ref,
    strength_ref,
    drive_ref,
    stage,
    held,
    table,
    weight_high,
    weight_low,
    masks,
    diagonal,
    field,
    total,
    final,
    psi,
    back,
    landed,
    local_sem,
    send_sem,
    recv_sem,
):
    grp_size, dev_size, block_rows = sizes
    devices = grp_size * dev_size
    lead = spin_count(devices)
    parts, row_count, col_count = amp_ref.shape
    kinds = coup_ref.shape[1]
    sections = drive_ref.shape[0]
    share = row_count // devices
    planes = parts * share
    me = lax.axis_index("grp") * dev_size + lax.axis_index("dev")

    def place(hop):
        other = lax.rem(me + hop, devices)
        return other, (other // dev_size, lax.rem(other, dev_size))

    barrier = pltpu.get_barrier_semaphore()

    for hop in range(1, devices):
        pl.semaphore_signal(barrier, inc=1, device_id=place(hop)[1], device_id_type=MESH)
    loads = [
        pltpu.make_async_copy(source, target, local_sem.at[3 + index])
        for index, (source, target) in enumerate(
            (
                (kind_hbm, kind_ref),
                (amp_ref, final),
                (coup_ref, table),
                (bond_hbm, bond_ref),
                (strength_hbm, strength_ref),
                (drive_hbm, drive_ref),
            )
        )
    ]
    for load in loads:
        load.start()
    loads[0].wait()
    owner = lax.broadcasted_iota(jnp.int32, (devices, col_count), 0) * share // block_rows
    kind_rows = jnp.zeros((devices, col_count), jnp.float32)
    for block in range(row_count // block_rows):
        kind_rows = jnp.where(owner == block, kind_ref[block].astype(jnp.float32), kind_rows)
    stage[pl.ds(planes, devices, stride=planes + 1), :] = kind_rows
    loads[1].wait()
    for part in range(parts):
        for spot in range(share):
            stage[pl.ds(part * share + spot, devices, stride=planes + 1), :] = final[
                part, pl.ds(spot, devices, stride=share), :
            ]
    pl.semaphore_wait(barrier, devices - 1)

    def exchange(source, target, phase):
        width = source.shape[0] // devices
        mine = pl.ds(me * width, width)
        for hop in range(1, devices):
            other, where = place(hop)
            pltpu.make_async_remote_copy(
                src_ref=source.at[pl.ds(other * width, width)],
                dst_ref=target.at[mine],
                send_sem=send_sem.at[phase],
                recv_sem=recv_sem.at[phase],
                device_id=where,
                device_id_type=MESH,
            ).start()
        own = pltpu.make_async_copy(source.at[mine], target.at[mine], local_sem.at[phase])
        own.start()
        return own

    def finish(source, target, phase, own):
        own.wait()
        others = pl.ds(0, source.shape[0] // devices * (devices - 1))
        sent = source.at[others]
        pltpu.make_async_copy(sent, sent, send_sem.at[phase]).wait()
        came = target.at[others]
        pltpu.make_async_copy(came, came, recv_sem.at[phase]).wait()

    own = exchange(stage, held, 0)
    for load in loads[2:]:
        load.wait()

    def split(kind, carry):
        rows = pl.ds(pl.multiple_of(kind * col_count, col_count), col_count)
        for part in range(2):
            columns = slice(part * col_count, (part + 1) * col_count)
            full = table[part, kind]
            high = full.astype(jnp.bfloat16)
            weight_high[rows, columns] = high
            weight_low[rows, columns] = (full - high.astype(jnp.float32)).astype(jnp.bfloat16)
        return carry

    lax.fori_loop(0, kinds, split, 0)

    row = lax.broadcasted_iota(jnp.int32, (row_count, col_count), 0)
    column = lax.broadcasted_iota(jnp.int32, (row_count, col_count), 1)
    diag = jnp.zeros((row_count, col_count), jnp.float32)
    shuffles = []
    for spin in range(lead):
        target = bond_ref[spin]
        shuffles.append(jnp.bitwise_xor(column, jnp.left_shift(jnp.int32(1), target)))
        parity = jnp.bitwise_xor(
            jnp.right_shift(row % devices, spin), jnp.right_shift(column, target)
        )
        sign = (1 - 2 * jnp.bitwise_and(parity, 1)).astype(jnp.float32)
        diag = diag + strength_ref[spin] * sign
    diagonal[...] = diag

    finish(stage, held, 0, own)
    kind_now = held[pl.ds(planes, devices, stride=planes + 1), :]
    kind_now = jnp.concatenate([kind_now] * share, 0)
    for kind in range(kinds):
        masks[kind] = (kind_now == float(kind)).astype(jnp.float32).astype(jnp.bfloat16)
    for part in range(parts):
        for spot in range(share):
            came = held[pl.ds(part * share + spot, devices, stride=planes + 1), :]
            rows = slice(spot * devices, (spot + 1) * devices)
            psi[part, rows] = came
            field[part, rows] = came
    total[...] = jnp.zeros_like(total)

    def section(now, carry):
        both = jnp.concatenate([field[0], field[1]], 0)
        high = both.astype(jnp.bfloat16)
        low = (both - high.astype(jnp.float32)).astype(jnp.bfloat16)
        high_parts = []
        low_parts = []
        for kind in range(kinds):
            mask = jnp.concatenate([masks[kind], masks[kind]], 0)
            high_parts.append(high * mask)
            low_parts.append(low * mask)
        high_all = jnp.concatenate(high_parts, 1)
        low_all = jnp.concatenate(low_parts, 1)
        main = jnp.dot(
            jnp.concatenate([high_all, low_all], 0),
            weight_high[...],
            preferred_element_type=jnp.float32,
        )
        rest = jnp.dot(high_all, weight_low[...], preferred_element_type=jnp.float32)
        product = main[: 2 * row_count] + (main[2 * row_count :] + rest)
        from_real, from_imag = product[:row_count], product[row_count:]
        column_real = from_imag[:, :col_count] - from_real[:, col_count:]
        column_imag = -from_real[:, :col_count] - from_imag[:, col_count:]
        leads = []
        for part in range(2):
            here = field[part]
            other = diagonal[...] * here
            for spin in range(lead):
                there = flipped(here, 1 << spin)
                moved = jnp.take_along_axis(
                    there, shuffles[spin], axis=1, mode="promise_in_bounds"
                )
                other = other + strength_ref[spin] * moved + drive_ref[now, spin] * there
            leads.append(other)
        slope = (column_real + leads[1], column_imag - leads[0])
        edge = (now == 0) | (now == sections - 1)
        weight = jnp.where(edge, 1.0, 2.0)
        step = jnp.where(now == sections - 2, STEP_SIZE, 0.5 * STEP_SIZE)
        for part in range(2):
            total[part] = total[part] + weight * slope[part]
            field[part] = psi[part] + step * slope[part]
        return carry

    lax.fori_loop(0, sections, section, 0)
    final[...] = psi[...] + (STEP_SIZE / 6.0) * total[...]
    for part in range(parts):
        for spot in range(share):
            back[pl.ds(part * share + spot, devices, stride=planes), :] = final[
                part, spot * devices : (spot + 1) * devices
            ]
    own = exchange(back, landed, 1)
    finish(back, landed, 1, own)
    for part in range(parts):
        for spot in range(share):
            out_ref[part, pl.ds(spot, devices, stride=share), :] = landed[
                pl.ds(part * share + spot, devices, stride=planes), :
            ]


def body_by_rows(
    sizes, amplitudes, couplings, block_index, bond_map, bond_strength, drive_amplitude
):
    parts, row_count, col_count = amplitudes.shape
    kinds = couplings.shape[1]
    block_rows = row_count // block_index.shape[0]
    half = (parts, row_count, col_count)
    weight = pltpu.VMEM((kinds * col_count, 2 * col_count), jnp.bfloat16)
    homeward = pltpu.VMEM((parts * row_count, col_count), jnp.float32)
    outward = pltpu.VMEM((parts * row_count + sizes[0] * sizes[1], col_count), jnp.float32)
    return pl.pallas_call(
        functools.partial(step_kernel, (*sizes, block_rows)),
        out_shape=pltpu.VMEM(half, jnp.float32),
        in_specs=[pl.BlockSpec(memory_space=pltpu.HBM)] * 6,
        out_specs=pl.BlockSpec(memory_space=pltpu.VMEM),
        scratch_shapes=[
            pltpu.SMEM(block_index.shape, jnp.int32),
            pltpu.SMEM(bond_map.shape, jnp.int32),
            pltpu.SMEM(bond_strength.shape, jnp.float32),
            pltpu.SMEM(drive_amplitude.shape, jnp.float32),
            outward,
            outward,
            pltpu.VMEM(couplings.shape, jnp.float32),
            weight,
            weight,
            pltpu.VMEM((kinds, row_count, col_count), jnp.bfloat16),
            pltpu.VMEM((row_count, col_count), jnp.float32),
            pltpu.VMEM(half, jnp.float32),
            pltpu.VMEM(half, jnp.float32),
            pltpu.VMEM(half, jnp.float32),
            pltpu.VMEM(half, jnp.float32),
            homeward,
            homeward,
            pltpu.SemaphoreType.DMA((9,)),
            pltpu.SemaphoreType.DMA((2,)),
            pltpu.SemaphoreType.DMA((2,)),
        ],
        compiler_params=pltpu.CompilerParams(
            collective_id=0, has_side_effects=True, vmem_limit_bytes=VMEM_GRANT
        ),
    )(block_index, bond_map, bond_strength, drive_amplitude, amplitudes, couplings)


def chosen_body(sizes, amplitudes, couplings, block_index, *rest):
    row_count = amplitudes.shape[1]
    devices = sizes[0] * sizes[1]
    block_rows = row_count // block_index.shape[0]
    if row_count % devices == 0 and block_rows % (row_count // devices) == 0:
        return body_by_rows(sizes, amplitudes, couplings, block_index, *rest)
    return body(amplitudes, couplings, block_index, *rest)


def solution(mesh):
    in_specs = (P(None, ("grp", "dev"), None), P(), P(("grp", "dev")), P(), P(), P())
    out_specs = P(None, ("grp", "dev"), None)
    sizes = (mesh.shape["grp"], mesh.shape["dev"])
    return jax.shard_map(
        functools.partial(chosen_body, sizes),
        mesh=mesh,
        in_specs=in_specs,
        out_specs=out_specs,
        check_vma=False,
    )
```

```python
import functools

import jax
import jax.numpy as jnp
from jax import lax
from jax.experimental import pallas as pl
from jax.experimental.pallas import tpu as pltpu
from jax.sharding import PartitionSpec as P

BROWS = 16


STEP_SIZE = 0.5
HIGHEST = lax.Precision.HIGHEST


def swapped(shard, axis, distance):
    return lax.ppermute(shard, axis, [(i, i ^ 1 << distance) for i in range(lax.axis_size(axis))])


def spin_count(number):
    return number.bit_length() - 1


def flip_group(real_part, imag_part, bit_now):
    return swapped((real_part, imag_part), "grp", bit_now)


def coupled(real_part, imag_part, table, row_kind, kinds):
    row_count, col_count = real_part.shape
    product = jnp.dot(
        jnp.concatenate([real_part, imag_part], 0),
        table,
        precision=HIGHEST,
        preferred_element_type=jnp.float32,
    )
    extent = kinds * col_count
    left_part = product[:, :extent]
    right_part = product[:, extent:]
    all_real = left_part[:row_count] - right_part[row_count:]
    all_imag = left_part[row_count:] + right_part[:row_count]
    select = (row_kind[:, None] == jnp.arange(kinds, dtype=jnp.int32)[None, :]).astype(jnp.float32)[
        :, :, None
    ]
    out_real = jnp.sum(all_real.reshape(row_count, kinds, col_count) * select, axis=1)
    out_imag = jnp.sum(all_imag.reshape(row_count, kinds, col_count) * select, axis=1)
    return (out_real, out_imag)


def evaluate_field(
    real_part, imag_part, table, row_kind, kinds, bond_map, bond_strength, drive_row
):
    out_real, out_imag = coupled(real_part, imag_part, table, row_kind, kinds)
    row_count, col_count = real_part.shape
    dev_bits = spin_count(lax.axis_size("dev"))
    grp_bits = spin_count(lax.axis_size("grp"))
    columns = jnp.arange(col_count, dtype=jnp.int32)
    for lead_spin in range(dev_bits + grp_bits):
        target = bond_map[lead_spin]
        shuffle = jnp.bitwise_xor(columns, jnp.left_shift(jnp.int32(1), target))
        sign_col = (1 - 2 * jnp.bitwise_and(jnp.right_shift(columns, target), 1)).astype(
            jnp.float32
        )[None, :]
        if lead_spin < dev_bits:
            part_real, part_imag = swapped((real_part, imag_part), "dev", lead_spin)
            sign_lead = (
                1 - 2 * jnp.bitwise_and(jnp.right_shift(lax.axis_index("dev"), lead_spin), 1)
            ).astype(jnp.float32)
        else:
            part_real, part_imag = flip_group(real_part, imag_part, lead_spin - dev_bits)
            sign_lead = (
                1
                - 2
                * jnp.bitwise_and(jnp.right_shift(lax.axis_index("grp"), lead_spin - dev_bits), 1)
            ).astype(jnp.float32)
        strength = bond_strength[lead_spin]
        drive_now = drive_row[lead_spin]
        out_real = (
            out_real
            + strength * (sign_lead * sign_col * real_part + jnp.take(part_real, shuffle, axis=1))
            + drive_now * part_real
        )
        out_imag = (
            out_imag
            + strength * (sign_lead * sign_col * imag_part + jnp.take(part_imag, shuffle, axis=1))
            + drive_now * part_imag
        )
    return (out_imag, -out_real)


def runge_kutta(real_part, imag_part, evaluate):
    half_step = 0.5 * STEP_SIZE
    slope_one = evaluate(0, real_part, imag_part)
    slope_two = evaluate(
        1, real_part + half_step * slope_one[0], imag_part + half_step * slope_one[1]
    )
    slope_three = evaluate(
        2, real_part + half_step * slope_two[0], imag_part + half_step * slope_two[1]
    )
    slope_four = evaluate(
        3, real_part + STEP_SIZE * slope_three[0], imag_part + STEP_SIZE * slope_three[1]
    )
    factor = STEP_SIZE / 6.0
    new_real = real_part + factor * (
        slope_one[0] + 2.0 * slope_two[0] + 2.0 * slope_three[0] + slope_four[0]
    )
    new_imag = imag_part + factor * (
        slope_one[1] + 2.0 * slope_two[1] + 2.0 * slope_three[1] + slope_four[1]
    )
    return (new_real, new_imag)


def body(amplitudes, couplings, block_index, bond_map, bond_strength, drive_amplitude):
    kinds = couplings.shape[1]
    col_count = couplings.shape[2]
    table_real = jnp.transpose(couplings[0], (2, 0, 1)).reshape(col_count, kinds * col_count)
    table_imag = jnp.transpose(couplings[1], (2, 0, 1)).reshape(col_count, kinds * col_count)
    table = jnp.concatenate([table_real, table_imag], 1)
    real_part = amplitudes[0]
    imag_part = amplitudes[1]
    row_count = real_part.shape[0]
    row_kind = jnp.repeat(block_index, BROWS, total_repeat_length=row_count)

    def evaluate(section, first, second):
        return evaluate_field(
            first, second, table, row_kind, kinds, bond_map, bond_strength, drive_amplitude[section]
        )

    new_real, new_imag = runge_kutta(real_part, imag_part, evaluate)
    return jnp.stack([new_real, new_imag])


SUBLANES = 8
VMEM_GRANT = 64 * 2**20 - 2**18
MESH = pl.DeviceIdType.MESH


def flipped(field, stride):
    row_count, col_count = field.shape
    if stride >= SUBLANES:
        folded = field.reshape(row_count // (2 * stride), 2, stride, col_count)
        return jnp.concatenate([folded[:, 1:], folded[:, :1]], 1).reshape(row_count, col_count)
    tiles = field.reshape(row_count // SUBLANES, SUBLANES, col_count)
    down = pltpu.roll(tiles, stride, 1)
    if 2 * stride < SUBLANES:
        row = lax.broadcasted_iota(jnp.int32, tiles.shape, 1)
        up = pltpu.roll(tiles, SUBLANES - stride, 1)
        down = jnp.where(row // stride % 2 == 1, down, up)
    return down.reshape(row_count, col_count)


def step_kernel(
    sizes,
    kind_hbm,
    bond_hbm,
    strength_hbm,
    drive_hbm,
    amp_ref,
    coup_ref,
    out_ref,
    kind_ref,
    bond_ref,
    strength_ref,
    drive_ref,
    stage,
    held,
    table,
    weight_high,
    weight_low,
    masks,
    diagonal,
    field,
    total,
    final,
    psi,
    back,
    landed,
    local_sem,
    send_sem,
    recv_sem,
):
    grp_size, dev_size, block_rows = sizes
    devices = grp_size * dev_size
    lead = spin_count(devices)
    parts, row_count, col_count = amp_ref.shape
    kinds = coup_ref.shape[1]
    sections = drive_ref.shape[0]
    share = row_count // devices
    planes = parts * share
    me = lax.axis_index("grp") * dev_size + lax.axis_index("dev")

    hops = sorted(
        range(1, devices), key=lambda hop: -min(hop % dev_size, dev_size - hop % dev_size)
    )

    def place(hop):
        other = lax.rem(me + hop, devices)
        return other, (other // dev_size, lax.rem(other, dev_size))

    loads = [
        pltpu.make_async_copy(source, target, local_sem.at[3 + index])
        for index, (source, target) in enumerate(
            (
                (kind_hbm, kind_ref),
                (amp_ref, final),
                (coup_ref, table),
                (bond_hbm, bond_ref),
                (strength_hbm, strength_ref),
                (drive_hbm, drive_ref),
            )
        )
    ]
    for load in loads:
        load.start()
    barrier = pltpu.get_barrier_semaphore()

    for hop in hops:
        pl.semaphore_signal(barrier, inc=1, device_id=place(hop)[1], device_id_type=MESH)
    loads[0].wait()
    owner = lax.broadcasted_iota(jnp.int32, (devices, col_count), 0) * share // block_rows
    kind_rows = jnp.zeros((devices, col_count), jnp.float32)
    for block in range(row_count // block_rows):
        kind_rows = jnp.where(owner == block, kind_ref[block].astype(jnp.float32), kind_rows)
    stage[pl.ds(planes, devices, stride=planes + 1), :] = kind_rows
    loads[1].wait()
    for part in range(parts):
        for spot in range(share):
            stage[pl.ds(part * share + spot, devices, stride=planes + 1), :] = final[
                part, pl.ds(spot, devices, stride=share), :
            ]
    pl.semaphore_wait(barrier, devices - 1)

    def exchange(source, target, phase):
        width = source.shape[0] // devices
        mine = pl.ds(me * width, width)
        for hop in hops:
            other, where = place(hop)
            pltpu.make_async_remote_copy(
                src_ref=source.at[pl.ds(other * width, width)],
                dst_ref=target.at[mine],
                send_sem=send_sem.at[phase],
                recv_sem=recv_sem.at[phase],
                device_id=where,
                device_id_type=MESH,
            ).start()
        own = pltpu.make_async_copy(source.at[mine], target.at[mine], local_sem.at[phase])
        own.start()
        return own

    def finish(source, target, phase, own):
        own.wait()
        others = pl.ds(0, source.shape[0] // devices * (devices - 1))
        sent = source.at[others]
        pltpu.make_async_copy(sent, sent, send_sem.at[phase]).wait()
        came = target.at[others]
        pltpu.make_async_copy(came, came, recv_sem.at[phase]).wait()

    own = exchange(stage, held, 0)
    for load in loads[2:]:
        load.wait()

    def split(kind, carry):
        rows = pl.ds(pl.multiple_of(kind * col_count, col_count), col_count)
        for part in range(2):
            columns = slice(part * col_count, (part + 1) * col_count)
            full = table[part, kind]
            high = full.astype(jnp.bfloat16)
            weight_high[rows, columns] = high
            weight_low[rows, columns] = (full - high.astype(jnp.float32)).astype(jnp.bfloat16)
        return carry

    lax.fori_loop(0, kinds, split, 0)

    row = lax.broadcasted_iota(jnp.int32, (row_count, col_count), 0)
    column = lax.broadcasted_iota(jnp.int32, (row_count, col_count), 1)
    diag = jnp.zeros((row_count, col_count), jnp.float32)
    shuffles = []
    for spin in range(lead):
        target = bond_ref[spin]
        shuffles.append(jnp.bitwise_xor(column, jnp.left_shift(jnp.int32(1), target)))
        parity = jnp.bitwise_xor(
            jnp.right_shift(row % devices, spin), jnp.right_shift(column, target)
        )
        sign = (1 - 2 * jnp.bitwise_and(parity, 1)).astype(jnp.float32)
        diag = diag + strength_ref[spin] * sign
    diagonal[...] = diag

    finish(stage, held, 0, own)
    kind_now = held[pl.ds(planes, devices, stride=planes + 1), :]
    kind_now = jnp.concatenate([kind_now] * share, 0)
    for kind in range(kinds):
        masks[kind] = (kind_now == float(kind)).astype(jnp.float32).astype(jnp.bfloat16)
    for part in range(parts):
        for spot in range(share):
            came = held[pl.ds(part * share + spot, devices, stride=planes + 1), :]
            rows = slice(spot * devices, (spot + 1) * devices)
            psi[part, rows] = came
            field[part, rows] = came
    total[...] = jnp.zeros_like(total)

    def section(now, carry):
        both = jnp.concatenate([field[0], field[1]], 0)
        high = both.astype(jnp.bfloat16)
        low = (both - high.astype(jnp.float32)).astype(jnp.bfloat16)
        product = jnp.zeros((2 * row_count, 2 * col_count), jnp.float32)
        for first in range(0, kinds, 2):
            group = range(first, min(first + 2, kinds))
            rows = slice(first * col_count, (group[-1] + 1) * col_count)
            chosen = [jnp.concatenate([masks[kind], masks[kind]], 0) for kind in group]
            high_now = jnp.concatenate([high * mask for mask in chosen], 1)
            low_now = jnp.concatenate([low * mask for mask in chosen], 1)
            for left, right in (
                (high_now, weight_high),
                (low_now, weight_high),
                (high_now, weight_low),
            ):
                product = product + jnp.dot(
                    left, right[rows], preferred_element_type=jnp.float32
                )
        from_real, from_imag = product[:row_count], product[row_count:]
        column_real = from_imag[:, :col_count] - from_real[:, col_count:]
        column_imag = -from_real[:, :col_count] - from_imag[:, col_count:]
        leads = []
        for part in range(2):
            here = field[part]
            other = diagonal[...] * here
            for spin in range(lead):
                there = flipped(here, 1 << spin)
                moved = jnp.take_along_axis(
                    there, shuffles[spin], axis=1, mode="promise_in_bounds"
                )
                other = other + strength_ref[spin] * moved + drive_ref[now, spin] * there
            leads.append(other)
        slope = (column_real + leads[1], column_imag - leads[0])
        edge = (now == 0) | (now == sections - 1)
        weight = jnp.where(edge, 1.0, 2.0)
        step = jnp.where(now == sections - 2, STEP_SIZE, 0.5 * STEP_SIZE)
        for part in range(2):
            total[part] = total[part] + weight * slope[part]
            field[part] = psi[part] + step * slope[part]
        return carry

    lax.fori_loop(0, sections, section, 0)
    final[...] = psi[...] + (STEP_SIZE / 6.0) * total[...]
    for part in range(parts):
        for spot in range(share):
            back[pl.ds(part * share + spot, devices, stride=planes), :] = final[
                part, spot * devices : (spot + 1) * devices
            ]
    own = exchange(back, landed, 1)
    finish(back, landed, 1, own)
    for part in range(parts):
        for spot in range(share):
            out_ref[part, pl.ds(spot, devices, stride=share), :] = landed[
                pl.ds(part * share + spot, devices, stride=planes), :
            ]


def body_by_rows(
    sizes, amplitudes, couplings, block_index, bond_map, bond_strength, drive_amplitude
):
    parts, row_count, col_count = amplitudes.shape
    kinds = couplings.shape[1]
    block_rows = row_count // block_index.shape[0]
    half = (parts, row_count, col_count)
    weight = pltpu.VMEM((kinds * col_count, 2 * col_count), jnp.bfloat16)
    homeward = pltpu.VMEM((parts * row_count, col_count), jnp.float32)
    outward = pltpu.VMEM((parts * row_count + sizes[0] * sizes[1], col_count), jnp.float32)
    return pl.pallas_call(
        functools.partial(step_kernel, (*sizes, block_rows)),
        out_shape=pltpu.VMEM(half, jnp.float32),
        in_specs=[pl.BlockSpec(memory_space=pltpu.HBM)] * 6,
        out_specs=pl.BlockSpec(memory_space=pltpu.VMEM),
        scratch_shapes=[
            pltpu.SMEM(block_index.shape, jnp.int32),
            pltpu.SMEM(bond_map.shape, jnp.int32),
            pltpu.SMEM(bond_strength.shape, jnp.float32),
            pltpu.SMEM(drive_amplitude.shape, jnp.float32),
            outward,
            outward,
            pltpu.VMEM(couplings.shape, jnp.float32),
            weight,
            weight,
            pltpu.VMEM((kinds, row_count, col_count), jnp.bfloat16),
            pltpu.VMEM((row_count, col_count), jnp.float32),
            pltpu.VMEM(half, jnp.float32),
            pltpu.VMEM(half, jnp.float32),
            pltpu.VMEM(half, jnp.float32),
            pltpu.VMEM(half, jnp.float32),
            homeward,
            homeward,
            pltpu.SemaphoreType.DMA((9,)),
            pltpu.SemaphoreType.DMA((2,)),
            pltpu.SemaphoreType.DMA((2,)),
        ],
        compiler_params=pltpu.CompilerParams(
            collective_id=0, has_side_effects=True, vmem_limit_bytes=VMEM_GRANT
        ),
    )(block_index, bond_map, bond_strength, drive_amplitude, amplitudes, couplings)


def chosen_body(sizes, amplitudes, couplings, block_index, *rest):
    row_count = amplitudes.shape[1]
    devices = sizes[0] * sizes[1]
    block_rows = row_count // block_index.shape[0]
    if row_count % devices == 0 and block_rows % (row_count // devices) == 0:
        return body_by_rows(sizes, amplitudes, couplings, block_index, *rest)
    return body(amplitudes, couplings, block_index, *rest)


def solution(mesh):
    in_specs = (P(None, ("grp", "dev"), None), P(), P(("grp", "dev")), P(), P(), P())
    out_specs = P(None, ("grp", "dev"), None)
    sizes = (mesh.shape["grp"], mesh.shape["dev"])
    return jax.shard_map(
        functools.partial(chosen_body, sizes),
        mesh=mesh,
        in_specs=in_specs,
        out_specs=out_specs,
        check_vma=False,
    )
```

```python
import functools

import jax
import jax.numpy as jnp
from jax import lax
from jax.experimental import pallas as pl
from jax.experimental.pallas import tpu as pltpu
from jax.sharding import PartitionSpec as P

BROWS = 16


STEP_SIZE = 0.5
HIGHEST = lax.Precision.HIGHEST


def swapped(shard, axis, distance):
    return lax.ppermute(shard, axis, [(i, i ^ 1 << distance) for i in range(lax.axis_size(axis))])


def spin_count(number):
    return number.bit_length() - 1


def flip_group(real_part, imag_part, bit_now):
    return swapped((real_part, imag_part), "grp", bit_now)


def coupled(real_part, imag_part, table, row_kind, kinds):
    row_count, col_count = real_part.shape
    product = jnp.dot(
        jnp.concatenate([real_part, imag_part], 0),
        table,
        precision=HIGHEST,
        preferred_element_type=jnp.float32,
    )
    extent = kinds * col_count
    left_part = product[:, :extent]
    right_part = product[:, extent:]
    all_real = left_part[:row_count] - right_part[row_count:]
    all_imag = left_part[row_count:] + right_part[:row_count]
    select = (row_kind[:, None] == jnp.arange(kinds, dtype=jnp.int32)[None, :]).astype(jnp.float32)[
        :, :, None
    ]
    out_real = jnp.sum(all_real.reshape(row_count, kinds, col_count) * select, axis=1)
    out_imag = jnp.sum(all_imag.reshape(row_count, kinds, col_count) * select, axis=1)
    return (out_real, out_imag)


def evaluate_field(
    real_part, imag_part, table, row_kind, kinds, bond_map, bond_strength, drive_row
):
    out_real, out_imag = coupled(real_part, imag_part, table, row_kind, kinds)
    row_count, col_count = real_part.shape
    dev_bits = spin_count(lax.axis_size("dev"))
    grp_bits = spin_count(lax.axis_size("grp"))
    columns = jnp.arange(col_count, dtype=jnp.int32)
    for lead_spin in range(dev_bits + grp_bits):
        target = bond_map[lead_spin]
        shuffle = jnp.bitwise_xor(columns, jnp.left_shift(jnp.int32(1), target))
        sign_col = (1 - 2 * jnp.bitwise_and(jnp.right_shift(columns, target), 1)).astype(
            jnp.float32
        )[None, :]
        if lead_spin < dev_bits:
            part_real, part_imag = swapped((real_part, imag_part), "dev", lead_spin)
            sign_lead = (
                1 - 2 * jnp.bitwise_and(jnp.right_shift(lax.axis_index("dev"), lead_spin), 1)
            ).astype(jnp.float32)
        else:
            part_real, part_imag = flip_group(real_part, imag_part, lead_spin - dev_bits)
            sign_lead = (
                1
                - 2
                * jnp.bitwise_and(jnp.right_shift(lax.axis_index("grp"), lead_spin - dev_bits), 1)
            ).astype(jnp.float32)
        strength = bond_strength[lead_spin]
        drive_now = drive_row[lead_spin]
        out_real = (
            out_real
            + strength * (sign_lead * sign_col * real_part + jnp.take(part_real, shuffle, axis=1))
            + drive_now * part_real
        )
        out_imag = (
            out_imag
            + strength * (sign_lead * sign_col * imag_part + jnp.take(part_imag, shuffle, axis=1))
            + drive_now * part_imag
        )
    return (out_imag, -out_real)


def runge_kutta(real_part, imag_part, evaluate):
    half_step = 0.5 * STEP_SIZE
    slope_one = evaluate(0, real_part, imag_part)
    slope_two = evaluate(
        1, real_part + half_step * slope_one[0], imag_part + half_step * slope_one[1]
    )
    slope_three = evaluate(
        2, real_part + half_step * slope_two[0], imag_part + half_step * slope_two[1]
    )
    slope_four = evaluate(
        3, real_part + STEP_SIZE * slope_three[0], imag_part + STEP_SIZE * slope_three[1]
    )
    factor = STEP_SIZE / 6.0
    new_real = real_part + factor * (
        slope_one[0] + 2.0 * slope_two[0] + 2.0 * slope_three[0] + slope_four[0]
    )
    new_imag = imag_part + factor * (
        slope_one[1] + 2.0 * slope_two[1] + 2.0 * slope_three[1] + slope_four[1]
    )
    return (new_real, new_imag)


def body(amplitudes, couplings, block_index, bond_map, bond_strength, drive_amplitude):
    kinds = couplings.shape[1]
    col_count = couplings.shape[2]
    table_real = jnp.transpose(couplings[0], (2, 0, 1)).reshape(col_count, kinds * col_count)
    table_imag = jnp.transpose(couplings[1], (2, 0, 1)).reshape(col_count, kinds * col_count)
    table = jnp.concatenate([table_real, table_imag], 1)
    real_part = amplitudes[0]
    imag_part = amplitudes[1]
    row_count = real_part.shape[0]
    row_kind = jnp.repeat(block_index, BROWS, total_repeat_length=row_count)

    def evaluate(section, first, second):
        return evaluate_field(
            first, second, table, row_kind, kinds, bond_map, bond_strength, drive_amplitude[section]
        )

    new_real, new_imag = runge_kutta(real_part, imag_part, evaluate)
    return jnp.stack([new_real, new_imag])


SUBLANES = 8
VMEM_GRANT = 64 * 2**20 - 2**18
MESH = pl.DeviceIdType.MESH


def flipped(field, stride):
    row_count, col_count = field.shape
    if stride >= SUBLANES:
        folded = field.reshape(row_count // (2 * stride), 2, stride, col_count)
        return jnp.concatenate([folded[:, 1:], folded[:, :1]], 1).reshape(row_count, col_count)
    tiles = field.reshape(row_count // SUBLANES, SUBLANES, col_count)
    down = pltpu.roll(tiles, stride, 1)
    if 2 * stride < SUBLANES:
        row = lax.broadcasted_iota(jnp.int32, tiles.shape, 1)
        up = pltpu.roll(tiles, SUBLANES - stride, 1)
        down = jnp.where(row // stride % 2 == 1, down, up)
    return down.reshape(row_count, col_count)


def step_kernel(
    sizes,
    kind_hbm,
    bond_hbm,
    strength_hbm,
    drive_hbm,
    amp_ref,
    coup_ref,
    out_ref,
    kind_ref,
    bond_ref,
    strength_ref,
    drive_ref,
    stage,
    held,
    table,
    weight_high,
    weight_low,
    masks,
    diagonal,
    field,
    total,
    final,
    psi,
    back,
    landed,
    local_sem,
    send_sem,
    recv_sem,
):
    grp_size, dev_size, block_rows = sizes
    devices = grp_size * dev_size
    lead = spin_count(devices)
    parts, row_count, col_count = amp_ref.shape
    kinds = coup_ref.shape[1]
    sections = drive_ref.shape[0]
    share = row_count // devices
    planes = parts * share
    grp, dev = lax.axis_index("grp"), lax.axis_index("dev")
    me = grp * dev_size + dev
    grps = [grp] + [lax.rem(grp + hop, grp_size) for hop in range(1, grp_size)]
    devs = [dev] + [lax.rem(dev + hop, dev_size) for hop in range(1, dev_size)]
    hops = sorted(range(dev_size), key=lambda hop: -min(hop, dev_size - hop))
    others = [
        (grps[grp_hop] * dev_size + devs[dev_hop], (grps[grp_hop], devs[dev_hop]))
        for dev_hop in hops
        for grp_hop in reversed(range(grp_size))
        if grp_hop + dev_hop > 0
    ]
    loads = [
        pltpu.make_async_copy(source, target, local_sem.at[3 + index])
        for index, (source, target) in enumerate(
            (
                (kind_hbm, kind_ref),
                (amp_ref, final),
                (coup_ref, table),
                (bond_hbm, bond_ref),
                (strength_hbm, strength_ref),
                (drive_hbm, drive_ref),
            )
        )
    ]
    for load in loads[:2]:
        load.start()
    barrier = pltpu.get_barrier_semaphore()

    for _, where in others:
        pl.semaphore_signal(barrier, inc=1, device_id=where, device_id_type=MESH)
    for load in loads[2:]:
        load.start()
    loads[0].wait()
    owner = lax.broadcasted_iota(jnp.int32, (devices, col_count), 0) * share // block_rows
    kind_rows = jnp.zeros((devices, col_count), jnp.float32)
    for block in range(row_count // block_rows):
        kind_rows = jnp.where(owner == block, kind_ref[block].astype(jnp.float32), kind_rows)
    stage[pl.ds(planes, devices, stride=planes + 1), :] = kind_rows
    loads[1].wait()
    for part in range(parts):
        for spot in range(share):
            stage[pl.ds(part * share + spot, devices, stride=planes + 1), :] = final[
                part, pl.ds(spot, devices, stride=share), :
            ]
    pl.semaphore_wait(barrier, devices - 1)

    def exchange(source, target, phase):
        width = source.shape[0] // devices
        mine = pl.ds(me * width, width)
        for other, where in others:
            pltpu.make_async_remote_copy(
                src_ref=source.at[pl.ds(other * width, width)],
                dst_ref=target.at[mine],
                send_sem=send_sem.at[phase],
                recv_sem=recv_sem.at[phase],
                device_id=where,
                device_id_type=MESH,
            ).start()
        own = pltpu.make_async_copy(source.at[mine], target.at[mine], local_sem.at[phase])
        own.start()
        return own

    def finish(source, target, phase, own):
        own.wait()
        foreign = pl.ds(0, source.shape[0] // devices * (devices - 1))
        sent = source.at[foreign]
        pltpu.make_async_copy(sent, sent, send_sem.at[phase]).wait()
        came = target.at[foreign]
        pltpu.make_async_copy(came, came, recv_sem.at[phase]).wait()

    own = exchange(stage, held, 0)
    for load in loads[2:]:
        load.wait()

    def split(kind, carry):
        rows = pl.ds(pl.multiple_of(kind * col_count, col_count), col_count)
        for part in range(2):
            columns = slice(part * col_count, (part + 1) * col_count)
            full = table[part, kind]
            high = full.astype(jnp.bfloat16)
            weight_high[rows, columns] = high
            weight_low[rows, columns] = (full - high.astype(jnp.float32)).astype(jnp.bfloat16)
        return carry

    lax.fori_loop(0, kinds, split, 0)

    row = lax.broadcasted_iota(jnp.int32, (row_count, col_count), 0)
    column = lax.broadcasted_iota(jnp.int32, (row_count, col_count), 1)
    diag = jnp.zeros((row_count, col_count), jnp.float32)
    shuffles = []
    for spin in range(lead):
        target = bond_ref[spin]
        shuffles.append(jnp.bitwise_xor(column, jnp.left_shift(jnp.int32(1), target)))
        parity = jnp.bitwise_xor(
            jnp.right_shift(row % devices, spin), jnp.right_shift(column, target)
        )
        sign = (1 - 2 * jnp.bitwise_and(parity, 1)).astype(jnp.float32)
        diag = diag + strength_ref[spin] * sign
    diagonal[...] = diag

    finish(stage, held, 0, own)
    kind_now = held[pl.ds(planes, devices, stride=planes + 1), :]
    kind_now = jnp.concatenate([kind_now] * share, 0)
    for kind in range(kinds):
        masks[kind] = (kind_now == float(kind)).astype(jnp.float32).astype(jnp.bfloat16)
    for part in range(parts):
        for spot in range(share):
            came = held[pl.ds(part * share + spot, devices, stride=planes + 1), :]
            rows = slice(spot * devices, (spot + 1) * devices)
            psi[part, rows] = came
            field[part, rows] = came
    total[...] = jnp.zeros_like(total)

    def section(now, carry):
        both = jnp.concatenate([field[0], field[1]], 0)
        high = both.astype(jnp.bfloat16)
        low = (both - high.astype(jnp.float32)).astype(jnp.bfloat16)
        high_parts = []
        low_parts = []
        for kind in range(kinds):
            mask = jnp.concatenate([masks[kind], masks[kind]], 0)
            high_parts.append(high * mask)
            low_parts.append(low * mask)
        high_all = jnp.concatenate(high_parts, 1)
        low_all = jnp.concatenate(low_parts, 1)
        main = jnp.dot(
            jnp.concatenate([high_all, low_all], 0),
            weight_high[...],
            preferred_element_type=jnp.float32,
        )
        rest = jnp.dot(high_all, weight_low[...], preferred_element_type=jnp.float32)
        product = main[: 2 * row_count] + (main[2 * row_count :] + rest)
        from_real, from_imag = product[:row_count], product[row_count:]
        column_real = from_imag[:, :col_count] - from_real[:, col_count:]
        column_imag = -from_real[:, :col_count] - from_imag[:, col_count:]
        leads = []
        for part in range(2):
            here = field[part]
            other = diagonal[...] * here
            for spin in range(lead):
                there = flipped(here, 1 << spin)
                moved = jnp.take_along_axis(
                    there, shuffles[spin], axis=1, mode="promise_in_bounds"
                )
                other = other + strength_ref[spin] * moved + drive_ref[now, spin] * there
            leads.append(other)
        slope = (column_real + leads[1], column_imag - leads[0])
        edge = (now == 0) | (now == sections - 1)
        weight = jnp.where(edge, 1.0, 2.0)
        step = jnp.where(now == sections - 2, STEP_SIZE, 0.5 * STEP_SIZE)
        for part in range(2):
            total[part] = total[part] + weight * slope[part]
            field[part] = psi[part] + step * slope[part]
        return carry

    lax.fori_loop(0, sections, section, 0)
    final[...] = psi[...] + (STEP_SIZE / 6.0) * total[...]
    for part in range(parts):
        for spot in range(share):
            back[pl.ds(part * share + spot, devices, stride=planes), :] = final[
                part, spot * devices : (spot + 1) * devices
            ]
    own = exchange(back, landed, 1)
    finish(back, landed, 1, own)
    for part in range(parts):
        for spot in range(share):
            out_ref[part, pl.ds(spot, devices, stride=share), :] = landed[
                pl.ds(part * share + spot, devices, stride=planes), :
            ]


def body_by_rows(
    sizes, amplitudes, couplings, block_index, bond_map, bond_strength, drive_amplitude
):
    parts, row_count, col_count = amplitudes.shape
    kinds = couplings.shape[1]
    block_rows = row_count // block_index.shape[0]
    half = (parts, row_count, col_count)
    weight = pltpu.VMEM((kinds * col_count, 2 * col_count), jnp.bfloat16)
    homeward = pltpu.VMEM((parts * row_count, col_count), jnp.float32)
    outward = pltpu.VMEM((parts * row_count + sizes[0] * sizes[1], col_count), jnp.float32)
    return pl.pallas_call(
        functools.partial(step_kernel, (*sizes, block_rows)),
        out_shape=pltpu.VMEM(half, jnp.float32),
        in_specs=[pl.BlockSpec(memory_space=pltpu.HBM)] * 6,
        out_specs=pl.BlockSpec(memory_space=pltpu.VMEM),
        scratch_shapes=[
            pltpu.SMEM(block_index.shape, jnp.int32),
            pltpu.SMEM(bond_map.shape, jnp.int32),
            pltpu.SMEM(bond_strength.shape, jnp.float32),
            pltpu.SMEM(drive_amplitude.shape, jnp.float32),
            outward,
            outward,
            pltpu.VMEM(couplings.shape, jnp.float32),
            weight,
            weight,
            pltpu.VMEM((kinds, row_count, col_count), jnp.bfloat16),
            pltpu.VMEM((row_count, col_count), jnp.float32),
            pltpu.VMEM(half, jnp.float32),
            pltpu.VMEM(half, jnp.float32),
            pltpu.VMEM(half, jnp.float32),
            pltpu.VMEM(half, jnp.float32),
            homeward,
            homeward,
            pltpu.SemaphoreType.DMA((9,)),
            pltpu.SemaphoreType.DMA((2,)),
            pltpu.SemaphoreType.DMA((2,)),
        ],
        compiler_params=pltpu.CompilerParams(
            collective_id=0, has_side_effects=True, vmem_limit_bytes=VMEM_GRANT
        ),
    )(block_index, bond_map, bond_strength, drive_amplitude, amplitudes, couplings)


def chosen_body(sizes, amplitudes, couplings, block_index, *rest):
    row_count = amplitudes.shape[1]
    devices = sizes[0] * sizes[1]
    block_rows = row_count // block_index.shape[0]
    if row_count % devices == 0 and block_rows % (row_count // devices) == 0:
        return body_by_rows(sizes, amplitudes, couplings, block_index, *rest)
    return body(amplitudes, couplings, block_index, *rest)


def solution(mesh):
    in_specs = (P(None, ("grp", "dev"), None), P(), P(("grp", "dev")), P(), P(), P())
    out_specs = P(None, ("grp", "dev"), None)
    sizes = (mesh.shape["grp"], mesh.shape["dev"])
    return jax.shard_map(
        functools.partial(chosen_body, sizes),
        mesh=mesh,
        in_specs=in_specs,
        out_specs=out_specs,
        check_vma=False,
    )
```

```python
import functools

import jax
import jax.numpy as jnp
from jax import lax
from jax.experimental import pallas as pl
from jax.experimental.pallas import tpu as pltpu
from jax.sharding import PartitionSpec as P

BROWS = 16


STEP_SIZE = 0.5
HIGHEST = lax.Precision.HIGHEST


def swapped(shard, axis, distance):
    return lax.ppermute(shard, axis, [(i, i ^ 1 << distance) for i in range(lax.axis_size(axis))])


def spin_count(number):
    return number.bit_length() - 1


def flip_group(real_part, imag_part, bit_now):
    return swapped((real_part, imag_part), "grp", bit_now)


def coupled(real_part, imag_part, table, row_kind, kinds):
    row_count, col_count = real_part.shape
    product = jnp.dot(
        jnp.concatenate([real_part, imag_part], 0),
        table,
        precision=HIGHEST,
        preferred_element_type=jnp.float32,
    )
    extent = kinds * col_count
    left_part = product[:, :extent]
    right_part = product[:, extent:]
    all_real = left_part[:row_count] - right_part[row_count:]
    all_imag = left_part[row_count:] + right_part[:row_count]
    select = (row_kind[:, None] == jnp.arange(kinds, dtype=jnp.int32)[None, :]).astype(jnp.float32)[
        :, :, None
    ]
    out_real = jnp.sum(all_real.reshape(row_count, kinds, col_count) * select, axis=1)
    out_imag = jnp.sum(all_imag.reshape(row_count, kinds, col_count) * select, axis=1)
    return (out_real, out_imag)


def evaluate_field(
    real_part, imag_part, table, row_kind, kinds, bond_map, bond_strength, drive_row
):
    out_real, out_imag = coupled(real_part, imag_part, table, row_kind, kinds)
    row_count, col_count = real_part.shape
    dev_bits = spin_count(lax.axis_size("dev"))
    grp_bits = spin_count(lax.axis_size("grp"))
    columns = jnp.arange(col_count, dtype=jnp.int32)
    for lead_spin in range(dev_bits + grp_bits):
        target = bond_map[lead_spin]
        shuffle = jnp.bitwise_xor(columns, jnp.left_shift(jnp.int32(1), target))
        sign_col = (1 - 2 * jnp.bitwise_and(jnp.right_shift(columns, target), 1)).astype(
            jnp.float32
        )[None, :]
        if lead_spin < dev_bits:
            part_real, part_imag = swapped((real_part, imag_part), "dev", lead_spin)
            sign_lead = (
                1 - 2 * jnp.bitwise_and(jnp.right_shift(lax.axis_index("dev"), lead_spin), 1)
            ).astype(jnp.float32)
        else:
            part_real, part_imag = flip_group(real_part, imag_part, lead_spin - dev_bits)
            sign_lead = (
                1
                - 2
                * jnp.bitwise_and(jnp.right_shift(lax.axis_index("grp"), lead_spin - dev_bits), 1)
            ).astype(jnp.float32)
        strength = bond_strength[lead_spin]
        drive_now = drive_row[lead_spin]
        out_real = (
            out_real
            + strength * (sign_lead * sign_col * real_part + jnp.take(part_real, shuffle, axis=1))
            + drive_now * part_real
        )
        out_imag = (
            out_imag
            + strength * (sign_lead * sign_col * imag_part + jnp.take(part_imag, shuffle, axis=1))
            + drive_now * part_imag
        )
    return (out_imag, -out_real)


def runge_kutta(real_part, imag_part, evaluate):
    half_step = 0.5 * STEP_SIZE
    slope_one = evaluate(0, real_part, imag_part)
    slope_two = evaluate(
        1, real_part + half_step * slope_one[0], imag_part + half_step * slope_one[1]
    )
    slope_three = evaluate(
        2, real_part + half_step * slope_two[0], imag_part + half_step * slope_two[1]
    )
    slope_four = evaluate(
        3, real_part + STEP_SIZE * slope_three[0], imag_part + STEP_SIZE * slope_three[1]
    )
    factor = STEP_SIZE / 6.0
    new_real = real_part + factor * (
        slope_one[0] + 2.0 * slope_two[0] + 2.0 * slope_three[0] + slope_four[0]
    )
    new_imag = imag_part + factor * (
        slope_one[1] + 2.0 * slope_two[1] + 2.0 * slope_three[1] + slope_four[1]
    )
    return (new_real, new_imag)


def body(amplitudes, couplings, block_index, bond_map, bond_strength, drive_amplitude):
    kinds = couplings.shape[1]
    col_count = couplings.shape[2]
    table_real = jnp.transpose(couplings[0], (2, 0, 1)).reshape(col_count, kinds * col_count)
    table_imag = jnp.transpose(couplings[1], (2, 0, 1)).reshape(col_count, kinds * col_count)
    table = jnp.concatenate([table_real, table_imag], 1)
    real_part = amplitudes[0]
    imag_part = amplitudes[1]
    row_count = real_part.shape[0]
    row_kind = jnp.repeat(block_index, BROWS, total_repeat_length=row_count)

    def evaluate(section, first, second):
        return evaluate_field(
            first, second, table, row_kind, kinds, bond_map, bond_strength, drive_amplitude[section]
        )

    new_real, new_imag = runge_kutta(real_part, imag_part, evaluate)
    return jnp.stack([new_real, new_imag])


SUBLANES = 8
VMEM_GRANT = 64 * 2**20 - 2**18
MESH = pl.DeviceIdType.MESH


def flipped(field, stride):
    row_count, col_count = field.shape
    if stride >= SUBLANES:
        folded = field.reshape(row_count // (2 * stride), 2, stride, col_count)
        return jnp.concatenate([folded[:, 1:], folded[:, :1]], 1).reshape(row_count, col_count)
    tiles = field.reshape(row_count // SUBLANES, SUBLANES, col_count)
    down = pltpu.roll(tiles, stride, 1)
    if 2 * stride < SUBLANES:
        row = lax.broadcasted_iota(jnp.int32, tiles.shape, 1)
        up = pltpu.roll(tiles, SUBLANES - stride, 1)
        down = jnp.where(row // stride % 2 == 1, down, up)
    return down.reshape(row_count, col_count)


def mixed_order(count):
    order = [0]
    while len(order) < count:
        order = [2 * place for place in order] + [2 * place + 1 for place in order]
    return order


def step_kernel(
    sizes,
    kind_hbm,
    bond_hbm,
    strength_hbm,
    drive_hbm,
    amp_ref,
    coup_ref,
    out_ref,
    kind_ref,
    bond_ref,
    strength_ref,
    drive_ref,
    stage,
    held,
    table,
    weight_high,
    weight_low,
    masks,
    diagonal,
    field,
    total,
    final,
    psi,
    back,
    landed,
    local_sem,
    send_sem,
    recv_sem,
):
    grp_size, dev_size, block_rows = sizes
    devices = grp_size * dev_size
    lead = spin_count(devices)
    parts, row_count, col_count = amp_ref.shape
    kinds = coup_ref.shape[1]
    sections = drive_ref.shape[0]
    share = row_count // devices
    planes = parts * share
    grp, dev = lax.axis_index("grp"), lax.axis_index("dev")
    me = grp * dev_size + dev
    grps = [grp] + [lax.rem(grp + hop, grp_size) for hop in range(1, grp_size)]
    devs = [dev] + [lax.rem(dev + hop, dev_size) for hop in range(1, dev_size)]
    hops = mixed_order(dev_size)
    others = [
        (grps[grp_hop] * dev_size + devs[dev_hop], (grps[grp_hop], devs[dev_hop]))
        for grp_hop in reversed(range(grp_size))
        for dev_hop in hops
        if grp_hop + dev_hop > 0
    ]
    loads = [
        pltpu.make_async_copy(source, target, local_sem.at[3 + index])
        for index, (source, target) in enumerate(
            (
                (kind_hbm, kind_ref),
                (amp_ref, final),
                (coup_ref, table),
                (bond_hbm, bond_ref),
                (strength_hbm, strength_ref),
                (drive_hbm, drive_ref),
            )
        )
    ]
    for load in loads[:2]:
        load.start()
    barrier = pltpu.get_barrier_semaphore()

    for _, where in others:
        pl.semaphore_signal(barrier, inc=1, device_id=where, device_id_type=MESH)
    for load in loads[2:]:
        load.start()
    loads[0].wait()
    owner = lax.broadcasted_iota(jnp.int32, (devices, col_count), 0) * share // block_rows
    kind_rows = jnp.zeros((devices, col_count), jnp.float32)
    for block in range(row_count // block_rows):
        kind_rows = jnp.where(owner == block, kind_ref[block].astype(jnp.float32), kind_rows)
    stage[pl.ds(planes, devices, stride=planes + 1), :] = kind_rows
    loads[1].wait()
    for part in range(parts):
        for spot in range(share):
            stage[pl.ds(part * share + spot, devices, stride=planes + 1), :] = final[
                part, pl.ds(spot, devices, stride=share), :
            ]
    pl.semaphore_wait(barrier, devices - 1)

    def exchange(source, target, phase):
        width = source.shape[0] // devices
        mine = pl.ds(me * width, width)
        for other, where in others:
            pltpu.make_async_remote_copy(
                src_ref=source.at[pl.ds(other * width, width)],
                dst_ref=target.at[mine],
                send_sem=send_sem.at[phase],
                recv_sem=recv_sem.at[phase],
                device_id=where,
                device_id_type=MESH,
            ).start()
        own = pltpu.make_async_copy(source.at[mine], target.at[mine], local_sem.at[phase])
        own.start()
        return own

    def finish(source, target, phase, own):
        own.wait()
        foreign = pl.ds(0, source.shape[0] // devices * (devices - 1))
        sent = source.at[foreign]
        pltpu.make_async_copy(sent, sent, send_sem.at[phase]).wait()
        came = target.at[foreign]
        pltpu.make_async_copy(came, came, recv_sem.at[phase]).wait()

    own = exchange(stage, held, 0)
    for load in loads[2:]:
        load.wait()

    def split(kind, carry):
        rows = pl.ds(pl.multiple_of(kind * col_count, col_count), col_count)
        for part in range(2):
            columns = slice(part * col_count, (part + 1) * col_count)
            full = table[part, kind]
            high = full.astype(jnp.bfloat16)
            weight_high[rows, columns] = high
            weight_low[rows, columns] = (full - high.astype(jnp.float32)).astype(jnp.bfloat16)
        return carry

    lax.fori_loop(0, kinds, split, 0)

    row = lax.broadcasted_iota(jnp.int32, (row_count, col_count), 0)
    column = lax.broadcasted_iota(jnp.int32, (row_count, col_count), 1)
    diag = jnp.zeros((row_count, col_count), jnp.float32)
    shuffles = []
    for spin in range(lead):
        target = bond_ref[spin]
        shuffles.append(jnp.bitwise_xor(column, jnp.left_shift(jnp.int32(1), target)))
        parity = jnp.bitwise_xor(
            jnp.right_shift(row % devices, spin), jnp.right_shift(column, target)
        )
        sign = (1 - 2 * jnp.bitwise_and(parity, 1)).astype(jnp.float32)
        diag = diag + strength_ref[spin] * sign
    diagonal[...] = diag

    finish(stage, held, 0, own)
    kind_now = held[pl.ds(planes, devices, stride=planes + 1), :]
    kind_now = jnp.concatenate([kind_now] * share, 0)
    for kind in range(kinds):
        masks[kind] = (kind_now == float(kind)).astype(jnp.float32).astype(jnp.bfloat16)
    for part in range(parts):
        for spot in range(share):
            came = held[pl.ds(part * share + spot, devices, stride=planes + 1), :]
            rows = slice(spot * devices, (spot + 1) * devices)
            psi[part, rows] = came
            field[part, rows] = came
    total[...] = jnp.zeros_like(total)

    def section(now, carry):
        both = jnp.concatenate([field[0], field[1]], 0)
        high = both.astype(jnp.bfloat16)
        low = (both - high.astype(jnp.float32)).astype(jnp.bfloat16)
        high_parts = []
        low_parts = []
        for kind in range(kinds):
            mask = jnp.concatenate([masks[kind], masks[kind]], 0)
            high_parts.append(high * mask)
            low_parts.append(low * mask)
        high_all = jnp.concatenate(high_parts, 1)
        low_all = jnp.concatenate(low_parts, 1)
        main = jnp.dot(
            jnp.concatenate([high_all, low_all], 0),
            weight_high[...],
            preferred_element_type=jnp.float32,
        )
        rest = jnp.dot(high_all, weight_low[...], preferred_element_type=jnp.float32)
        product = main[: 2 * row_count] + (main[2 * row_count :] + rest)
        from_real, from_imag = product[:row_count], product[row_count:]
        column_real = from_imag[:, :col_count] - from_real[:, col_count:]
        column_imag = -from_real[:, :col_count] - from_imag[:, col_count:]
        leads = []
        for part in range(2):
            here = field[part]
            other = diagonal[...] * here
            for spin in range(lead):
                there = flipped(here, 1 << spin)
                moved = jnp.take_along_axis(
                    there, shuffles[spin], axis=1, mode="promise_in_bounds"
                )
                other = other + strength_ref[spin] * moved + drive_ref[now, spin] * there
            leads.append(other)
        slope = (column_real + leads[1], column_imag - leads[0])
        edge = (now == 0) | (now == sections - 1)
        weight = jnp.where(edge, 1.0, 2.0)
        step = jnp.where(now == sections - 2, STEP_SIZE, 0.5 * STEP_SIZE)
        for part in range(2):
            total[part] = total[part] + weight * slope[part]
            field[part] = psi[part] + step * slope[part]
        return carry

    lax.fori_loop(0, sections, section, 0)
    final[...] = psi[...] + (STEP_SIZE / 6.0) * total[...]
    for part in range(parts):
        for spot in range(share):
            back[pl.ds(part * share + spot, devices, stride=planes), :] = final[
                part, spot * devices : (spot + 1) * devices
            ]
    own = exchange(back, landed, 1)
    finish(back, landed, 1, own)
    for part in range(parts):
        for spot in range(share):
            out_ref[part, pl.ds(spot, devices, stride=share), :] = landed[
                pl.ds(part * share + spot, devices, stride=planes), :
            ]


def body_by_rows(
    sizes, amplitudes, couplings, block_index, bond_map, bond_strength, drive_amplitude
):
    parts, row_count, col_count = amplitudes.shape
    kinds = couplings.shape[1]
    block_rows = row_count // block_index.shape[0]
    half = (parts, row_count, col_count)
    weight = pltpu.VMEM((kinds * col_count, 2 * col_count), jnp.bfloat16)
    homeward = pltpu.VMEM((parts * row_count, col_count), jnp.float32)
    outward = pltpu.VMEM((parts * row_count + sizes[0] * sizes[1], col_count), jnp.float32)
    return pl.pallas_call(
        functools.partial(step_kernel, (*sizes, block_rows)),
        out_shape=pltpu.VMEM(half, jnp.float32),
        in_specs=[pl.BlockSpec(memory_space=pltpu.HBM)] * 6,
        out_specs=pl.BlockSpec(memory_space=pltpu.VMEM),
        scratch_shapes=[
            pltpu.SMEM(block_index.shape, jnp.int32),
            pltpu.SMEM(bond_map.shape, jnp.int32),
            pltpu.SMEM(bond_strength.shape, jnp.float32),
            pltpu.SMEM(drive_amplitude.shape, jnp.float32),
            outward,
            outward,
            pltpu.VMEM(couplings.shape, jnp.float32),
            weight,
            weight,
            pltpu.VMEM((kinds, row_count, col_count), jnp.bfloat16),
            pltpu.VMEM((row_count, col_count), jnp.float32),
            pltpu.VMEM(half, jnp.float32),
            pltpu.VMEM(half, jnp.float32),
            pltpu.VMEM(half, jnp.float32),
            pltpu.VMEM(half, jnp.float32),
            homeward,
            homeward,
            pltpu.SemaphoreType.DMA((9,)),
            pltpu.SemaphoreType.DMA((2,)),
            pltpu.SemaphoreType.DMA((2,)),
        ],
        compiler_params=pltpu.CompilerParams(
            collective_id=0, has_side_effects=True, vmem_limit_bytes=VMEM_GRANT
        ),
    )(block_index, bond_map, bond_strength, drive_amplitude, amplitudes, couplings)


def chosen_body(sizes, amplitudes, couplings, block_index, *rest):
    row_count = amplitudes.shape[1]
    devices = sizes[0] * sizes[1]
    block_rows = row_count // block_index.shape[0]
    if row_count % devices == 0 and block_rows % (row_count // devices) == 0:
        return body_by_rows(sizes, amplitudes, couplings, block_index, *rest)
    return body(amplitudes, couplings, block_index, *rest)


def solution(mesh):
    in_specs = (P(None, ("grp", "dev"), None), P(), P(("grp", "dev")), P(), P(), P())
    out_specs = P(None, ("grp", "dev"), None)
    sizes = (mesh.shape["grp"], mesh.shape["dev"])
    return jax.shard_map(
        functools.partial(chosen_body, sizes),
        mesh=mesh,
        in_specs=in_specs,
        out_specs=out_specs,
        check_vma=False,
    )
```

```python
import functools

import jax
import jax.numpy as jnp
from jax import lax
from jax.experimental import pallas as pl
from jax.experimental.pallas import tpu as pltpu
from jax.sharding import PartitionSpec as P

BROWS = 16


STEP_SIZE = 0.5
HIGHEST = lax.Precision.HIGHEST


def swapped(shard, axis, distance):
    return lax.ppermute(shard, axis, [(i, i ^ 1 << distance) for i in range(lax.axis_size(axis))])


def spin_count(number):
    return number.bit_length() - 1


def flip_group(real_part, imag_part, bit_now):
    return swapped((real_part, imag_part), "grp", bit_now)


def coupled(real_part, imag_part, table, row_kind, kinds):
    row_count, col_count = real_part.shape
    product = jnp.dot(
        jnp.concatenate([real_part, imag_part], 0),
        table,
        precision=HIGHEST,
        preferred_element_type=jnp.float32,
    )
    extent = kinds * col_count
    left_part = product[:, :extent]
    right_part = product[:, extent:]
    all_real = left_part[:row_count] - right_part[row_count:]
    all_imag = left_part[row_count:] + right_part[:row_count]
    select = (row_kind[:, None] == jnp.arange(kinds, dtype=jnp.int32)[None, :]).astype(jnp.float32)[
        :, :, None
    ]
    out_real = jnp.sum(all_real.reshape(row_count, kinds, col_count) * select, axis=1)
    out_imag = jnp.sum(all_imag.reshape(row_count, kinds, col_count) * select, axis=1)
    return (out_real, out_imag)


def evaluate_field(
    real_part, imag_part, table, row_kind, kinds, bond_map, bond_strength, drive_row
):
    out_real, out_imag = coupled(real_part, imag_part, table, row_kind, kinds)
    row_count, col_count = real_part.shape
    dev_bits = spin_count(lax.axis_size("dev"))
    grp_bits = spin_count(lax.axis_size("grp"))
    columns = jnp.arange(col_count, dtype=jnp.int32)
    for lead_spin in range(dev_bits + grp_bits):
        target = bond_map[lead_spin]
        shuffle = jnp.bitwise_xor(columns, jnp.left_shift(jnp.int32(1), target))
        sign_col = (1 - 2 * jnp.bitwise_and(jnp.right_shift(columns, target), 1)).astype(
            jnp.float32
        )[None, :]
        if lead_spin < dev_bits:
            part_real, part_imag = swapped((real_part, imag_part), "dev", lead_spin)
            sign_lead = (
                1 - 2 * jnp.bitwise_and(jnp.right_shift(lax.axis_index("dev"), lead_spin), 1)
            ).astype(jnp.float32)
        else:
            part_real, part_imag = flip_group(real_part, imag_part, lead_spin - dev_bits)
            sign_lead = (
                1
                - 2
                * jnp.bitwise_and(jnp.right_shift(lax.axis_index("grp"), lead_spin - dev_bits), 1)
            ).astype(jnp.float32)
        strength = bond_strength[lead_spin]
        drive_now = drive_row[lead_spin]
        out_real = (
            out_real
            + strength * (sign_lead * sign_col * real_part + jnp.take(part_real, shuffle, axis=1))
            + drive_now * part_real
        )
        out_imag = (
            out_imag
            + strength * (sign_lead * sign_col * imag_part + jnp.take(part_imag, shuffle, axis=1))
            + drive_now * part_imag
        )
    return (out_imag, -out_real)


def runge_kutta(real_part, imag_part, evaluate):
    half_step = 0.5 * STEP_SIZE
    slope_one = evaluate(0, real_part, imag_part)
    slope_two = evaluate(
        1, real_part + half_step * slope_one[0], imag_part + half_step * slope_one[1]
    )
    slope_three = evaluate(
        2, real_part + half_step * slope_two[0], imag_part + half_step * slope_two[1]
    )
    slope_four = evaluate(
        3, real_part + STEP_SIZE * slope_three[0], imag_part + STEP_SIZE * slope_three[1]
    )
    factor = STEP_SIZE / 6.0
    new_real = real_part + factor * (
        slope_one[0] + 2.0 * slope_two[0] + 2.0 * slope_three[0] + slope_four[0]
    )
    new_imag = imag_part + factor * (
        slope_one[1] + 2.0 * slope_two[1] + 2.0 * slope_three[1] + slope_four[1]
    )
    return (new_real, new_imag)


def body(amplitudes, couplings, block_index, bond_map, bond_strength, drive_amplitude):
    kinds = couplings.shape[1]
    col_count = couplings.shape[2]
    table_real = jnp.transpose(couplings[0], (2, 0, 1)).reshape(col_count, kinds * col_count)
    table_imag = jnp.transpose(couplings[1], (2, 0, 1)).reshape(col_count, kinds * col_count)
    table = jnp.concatenate([table_real, table_imag], 1)
    real_part = amplitudes[0]
    imag_part = amplitudes[1]
    row_count = real_part.shape[0]
    row_kind = jnp.repeat(block_index, BROWS, total_repeat_length=row_count)

    def evaluate(section, first, second):
        return evaluate_field(
            first, second, table, row_kind, kinds, bond_map, bond_strength, drive_amplitude[section]
        )

    new_real, new_imag = runge_kutta(real_part, imag_part, evaluate)
    return jnp.stack([new_real, new_imag])


SUBLANES = 8
VMEM_GRANT = 64 * 2**20 - 2**18
MESH = pl.DeviceIdType.MESH


def flipped(field, stride):
    row_count, col_count = field.shape
    if stride >= SUBLANES:
        folded = field.reshape(row_count // (2 * stride), 2, stride, col_count)
        return jnp.concatenate([folded[:, 1:], folded[:, :1]], 1).reshape(row_count, col_count)
    tiles = field.reshape(row_count // SUBLANES, SUBLANES, col_count)
    down = pltpu.roll(tiles, stride, 1)
    if 2 * stride < SUBLANES:
        row = lax.broadcasted_iota(jnp.int32, tiles.shape, 1)
        up = pltpu.roll(tiles, SUBLANES - stride, 1)
        down = jnp.where(row // stride % 2 == 1, down, up)
    return down.reshape(row_count, col_count)


def step_kernel(
    sizes,
    kind_hbm,
    bond_hbm,
    strength_hbm,
    drive_hbm,
    amp_ref,
    coup_ref,
    out_ref,
    kind_ref,
    bond_ref,
    strength_ref,
    drive_ref,
    stage,
    held,
    table,
    weight_high,
    weight_low,
    masks,
    diagonal,
    field,
    total,
    final,
    psi,
    back,
    landed,
    local_sem,
    send_sem,
    recv_sem,
):
    grp_size, dev_size, block_rows = sizes
    devices = grp_size * dev_size
    lead = spin_count(devices)
    parts, row_count, col_count = amp_ref.shape
    kinds = coup_ref.shape[1]
    sections = drive_ref.shape[0]
    share = row_count // devices
    planes = parts * share
    grp, dev = lax.axis_index("grp"), lax.axis_index("dev")
    me = grp * dev_size + dev

    def for_others(action):
        def visit(hop, carry):
            there = lax.rem(grp + lax.div(hop, dev_size), grp_size)
            spot = lax.rem(dev + lax.rem(hop, dev_size), dev_size)
            action(there * dev_size + spot, (there, spot))
            return carry

        lax.fori_loop(1, devices, visit, 0)

    loads = [
        pltpu.make_async_copy(source, target, local_sem.at[3 + index])
        for index, (source, target) in enumerate(
            (
                (kind_hbm, kind_ref),
                (amp_ref, final),
                (coup_ref, table),
                (bond_hbm, bond_ref),
                (strength_hbm, strength_ref),
                (drive_hbm, drive_ref),
            )
        )
    ]
    for load in loads[:2]:
        load.start()
    barrier = pltpu.get_barrier_semaphore()

    for_others(
        lambda _, where: pl.semaphore_signal(
            barrier, inc=1, device_id=where, device_id_type=MESH
        )
    )
    for load in loads[2:]:
        load.start()
    loads[0].wait()
    owner = lax.broadcasted_iota(jnp.int32, (devices, col_count), 0) * share // block_rows
    kind_rows = jnp.zeros((devices, col_count), jnp.float32)
    for block in range(row_count // block_rows):
        kind_rows = jnp.where(owner == block, kind_ref[block].astype(jnp.float32), kind_rows)
    stage[pl.ds(planes, devices, stride=planes + 1), :] = kind_rows
    loads[1].wait()
    for part in range(parts):
        for spot in range(share):
            stage[pl.ds(part * share + spot, devices, stride=planes + 1), :] = final[
                part, pl.ds(spot, devices, stride=share), :
            ]
    pl.semaphore_wait(barrier, devices - 1)

    def exchange(source, target, phase):
        width = source.shape[0] // devices
        mine = pl.ds(me * width, width)

        def send(other, where):
            pltpu.make_async_remote_copy(
                src_ref=source.at[pl.ds(other * width, width)],
                dst_ref=target.at[mine],
                send_sem=send_sem.at[phase],
                recv_sem=recv_sem.at[phase],
                device_id=where,
                device_id_type=MESH,
            ).start()

        for_others(send)
        own = pltpu.make_async_copy(source.at[mine], target.at[mine], local_sem.at[phase])
        own.start()
        return own

    def finish(source, target, phase, own):
        own.wait()
        foreign = pl.ds(0, source.shape[0] // devices * (devices - 1))
        sent = source.at[foreign]
        pltpu.make_async_copy(sent, sent, send_sem.at[phase]).wait()
        came = target.at[foreign]
        pltpu.make_async_copy(came, came, recv_sem.at[phase]).wait()

    own = exchange(stage, held, 0)
    for load in loads[2:]:
        load.wait()

    def split(kind, carry):
        rows = pl.ds(pl.multiple_of(kind * col_count, col_count), col_count)
        for part in range(2):
            columns = slice(part * col_count, (part + 1) * col_count)
            full = table[part, kind]
            high = full.astype(jnp.bfloat16)
            weight_high[rows, columns] = high
            weight_low[rows, columns] = (full - high.astype(jnp.float32)).astype(jnp.bfloat16)
        return carry

    lax.fori_loop(0, kinds, split, 0)

    row = lax.broadcasted_iota(jnp.int32, (row_count, col_count), 0)
    column = lax.broadcasted_iota(jnp.int32, (row_count, col_count), 1)
    diag = jnp.zeros((row_count, col_count), jnp.float32)
    shuffles = []
    for spin in range(lead):
        target = bond_ref[spin]
        shuffles.append(jnp.bitwise_xor(column, jnp.left_shift(jnp.int32(1), target)))
        parity = jnp.bitwise_xor(
            jnp.right_shift(row % devices, spin), jnp.right_shift(column, target)
        )
        sign = (1 - 2 * jnp.bitwise_and(parity, 1)).astype(jnp.float32)
        diag = diag + strength_ref[spin] * sign
    diagonal[...] = diag

    finish(stage, held, 0, own)
    kind_now = held[pl.ds(planes, devices, stride=planes + 1), :]
    kind_now = jnp.concatenate([kind_now] * share, 0)
    for kind in range(kinds):
        masks[kind] = (kind_now == float(kind)).astype(jnp.float32).astype(jnp.bfloat16)
    for part in range(parts):
        for spot in range(share):
            came = held[pl.ds(part * share + spot, devices, stride=planes + 1), :]
            rows = slice(spot * devices, (spot + 1) * devices)
            psi[part, rows] = came
            field[part, rows] = came
    total[...] = jnp.zeros_like(total)

    def section(now, carry):
        both = jnp.concatenate([field[0], field[1]], 0)
        high = both.astype(jnp.bfloat16)
        low = (both - high.astype(jnp.float32)).astype(jnp.bfloat16)
        high_parts = []
        low_parts = []
        for kind in range(kinds):
            mask = jnp.concatenate([masks[kind], masks[kind]], 0)
            high_parts.append(high * mask)
            low_parts.append(low * mask)
        high_all = jnp.concatenate(high_parts, 1)
        low_all = jnp.concatenate(low_parts, 1)
        main = jnp.dot(
            jnp.concatenate([high_all, low_all], 0),
            weight_high[...],
            preferred_element_type=jnp.float32,
        )
        rest = jnp.dot(high_all, weight_low[...], preferred_element_type=jnp.float32)
        product = main[: 2 * row_count] + (main[2 * row_count :] + rest)
        from_real, from_imag = product[:row_count], product[row_count:]
        column_real = from_imag[:, :col_count] - from_real[:, col_count:]
        column_imag = -from_real[:, :col_count] - from_imag[:, col_count:]
        leads = []
        for part in range(2):
            here = field[part]
            other = diagonal[...] * here
            for spin in range(lead):
                there = flipped(here, 1 << spin)
                moved = jnp.take_along_axis(
                    there, shuffles[spin], axis=1, mode="promise_in_bounds"
                )
                other = other + strength_ref[spin] * moved + drive_ref[now, spin] * there
            leads.append(other)
        slope = (column_real + leads[1], column_imag - leads[0])
        edge = (now == 0) | (now == sections - 1)
        weight = jnp.where(edge, 1.0, 2.0)
        step = jnp.where(now == sections - 2, STEP_SIZE, 0.5 * STEP_SIZE)
        for part in range(2):
            total[part] = total[part] + weight * slope[part]
            field[part] = psi[part] + step * slope[part]
        return carry

    lax.fori_loop(0, sections, section, 0)
    final[...] = psi[...] + (STEP_SIZE / 6.0) * total[...]
    for part in range(parts):
        for spot in range(share):
            back[pl.ds(part * share + spot, devices, stride=planes), :] = final[
                part, spot * devices : (spot + 1) * devices
            ]
    own = exchange(back, landed, 1)
    finish(back, landed, 1, own)
    for part in range(parts):
        for spot in range(share):
            out_ref[part, pl.ds(spot, devices, stride=share), :] = landed[
                pl.ds(part * share + spot, devices, stride=planes), :
            ]


def body_by_rows(
    sizes, amplitudes, couplings, block_index, bond_map, bond_strength, drive_amplitude
):
    parts, row_count, col_count = amplitudes.shape
    kinds = couplings.shape[1]
    block_rows = row_count // block_index.shape[0]
    half = (parts, row_count, col_count)
    weight = pltpu.VMEM((kinds * col_count, 2 * col_count), jnp.bfloat16)
    homeward = pltpu.VMEM((parts * row_count, col_count), jnp.float32)
    outward = pltpu.VMEM((parts * row_count + sizes[0] * sizes[1], col_count), jnp.float32)
    return pl.pallas_call(
        functools.partial(step_kernel, (*sizes, block_rows)),
        out_shape=pltpu.VMEM(half, jnp.float32),
        in_specs=[pl.BlockSpec(memory_space=pltpu.HBM)] * 6,
        out_specs=pl.BlockSpec(memory_space=pltpu.VMEM),
        scratch_shapes=[
            pltpu.SMEM(block_index.shape, jnp.int32),
            pltpu.SMEM(bond_map.shape, jnp.int32),
            pltpu.SMEM(bond_strength.shape, jnp.float32),
            pltpu.SMEM(drive_amplitude.shape, jnp.float32),
            outward,
            outward,
            pltpu.VMEM(couplings.shape, jnp.float32),
            weight,
            weight,
            pltpu.VMEM((kinds, row_count, col_count), jnp.bfloat16),
            pltpu.VMEM((row_count, col_count), jnp.float32),
            pltpu.VMEM(half, jnp.float32),
            pltpu.VMEM(half, jnp.float32),
            pltpu.VMEM(half, jnp.float32),
            pltpu.VMEM(half, jnp.float32),
            homeward,
            homeward,
            pltpu.SemaphoreType.DMA((9,)),
            pltpu.SemaphoreType.DMA((2,)),
            pltpu.SemaphoreType.DMA((2,)),
        ],
        compiler_params=pltpu.CompilerParams(
            collective_id=0, has_side_effects=True, vmem_limit_bytes=VMEM_GRANT
        ),
    )(block_index, bond_map, bond_strength, drive_amplitude, amplitudes, couplings)


def chosen_body(sizes, amplitudes, couplings, block_index, *rest):
    row_count = amplitudes.shape[1]
    devices = sizes[0] * sizes[1]
    block_rows = row_count // block_index.shape[0]
    if row_count % devices == 0 and block_rows % (row_count // devices) == 0:
        return body_by_rows(sizes, amplitudes, couplings, block_index, *rest)
    return body(amplitudes, couplings, block_index, *rest)


def solution(mesh):
    in_specs = (P(None, ("grp", "dev"), None), P(), P(("grp", "dev")), P(), P(), P())
    out_specs = P(None, ("grp", "dev"), None)
    sizes = (mesh.shape["grp"], mesh.shape["dev"])
    return jax.shard_map(
        functools.partial(chosen_body, sizes),
        mesh=mesh,
        in_specs=in_specs,
        out_specs=out_specs,
        check_vma=False,
    )
```

```python
import functools

import jax
import jax.numpy as jnp
from jax import lax
from jax.experimental import pallas as pl
from jax.experimental.pallas import tpu as pltpu
from jax.sharding import PartitionSpec as P

BROWS = 16


STEP_SIZE = 0.5
HIGHEST = lax.Precision.HIGHEST


def swapped(shard, axis, distance):
    return lax.ppermute(shard, axis, [(i, i ^ 1 << distance) for i in range(lax.axis_size(axis))])


def spin_count(number):
    return number.bit_length() - 1


def flip_group(real_part, imag_part, bit_now):
    return swapped((real_part, imag_part), "grp", bit_now)


def coupled(real_part, imag_part, table, row_kind, kinds):
    row_count, col_count = real_part.shape
    product = jnp.dot(
        jnp.concatenate([real_part, imag_part], 0),
        table,
        precision=HIGHEST,
        preferred_element_type=jnp.float32,
    )
    extent = kinds * col_count
    left_part = product[:, :extent]
    right_part = product[:, extent:]
    all_real = left_part[:row_count] - right_part[row_count:]
    all_imag = left_part[row_count:] + right_part[:row_count]
    select = (row_kind[:, None] == jnp.arange(kinds, dtype=jnp.int32)[None, :]).astype(jnp.float32)[
        :, :, None
    ]
    out_real = jnp.sum(all_real.reshape(row_count, kinds, col_count) * select, axis=1)
    out_imag = jnp.sum(all_imag.reshape(row_count, kinds, col_count) * select, axis=1)
    return (out_real, out_imag)


def evaluate_field(
    real_part, imag_part, table, row_kind, kinds, bond_map, bond_strength, drive_row
):
    out_real, out_imag = coupled(real_part, imag_part, table, row_kind, kinds)
    row_count, col_count = real_part.shape
    dev_bits = spin_count(lax.axis_size("dev"))
    grp_bits = spin_count(lax.axis_size("grp"))
    columns = jnp.arange(col_count, dtype=jnp.int32)
    for lead_spin in range(dev_bits + grp_bits):
        target = bond_map[lead_spin]
        shuffle = jnp.bitwise_xor(columns, jnp.left_shift(jnp.int32(1), target))
        sign_col = (1 - 2 * jnp.bitwise_and(jnp.right_shift(columns, target), 1)).astype(
            jnp.float32
        )[None, :]
        if lead_spin < dev_bits:
            part_real, part_imag = swapped((real_part, imag_part), "dev", lead_spin)
            sign_lead = (
                1 - 2 * jnp.bitwise_and(jnp.right_shift(lax.axis_index("dev"), lead_spin), 1)
            ).astype(jnp.float32)
        else:
            part_real, part_imag = flip_group(real_part, imag_part, lead_spin - dev_bits)
            sign_lead = (
                1
                - 2
                * jnp.bitwise_and(jnp.right_shift(lax.axis_index("grp"), lead_spin - dev_bits), 1)
            ).astype(jnp.float32)
        strength = bond_strength[lead_spin]
        drive_now = drive_row[lead_spin]
        out_real = (
            out_real
            + strength * (sign_lead * sign_col * real_part + jnp.take(part_real, shuffle, axis=1))
            + drive_now * part_real
        )
        out_imag = (
            out_imag
            + strength * (sign_lead * sign_col * imag_part + jnp.take(part_imag, shuffle, axis=1))
            + drive_now * part_imag
        )
    return (out_imag, -out_real)


def runge_kutta(real_part, imag_part, evaluate):
    half_step = 0.5 * STEP_SIZE
    slope_one = evaluate(0, real_part, imag_part)
    slope_two = evaluate(
        1, real_part + half_step * slope_one[0], imag_part + half_step * slope_one[1]
    )
    slope_three = evaluate(
        2, real_part + half_step * slope_two[0], imag_part + half_step * slope_two[1]
    )
    slope_four = evaluate(
        3, real_part + STEP_SIZE * slope_three[0], imag_part + STEP_SIZE * slope_three[1]
    )
    factor = STEP_SIZE / 6.0
    new_real = real_part + factor * (
        slope_one[0] + 2.0 * slope_two[0] + 2.0 * slope_three[0] + slope_four[0]
    )
    new_imag = imag_part + factor * (
        slope_one[1] + 2.0 * slope_two[1] + 2.0 * slope_three[1] + slope_four[1]
    )
    return (new_real, new_imag)


def body(amplitudes, couplings, block_index, bond_map, bond_strength, drive_amplitude):
    kinds = couplings.shape[1]
    col_count = couplings.shape[2]
    table_real = jnp.transpose(couplings[0], (2, 0, 1)).reshape(col_count, kinds * col_count)
    table_imag = jnp.transpose(couplings[1], (2, 0, 1)).reshape(col_count, kinds * col_count)
    table = jnp.concatenate([table_real, table_imag], 1)
    real_part = amplitudes[0]
    imag_part = amplitudes[1]
    row_count = real_part.shape[0]
    row_kind = jnp.repeat(block_index, BROWS, total_repeat_length=row_count)

    def evaluate(section, first, second):
        return evaluate_field(
            first, second, table, row_kind, kinds, bond_map, bond_strength, drive_amplitude[section]
        )

    new_real, new_imag = runge_kutta(real_part, imag_part, evaluate)
    return jnp.stack([new_real, new_imag])


SUBLANES = 8
VMEM_GRANT = 64 * 2**20 - 2**18
MESH = pl.DeviceIdType.MESH


def flipped(field, stride):
    row_count, col_count = field.shape
    if stride >= SUBLANES:
        folded = field.reshape(row_count // (2 * stride), 2, stride, col_count)
        return jnp.concatenate([folded[:, 1:], folded[:, :1]], 1).reshape(row_count, col_count)
    tiles = field.reshape(row_count // SUBLANES, SUBLANES, col_count)
    down = pltpu.roll(tiles, stride, 1)
    if 2 * stride < SUBLANES:
        row = lax.broadcasted_iota(jnp.int32, tiles.shape, 1)
        up = pltpu.roll(tiles, SUBLANES - stride, 1)
        down = jnp.where(row // stride % 2 == 1, down, up)
    return down.reshape(row_count, col_count)


def mixed_order(count):
    order = [0]
    while len(order) < count:
        order = [2 * place for place in order] + [2 * place + 1 for place in order]
    return order


def step_kernel(
    sizes,
    kind_hbm,
    bond_hbm,
    strength_hbm,
    drive_hbm,
    amp_ref,
    coup_ref,
    out_ref,
    kind_ref,
    bond_ref,
    strength_ref,
    drive_ref,
    stage,
    held,
    table,
    weight_high,
    weight_low,
    masks,
    diagonal,
    field,
    total,
    final,
    psi,
    back,
    landed,
    local_sem,
    send_sem,
    recv_sem,
):
    grp_size, dev_size, block_rows = sizes
    devices = grp_size * dev_size
    lead = spin_count(devices)
    parts, row_count, col_count = amp_ref.shape
    kinds = coup_ref.shape[1]
    sections = drive_ref.shape[0]
    share = row_count // devices
    planes = parts * share
    grp, dev = lax.axis_index("grp"), lax.axis_index("dev")
    me = grp * dev_size + dev
    grps = [grp] + [lax.rem(grp + hop, grp_size) for hop in range(1, grp_size)]
    devs = [dev] + [lax.rem(dev + hop, dev_size) for hop in range(1, dev_size)]
    shift = lax.rem(grp, 2) * (dev_size // 4)
    turned = [lax.rem(dev + hop + shift, dev_size) for hop in range(dev_size)]
    others = []
    for grp_hop in reversed(range(grp_size)):
        row_of = turned if grp_hop else devs
        for dev_hop in mixed_order(dev_size):
            if grp_hop + dev_hop > 0:
                where = (grps[grp_hop], row_of[dev_hop])
                others.append((where[0] * dev_size + where[1], where))
    barrier = pltpu.get_barrier_semaphore()
    for dev_hop in sorted(range(dev_size), key=lambda hop: -min(hop, dev_size - hop)):
        for grp_hop in reversed(range(grp_size)):
            if grp_hop + dev_hop > 0:
                pl.semaphore_signal(
                    barrier,
                    inc=1,
                    device_id=(grps[grp_hop], devs[dev_hop]),
                    device_id_type=MESH,
                )
    loads = [
        pltpu.make_async_copy(source, target, local_sem.at[3 + index])
        for index, (source, target) in enumerate(
            (
                (kind_hbm, kind_ref),
                (amp_ref, final),
                (coup_ref, table),
                (bond_hbm, bond_ref),
                (strength_hbm, strength_ref),
                (drive_hbm, drive_ref),
            )
        )
    ]
    for load in loads:
        load.start()
    loads[0].wait()
    owner = lax.broadcasted_iota(jnp.int32, (devices, col_count), 0) * share // block_rows
    kind_rows = jnp.zeros((devices, col_count), jnp.float32)
    for block in range(row_count // block_rows):
        kind_rows = jnp.where(owner == block, kind_ref[block].astype(jnp.float32), kind_rows)
    stage[pl.ds(planes, devices, stride=planes + 1), :] = kind_rows
    loads[1].wait()
    for part in range(parts):
        for spot in range(share):
            stage[pl.ds(part * share + spot, devices, stride=planes + 1), :] = final[
                part, pl.ds(spot, devices, stride=share), :
            ]
    pl.semaphore_wait(barrier, devices - 1)

    def exchange(source, target, phase):
        width = source.shape[0] // devices
        mine = pl.ds(me * width, width)
        for other, where in others:
            pltpu.make_async_remote_copy(
                src_ref=source.at[pl.ds(other * width, width)],
                dst_ref=target.at[mine],
                send_sem=send_sem.at[phase],
                recv_sem=recv_sem.at[phase],
                device_id=where,
                device_id_type=MESH,
            ).start()
        own = pltpu.make_async_copy(source.at[mine], target.at[mine], local_sem.at[phase])
        own.start()
        return own

    def finish(source, target, phase, own):
        own.wait()
        foreign = pl.ds(0, source.shape[0] // devices * (devices - 1))
        sent = source.at[foreign]
        pltpu.make_async_copy(sent, sent, send_sem.at[phase]).wait()
        came = target.at[foreign]
        pltpu.make_async_copy(came, came, recv_sem.at[phase]).wait()

    own = exchange(stage, held, 0)
    for load in loads[2:]:
        load.wait()

    def split(kind, carry):
        rows = pl.ds(pl.multiple_of(kind * col_count, col_count), col_count)
        for part in range(2):
            columns = slice(part * col_count, (part + 1) * col_count)
            full = table[part, kind]
            high = full.astype(jnp.bfloat16)
            weight_high[rows, columns] = high
            weight_low[rows, columns] = (full - high.astype(jnp.float32)).astype(jnp.bfloat16)
        return carry

    lax.fori_loop(0, kinds, split, 0)

    row = lax.broadcasted_iota(jnp.int32, (row_count, col_count), 0)
    column = lax.broadcasted_iota(jnp.int32, (row_count, col_count), 1)
    diag = jnp.zeros((row_count, col_count), jnp.float32)
    shuffles = []
    for spin in range(lead):
        target = bond_ref[spin]
        shuffles.append(jnp.bitwise_xor(column, jnp.left_shift(jnp.int32(1), target)))
        parity = jnp.bitwise_xor(
            jnp.right_shift(row % devices, spin), jnp.right_shift(column, target)
        )
        sign = (1 - 2 * jnp.bitwise_and(parity, 1)).astype(jnp.float32)
        diag = diag + strength_ref[spin] * sign
    diagonal[...] = diag

    finish(stage, held, 0, own)
    kind_now = held[pl.ds(planes, devices, stride=planes + 1), :]
    kind_now = jnp.concatenate([kind_now] * share, 0)
    for kind in range(kinds):
        masks[kind] = (kind_now == float(kind)).astype(jnp.float32).astype(jnp.bfloat16)
    for part in range(parts):
        for spot in range(share):
            came = held[pl.ds(part * share + spot, devices, stride=planes + 1), :]
            rows = slice(spot * devices, (spot + 1) * devices)
            psi[part, rows] = came
            field[part, rows] = came
    total[...] = jnp.zeros_like(total)

    def section(now, carry):
        both = jnp.concatenate([field[0], field[1]], 0)
        high = both.astype(jnp.bfloat16)
        low = (both - high.astype(jnp.float32)).astype(jnp.bfloat16)
        high_parts = []
        low_parts = []
        for kind in range(kinds):
            mask = jnp.concatenate([masks[kind], masks[kind]], 0)
            high_parts.append(high * mask)
            low_parts.append(low * mask)
        high_all = jnp.concatenate(high_parts, 1)
        low_all = jnp.concatenate(low_parts, 1)
        main = jnp.dot(
            jnp.concatenate([high_all, low_all], 0),
            weight_high[...],
            preferred_element_type=jnp.float32,
        )
        rest = jnp.dot(high_all, weight_low[...], preferred_element_type=jnp.float32)
        product = main[: 2 * row_count] + (main[2 * row_count :] + rest)
        from_real, from_imag = product[:row_count], product[row_count:]
        column_real = from_imag[:, :col_count] - from_real[:, col_count:]
        column_imag = -from_real[:, :col_count] - from_imag[:, col_count:]
        leads = []
        for part in range(2):
            here = field[part]
            other = diagonal[...] * here
            for spin in range(lead):
                there = flipped(here, 1 << spin)
                moved = jnp.take_along_axis(
                    there, shuffles[spin], axis=1, mode="promise_in_bounds"
                )
                other = other + strength_ref[spin] * moved + drive_ref[now, spin] * there
            leads.append(other)
        slope = (column_real + leads[1], column_imag - leads[0])
        edge = (now == 0) | (now == sections - 1)
        weight = jnp.where(edge, 1.0, 2.0)
        step = jnp.where(now == sections - 2, STEP_SIZE, 0.5 * STEP_SIZE)
        for part in range(2):
            total[part] = total[part] + weight * slope[part]
            field[part] = psi[part] + step * slope[part]
        return carry

    lax.fori_loop(0, sections, section, 0)
    final[...] = psi[...] + (STEP_SIZE / 6.0) * total[...]
    for part in range(parts):
        for spot in range(share):
            back[pl.ds(part * share + spot, devices, stride=planes), :] = final[
                part, spot * devices : (spot + 1) * devices
            ]
    own = exchange(back, landed, 1)
    finish(back, landed, 1, own)
    for part in range(parts):
        for spot in range(share):
            out_ref[part, pl.ds(spot, devices, stride=share), :] = landed[
                pl.ds(part * share + spot, devices, stride=planes), :
            ]


def body_by_rows(
    sizes, amplitudes, couplings, block_index, bond_map, bond_strength, drive_amplitude
):
    parts, row_count, col_count = amplitudes.shape
    kinds = couplings.shape[1]
    block_rows = row_count // block_index.shape[0]
    half = (parts, row_count, col_count)
    weight = pltpu.VMEM((kinds * col_count, 2 * col_count), jnp.bfloat16)
    homeward = pltpu.VMEM((parts * row_count, col_count), jnp.float32)
    outward = pltpu.VMEM((parts * row_count + sizes[0] * sizes[1], col_count), jnp.float32)
    return pl.pallas_call(
        functools.partial(step_kernel, (*sizes, block_rows)),
        out_shape=pltpu.VMEM(half, jnp.float32),
        in_specs=[pl.BlockSpec(memory_space=pltpu.HBM)] * 6,
        out_specs=pl.BlockSpec(memory_space=pltpu.VMEM),
        scratch_shapes=[
            pltpu.SMEM(block_index.shape, jnp.int32),
            pltpu.SMEM(bond_map.shape, jnp.int32),
            pltpu.SMEM(bond_strength.shape, jnp.float32),
            pltpu.SMEM(drive_amplitude.shape, jnp.float32),
            outward,
            outward,
            pltpu.VMEM(couplings.shape, jnp.float32),
            weight,
            weight,
            pltpu.VMEM((kinds, row_count, col_count), jnp.bfloat16),
            pltpu.VMEM((row_count, col_count), jnp.float32),
            pltpu.VMEM(half, jnp.float32),
            pltpu.VMEM(half, jnp.float32),
            pltpu.VMEM(half, jnp.float32),
            pltpu.VMEM(half, jnp.float32),
            homeward,
            homeward,
            pltpu.SemaphoreType.DMA((9,)),
            pltpu.SemaphoreType.DMA((2,)),
            pltpu.SemaphoreType.DMA((2,)),
        ],
        compiler_params=pltpu.CompilerParams(
            collective_id=0, has_side_effects=True, vmem_limit_bytes=VMEM_GRANT
        ),
    )(block_index, bond_map, bond_strength, drive_amplitude, amplitudes, couplings)


def chosen_body(sizes, amplitudes, couplings, block_index, *rest):
    row_count = amplitudes.shape[1]
    devices = sizes[0] * sizes[1]
    block_rows = row_count // block_index.shape[0]
    if row_count % devices == 0 and block_rows % (row_count // devices) == 0:
        return body_by_rows(sizes, amplitudes, couplings, block_index, *rest)
    return body(amplitudes, couplings, block_index, *rest)


def solution(mesh):
    in_specs = (P(None, ("grp", "dev"), None), P(), P(("grp", "dev")), P(), P(), P())
    out_specs = P(None, ("grp", "dev"), None)
    sizes = (mesh.shape["grp"], mesh.shape["dev"])
    return jax.shard_map(
        functools.partial(chosen_body, sizes),
        mesh=mesh,
        in_specs=in_specs,
        out_specs=out_specs,
        check_vma=False,
    )
```

```python
import functools

import jax
import jax.numpy as jnp
from jax import lax
from jax.experimental import pallas as pl
from jax.experimental.pallas import tpu as pltpu
from jax.sharding import PartitionSpec as P

BROWS = 16


STEP_SIZE = 0.5
HIGHEST = lax.Precision.HIGHEST


def swapped(shard, axis, distance):
    return lax.ppermute(shard, axis, [(i, i ^ 1 << distance) for i in range(lax.axis_size(axis))])


def spin_count(number):
    return number.bit_length() - 1


def flip_group(real_part, imag_part, bit_now):
    return swapped((real_part, imag_part), "grp", bit_now)


def coupled(real_part, imag_part, table, row_kind, kinds):
    row_count, col_count = real_part.shape
    product = jnp.dot(
        jnp.concatenate([real_part, imag_part], 0),
        table,
        precision=HIGHEST,
        preferred_element_type=jnp.float32,
    )
    extent = kinds * col_count
    left_part = product[:, :extent]
    right_part = product[:, extent:]
    all_real = left_part[:row_count] - right_part[row_count:]
    all_imag = left_part[row_count:] + right_part[:row_count]
    select = (row_kind[:, None] == jnp.arange(kinds, dtype=jnp.int32)[None, :]).astype(jnp.float32)[
        :, :, None
    ]
    out_real = jnp.sum(all_real.reshape(row_count, kinds, col_count) * select, axis=1)
    out_imag = jnp.sum(all_imag.reshape(row_count, kinds, col_count) * select, axis=1)
    return (out_real, out_imag)


def evaluate_field(
    real_part, imag_part, table, row_kind, kinds, bond_map, bond_strength, drive_row
):
    out_real, out_imag = coupled(real_part, imag_part, table, row_kind, kinds)
    row_count, col_count = real_part.shape
    dev_bits = spin_count(lax.axis_size("dev"))
    grp_bits = spin_count(lax.axis_size("grp"))
    columns = jnp.arange(col_count, dtype=jnp.int32)
    for lead_spin in range(dev_bits + grp_bits):
        target = bond_map[lead_spin]
        shuffle = jnp.bitwise_xor(columns, jnp.left_shift(jnp.int32(1), target))
        sign_col = (1 - 2 * jnp.bitwise_and(jnp.right_shift(columns, target), 1)).astype(
            jnp.float32
        )[None, :]
        if lead_spin < dev_bits:
            part_real, part_imag = swapped((real_part, imag_part), "dev", lead_spin)
            sign_lead = (
                1 - 2 * jnp.bitwise_and(jnp.right_shift(lax.axis_index("dev"), lead_spin), 1)
            ).astype(jnp.float32)
        else:
            part_real, part_imag = flip_group(real_part, imag_part, lead_spin - dev_bits)
            sign_lead = (
                1
                - 2
                * jnp.bitwise_and(jnp.right_shift(lax.axis_index("grp"), lead_spin - dev_bits), 1)
            ).astype(jnp.float32)
        strength = bond_strength[lead_spin]
        drive_now = drive_row[lead_spin]
        out_real = (
            out_real
            + strength * (sign_lead * sign_col * real_part + jnp.take(part_real, shuffle, axis=1))
            + drive_now * part_real
        )
        out_imag = (
            out_imag
            + strength * (sign_lead * sign_col * imag_part + jnp.take(part_imag, shuffle, axis=1))
            + drive_now * part_imag
        )
    return (out_imag, -out_real)


def runge_kutta(real_part, imag_part, evaluate):
    half_step = 0.5 * STEP_SIZE
    slope_one = evaluate(0, real_part, imag_part)
    slope_two = evaluate(
        1, real_part + half_step * slope_one[0], imag_part + half_step * slope_one[1]
    )
    slope_three = evaluate(
        2, real_part + half_step * slope_two[0], imag_part + half_step * slope_two[1]
    )
    slope_four = evaluate(
        3, real_part + STEP_SIZE * slope_three[0], imag_part + STEP_SIZE * slope_three[1]
    )
    factor = STEP_SIZE / 6.0
    new_real = real_part + factor * (
        slope_one[0] + 2.0 * slope_two[0] + 2.0 * slope_three[0] + slope_four[0]
    )
    new_imag = imag_part + factor * (
        slope_one[1] + 2.0 * slope_two[1] + 2.0 * slope_three[1] + slope_four[1]
    )
    return (new_real, new_imag)


def body(amplitudes, couplings, block_index, bond_map, bond_strength, drive_amplitude):
    kinds = couplings.shape[1]
    col_count = couplings.shape[2]
    table_real = jnp.transpose(couplings[0], (2, 0, 1)).reshape(col_count, kinds * col_count)
    table_imag = jnp.transpose(couplings[1], (2, 0, 1)).reshape(col_count, kinds * col_count)
    table = jnp.concatenate([table_real, table_imag], 1)
    real_part = amplitudes[0]
    imag_part = amplitudes[1]
    row_count = real_part.shape[0]
    row_kind = jnp.repeat(block_index, BROWS, total_repeat_length=row_count)

    def evaluate(section, first, second):
        return evaluate_field(
            first, second, table, row_kind, kinds, bond_map, bond_strength, drive_amplitude[section]
        )

    new_real, new_imag = runge_kutta(real_part, imag_part, evaluate)
    return jnp.stack([new_real, new_imag])


SUBLANES = 8
VMEM_GRANT = 64 * 2**20 - 2**18
MESH = pl.DeviceIdType.MESH


def flipped(field, stride):
    row_count, col_count = field.shape
    if stride >= SUBLANES:
        folded = field.reshape(row_count // (2 * stride), 2, stride, col_count)
        return jnp.concatenate([folded[:, 1:], folded[:, :1]], 1).reshape(row_count, col_count)
    tiles = field.reshape(row_count // SUBLANES, SUBLANES, col_count)
    down = pltpu.roll(tiles, stride, 1)
    if 2 * stride < SUBLANES:
        row = lax.broadcasted_iota(jnp.int32, tiles.shape, 1)
        up = pltpu.roll(tiles, SUBLANES - stride, 1)
        down = jnp.where(row // stride % 2 == 1, down, up)
    return down.reshape(row_count, col_count)


def mixed_order(count):
    order = [0]
    while len(order) < count:
        order = [2 * place for place in order] + [2 * place + 1 for place in order]
    return order


def step_kernel(
    sizes,
    kind_hbm,
    bond_hbm,
    strength_hbm,
    drive_hbm,
    amp_ref,
    coup_ref,
    out_ref,
    kind_ref,
    bond_ref,
    strength_ref,
    drive_ref,
    stage,
    held,
    table,
    weight_high,
    weight_low,
    masks,
    diagonal,
    field,
    total,
    final,
    psi,
    back,
    landed,
    local_sem,
    send_sem,
    recv_sem,
):
    grp_size, dev_size, block_rows = sizes
    devices = grp_size * dev_size
    lead = spin_count(devices)
    parts, row_count, col_count = amp_ref.shape
    kinds = coup_ref.shape[1]
    sections = drive_ref.shape[0]
    share = row_count // devices
    planes = parts * share
    grp, dev = lax.axis_index("grp"), lax.axis_index("dev")
    me = grp * dev_size + dev
    grps = [grp] + [lax.rem(grp + hop, grp_size) for hop in range(1, grp_size)]
    devs = [dev] + [lax.rem(dev + hop, dev_size) for hop in range(1, dev_size)]
    shift = lax.rem(grp, 2) * (dev_size // 4)
    turned = [lax.rem(dev + hop + shift, dev_size) for hop in range(dev_size)]
    others = []
    for grp_hop in reversed(range(grp_size)):
        row_of = turned if grp_hop else devs
        for dev_hop in mixed_order(dev_size):
            if grp_hop + dev_hop > 0:
                where = (grps[grp_hop], row_of[dev_hop])
                others.append((where[0] * dev_size + where[1], where))
    barrier = pltpu.get_barrier_semaphore()
    for dev_hop in sorted(range(dev_size), key=lambda hop: -min(hop, dev_size - hop)):
        for grp_hop in reversed(range(grp_size)):
            if grp_hop + dev_hop > 0:
                pl.semaphore_signal(
                    barrier,
                    inc=1,
                    device_id=(grps[grp_hop], devs[dev_hop]),
                    device_id_type=MESH,
                )
    loads = [
        pltpu.make_async_copy(source, target, local_sem.at[3 + index])
        for index, (source, target) in enumerate(
            (
                (kind_hbm, kind_ref),
                (amp_ref, final),
                (coup_ref, table),
                (bond_hbm, bond_ref),
                (strength_hbm, strength_ref),
                (drive_hbm, drive_ref),
            )
        )
    ]
    for load in loads:
        load.start()
    loads[0].wait()
    owner = lax.broadcasted_iota(jnp.int32, (devices, col_count), 0) * share // block_rows
    kind_rows = jnp.zeros((devices, col_count), jnp.float32)
    for block in range(row_count // block_rows):
        kind_rows = jnp.where(owner == block, kind_ref[block].astype(jnp.float32), kind_rows)
    stage[pl.ds(planes, devices, stride=planes + 1), :] = kind_rows
    loads[1].wait()
    for part in range(parts):
        for spot in range(share):
            stage[pl.ds(part * share + spot, devices, stride=planes + 1), :] = final[
                part, pl.ds(spot, devices, stride=share), :
            ]
    pl.semaphore_wait(barrier, devices - 1)

    def exchange(source, target, phase):
        width = source.shape[0] // devices
        mine = pl.ds(me * width, width)
        for other, where in others:
            pltpu.make_async_remote_copy(
                src_ref=source.at[pl.ds(other * width, width)],
                dst_ref=target.at[mine],
                send_sem=send_sem.at[phase],
                recv_sem=recv_sem.at[phase],
                device_id=where,
                device_id_type=MESH,
            ).start()
        own = pltpu.make_async_copy(source.at[mine], target.at[mine], local_sem.at[phase])
        own.start()
        return own

    def finish(source, target, phase, own):
        own.wait()
        foreign = pl.ds(0, source.shape[0] // devices * (devices - 1))
        sent = source.at[foreign]
        pltpu.make_async_copy(sent, sent, send_sem.at[phase]).wait()
        came = target.at[foreign]
        pltpu.make_async_copy(came, came, recv_sem.at[phase]).wait()

    own = exchange(stage, held, 0)
    for load in loads[2:]:
        load.wait()

    def split(kind, carry):
        rows = pl.ds(pl.multiple_of(kind * col_count, col_count), col_count)
        for part in range(2):
            columns = slice(part * col_count, (part + 1) * col_count)
            full = table[part, kind]
            high = full.astype(jnp.bfloat16)
            weight_high[rows, columns] = high
            weight_low[rows, columns] = (full - high.astype(jnp.float32)).astype(jnp.bfloat16)
        return carry

    lax.fori_loop(0, kinds, split, 0)

    row = lax.broadcasted_iota(jnp.int32, (row_count, col_count), 0)
    column = lax.broadcasted_iota(jnp.int32, (row_count, col_count), 1)
    diag = jnp.zeros((row_count, col_count), jnp.float32)
    entry = lax.broadcasted_iota(jnp.int32, (col_count, col_count), 0)
    exit_column = lax.broadcasted_iota(jnp.int32, (col_count, col_count), 1)
    for spin in range(lead):
        target = bond_ref[spin]
        shuffle = entry == jnp.bitwise_xor(exit_column, jnp.left_shift(jnp.int32(1), target))
        rows = slice((kinds + spin) * col_count, (kinds + spin + 1) * col_count)
        weight_high[rows, :col_count] = shuffle.astype(jnp.float32).astype(jnp.bfloat16)
        weight_high[rows, col_count:] = jnp.zeros((col_count, col_count), jnp.bfloat16)
        parity = jnp.bitwise_xor(
            jnp.right_shift(row % devices, spin), jnp.right_shift(column, target)
        )
        sign = (1 - 2 * jnp.bitwise_and(parity, 1)).astype(jnp.float32)
        diag = diag + strength_ref[spin] * sign
    diagonal[...] = diag

    finish(stage, held, 0, own)
    kind_now = held[pl.ds(planes, devices, stride=planes + 1), :]
    kind_now = jnp.concatenate([kind_now] * share, 0)
    for kind in range(kinds):
        masks[kind] = (kind_now == float(kind)).astype(jnp.float32).astype(jnp.bfloat16)
    for part in range(parts):
        for spot in range(share):
            came = held[pl.ds(part * share + spot, devices, stride=planes + 1), :]
            rows = slice(spot * devices, (spot + 1) * devices)
            psi[part, rows] = came
            field[part, rows] = came
    total[...] = jnp.zeros_like(total)

    def section(now, carry):
        both = jnp.concatenate([field[0], field[1]], 0)
        high = both.astype(jnp.bfloat16)
        low = (both - high.astype(jnp.float32)).astype(jnp.bfloat16)
        high_parts = []
        low_parts = []
        for kind in range(kinds):
            mask = jnp.concatenate([masks[kind], masks[kind]], 0)
            high_parts.append(high * mask)
            low_parts.append(low * mask)
        others_high = []
        others_low = []
        leads = [diagonal[...] * field[part] for part in range(parts)]
        for spin in range(lead):
            there = [flipped(field[part], 1 << spin) for part in range(parts)]
            for part in range(parts):
                leads[part] = leads[part] + drive_ref[now, spin] * there[part]
            scaled = strength_ref[spin] * jnp.concatenate(there, 0)
            scaled_high = scaled.astype(jnp.bfloat16)
            others_high.append(scaled_high)
            others_low.append((scaled - scaled_high.astype(jnp.float32)).astype(jnp.bfloat16))
        high_all = jnp.concatenate(high_parts, 1)
        main_left = jnp.concatenate(
            [
                jnp.concatenate(high_parts + others_high, 1),
                jnp.concatenate(low_parts + others_low, 1),
            ],
            0,
        )
        main = jnp.dot(
            main_left,
            weight_high[...],
            preferred_element_type=jnp.float32,
        )
        rest = jnp.dot(high_all, weight_low[...], preferred_element_type=jnp.float32)
        product = main[: 2 * row_count] + (main[2 * row_count :] + rest)
        from_real, from_imag = product[:row_count], product[row_count:]
        column_real = from_imag[:, :col_count] - from_real[:, col_count:]
        column_imag = -from_real[:, :col_count] - from_imag[:, col_count:]
        slope = (column_real + leads[1], column_imag - leads[0])
        edge = (now == 0) | (now == sections - 1)
        weight = jnp.where(edge, 1.0, 2.0)
        step = jnp.where(now == sections - 2, STEP_SIZE, 0.5 * STEP_SIZE)
        for part in range(2):
            total[part] = total[part] + weight * slope[part]
            field[part] = psi[part] + step * slope[part]
        return carry

    lax.fori_loop(0, sections, section, 0)
    final[...] = psi[...] + (STEP_SIZE / 6.0) * total[...]
    for part in range(parts):
        for spot in range(share):
            back[pl.ds(part * share + spot, devices, stride=planes), :] = final[
                part, spot * devices : (spot + 1) * devices
            ]
    own = exchange(back, landed, 1)
    finish(back, landed, 1, own)
    for part in range(parts):
        for spot in range(share):
            out_ref[part, pl.ds(spot, devices, stride=share), :] = landed[
                pl.ds(part * share + spot, devices, stride=planes), :
            ]


def body_by_rows(
    sizes, amplitudes, couplings, block_index, bond_map, bond_strength, drive_amplitude
):
    parts, row_count, col_count = amplitudes.shape
    kinds = couplings.shape[1]
    block_rows = row_count // block_index.shape[0]
    half = (parts, row_count, col_count)
    lead = spin_count(sizes[0] * sizes[1])
    homeward = pltpu.VMEM((parts * row_count, col_count), jnp.float32)
    outward = pltpu.VMEM((parts * row_count + sizes[0] * sizes[1], col_count), jnp.float32)
    return pl.pallas_call(
        functools.partial(step_kernel, (*sizes, block_rows)),
        out_shape=pltpu.VMEM(half, jnp.float32),
        in_specs=[pl.BlockSpec(memory_space=pltpu.HBM)] * 6,
        out_specs=pl.BlockSpec(memory_space=pltpu.VMEM),
        scratch_shapes=[
            pltpu.SMEM(block_index.shape, jnp.int32),
            pltpu.SMEM(bond_map.shape, jnp.int32),
            pltpu.SMEM(bond_strength.shape, jnp.float32),
            pltpu.SMEM(drive_amplitude.shape, jnp.float32),
            outward,
            outward,
            pltpu.VMEM(couplings.shape, jnp.float32),
            pltpu.VMEM(((kinds + lead) * col_count, 2 * col_count), jnp.bfloat16),
            pltpu.VMEM((kinds * col_count, 2 * col_count), jnp.bfloat16),
            pltpu.VMEM((kinds, row_count, col_count), jnp.bfloat16),
            pltpu.VMEM((row_count, col_count), jnp.float32),
            pltpu.VMEM(half, jnp.float32),
            pltpu.VMEM(half, jnp.float32),
            pltpu.VMEM(half, jnp.float32),
            pltpu.VMEM(half, jnp.float32),
            homeward,
            homeward,
            pltpu.SemaphoreType.DMA((9,)),
            pltpu.SemaphoreType.DMA((2,)),
            pltpu.SemaphoreType.DMA((2,)),
        ],
        compiler_params=pltpu.CompilerParams(
            collective_id=0, has_side_effects=True, vmem_limit_bytes=VMEM_GRANT
        ),
    )(block_index, bond_map, bond_strength, drive_amplitude, amplitudes, couplings)


def chosen_body(sizes, amplitudes, couplings, block_index, *rest):
    row_count = amplitudes.shape[1]
    devices = sizes[0] * sizes[1]
    block_rows = row_count // block_index.shape[0]
    if row_count % devices == 0 and block_rows % (row_count // devices) == 0:
        return body_by_rows(sizes, amplitudes, couplings, block_index, *rest)
    return body(amplitudes, couplings, block_index, *rest)


def solution(mesh):
    in_specs = (P(None, ("grp", "dev"), None), P(), P(("grp", "dev")), P(), P(), P())
    out_specs = P(None, ("grp", "dev"), None)
    sizes = (mesh.shape["grp"], mesh.shape["dev"])
    return jax.shard_map(
        functools.partial(chosen_body, sizes),
        mesh=mesh,
        in_specs=in_specs,
        out_specs=out_specs,
        check_vma=False,
    )
```

```python
import functools

import jax
import jax.numpy as jnp
from jax import lax
from jax.experimental import pallas as pl
from jax.experimental.pallas import tpu as pltpu
from jax.sharding import PartitionSpec as P

BROWS = 16


STEP_SIZE = 0.5
HIGHEST = lax.Precision.HIGHEST


def swapped(shard, axis, distance):
    return lax.ppermute(shard, axis, [(i, i ^ 1 << distance) for i in range(lax.axis_size(axis))])


def spin_count(number):
    return number.bit_length() - 1


def flip_group(real_part, imag_part, bit_now):
    return swapped((real_part, imag_part), "grp", bit_now)


def coupled(real_part, imag_part, table, row_kind, kinds):
    row_count, col_count = real_part.shape
    product = jnp.dot(
        jnp.concatenate([real_part, imag_part], 0),
        table,
        precision=HIGHEST,
        preferred_element_type=jnp.float32,
    )
    extent = kinds * col_count
    left_part = product[:, :extent]
    right_part = product[:, extent:]
    all_real = left_part[:row_count] - right_part[row_count:]
    all_imag = left_part[row_count:] + right_part[:row_count]
    select = (row_kind[:, None] == jnp.arange(kinds, dtype=jnp.int32)[None, :]).astype(jnp.float32)[
        :, :, None
    ]
    out_real = jnp.sum(all_real.reshape(row_count, kinds, col_count) * select, axis=1)
    out_imag = jnp.sum(all_imag.reshape(row_count, kinds, col_count) * select, axis=1)
    return (out_real, out_imag)


def evaluate_field(
    real_part, imag_part, table, row_kind, kinds, bond_map, bond_strength, drive_row
):
    out_real, out_imag = coupled(real_part, imag_part, table, row_kind, kinds)
    row_count, col_count = real_part.shape
    dev_bits = spin_count(lax.axis_size("dev"))
    grp_bits = spin_count(lax.axis_size("grp"))
    columns = jnp.arange(col_count, dtype=jnp.int32)
    for lead_spin in range(dev_bits + grp_bits):
        target = bond_map[lead_spin]
        shuffle = jnp.bitwise_xor(columns, jnp.left_shift(jnp.int32(1), target))
        sign_col = (1 - 2 * jnp.bitwise_and(jnp.right_shift(columns, target), 1)).astype(
            jnp.float32
        )[None, :]
        if lead_spin < dev_bits:
            part_real, part_imag = swapped((real_part, imag_part), "dev", lead_spin)
            sign_lead = (
                1 - 2 * jnp.bitwise_and(jnp.right_shift(lax.axis_index("dev"), lead_spin), 1)
            ).astype(jnp.float32)
        else:
            part_real, part_imag = flip_group(real_part, imag_part, lead_spin - dev_bits)
            sign_lead = (
                1
                - 2
                * jnp.bitwise_and(jnp.right_shift(lax.axis_index("grp"), lead_spin - dev_bits), 1)
            ).astype(jnp.float32)
        strength = bond_strength[lead_spin]
        drive_now = drive_row[lead_spin]
        out_real = (
            out_real
            + strength * (sign_lead * sign_col * real_part + jnp.take(part_real, shuffle, axis=1))
            + drive_now * part_real
        )
        out_imag = (
            out_imag
            + strength * (sign_lead * sign_col * imag_part + jnp.take(part_imag, shuffle, axis=1))
            + drive_now * part_imag
        )
    return (out_imag, -out_real)


def runge_kutta(real_part, imag_part, evaluate):
    half_step = 0.5 * STEP_SIZE
    slope_one = evaluate(0, real_part, imag_part)
    slope_two = evaluate(
        1, real_part + half_step * slope_one[0], imag_part + half_step * slope_one[1]
    )
    slope_three = evaluate(
        2, real_part + half_step * slope_two[0], imag_part + half_step * slope_two[1]
    )
    slope_four = evaluate(
        3, real_part + STEP_SIZE * slope_three[0], imag_part + STEP_SIZE * slope_three[1]
    )
    factor = STEP_SIZE / 6.0
    new_real = real_part + factor * (
        slope_one[0] + 2.0 * slope_two[0] + 2.0 * slope_three[0] + slope_four[0]
    )
    new_imag = imag_part + factor * (
        slope_one[1] + 2.0 * slope_two[1] + 2.0 * slope_three[1] + slope_four[1]
    )
    return (new_real, new_imag)


def body(amplitudes, couplings, block_index, bond_map, bond_strength, drive_amplitude):
    kinds = couplings.shape[1]
    col_count = couplings.shape[2]
    table_real = jnp.transpose(couplings[0], (2, 0, 1)).reshape(col_count, kinds * col_count)
    table_imag = jnp.transpose(couplings[1], (2, 0, 1)).reshape(col_count, kinds * col_count)
    table = jnp.concatenate([table_real, table_imag], 1)
    real_part = amplitudes[0]
    imag_part = amplitudes[1]
    row_count = real_part.shape[0]
    row_kind = jnp.repeat(block_index, BROWS, total_repeat_length=row_count)

    def evaluate(section, first, second):
        return evaluate_field(
            first, second, table, row_kind, kinds, bond_map, bond_strength, drive_amplitude[section]
        )

    new_real, new_imag = runge_kutta(real_part, imag_part, evaluate)
    return jnp.stack([new_real, new_imag])


SUBLANES = 8
VMEM_GRANT = 64 * 2**20 - 2**18
MESH = pl.DeviceIdType.MESH


def flipped(field, stride):
    row_count, col_count = field.shape
    if stride >= SUBLANES:
        folded = field.reshape(row_count // (2 * stride), 2, stride, col_count)
        return jnp.concatenate([folded[:, 1:], folded[:, :1]], 1).reshape(row_count, col_count)
    tiles = field.reshape(row_count // SUBLANES, SUBLANES, col_count)
    down = pltpu.roll(tiles, stride, 1)
    if 2 * stride < SUBLANES:
        row = lax.broadcasted_iota(jnp.int32, tiles.shape, 1)
        up = pltpu.roll(tiles, SUBLANES - stride, 1)
        down = jnp.where(row // stride % 2 == 1, down, up)
    return down.reshape(row_count, col_count)


def mixed_order(count):
    order = [0]
    while len(order) < count:
        order = [2 * place for place in order] + [2 * place + 1 for place in order]
    return order


def step_kernel(
    sizes,
    kind_hbm,
    bond_hbm,
    strength_hbm,
    drive_hbm,
    amp_ref,
    coup_ref,
    out_ref,
    kind_ref,
    bond_ref,
    strength_ref,
    drive_ref,
    stage,
    held,
    table,
    weight_high,
    weight_low,
    masks,
    diagonal,
    field,
    total,
    final,
    psi,
    back,
    landed,
    local_sem,
    send_sem,
    recv_sem,
):
    grp_size, dev_size, block_rows = sizes
    devices = grp_size * dev_size
    lead = spin_count(devices)
    parts, row_count, col_count = amp_ref.shape
    kinds = coup_ref.shape[1]
    sections = drive_ref.shape[0]
    share = row_count // devices
    planes = parts * share
    grp, dev = lax.axis_index("grp"), lax.axis_index("dev")
    me = grp * dev_size + dev
    grps = [grp] + [lax.rem(grp + hop, grp_size) for hop in range(1, grp_size)]
    devs = [dev] + [lax.rem(dev + hop, dev_size) for hop in range(1, dev_size)]
    hops = mixed_order(dev_size)
    others = [
        (grps[grp_hop] * dev_size + devs[dev_hop], (grps[grp_hop], devs[dev_hop]))
        for grp_hop in reversed(range(grp_size))
        for dev_hop in hops
        if grp_hop + dev_hop > 0
    ]
    loads = [
        pltpu.make_async_copy(source, target, local_sem.at[3 + index])
        for index, (source, target) in enumerate(
            (
                (kind_hbm, kind_ref),
                (amp_ref, final),
                (coup_ref, table),
                (bond_hbm, bond_ref),
                (strength_hbm, strength_ref),
                (drive_hbm, drive_ref),
            )
        )
    ]
    for load in loads[:2]:
        load.start()
    barrier = pltpu.get_barrier_semaphore()

    for _, where in others:
        pl.semaphore_signal(barrier, inc=1, device_id=where, device_id_type=MESH)
    for load in loads[2:]:
        load.start()
    loads[0].wait()
    owner = lax.broadcasted_iota(jnp.int32, (devices, col_count), 0) * share // block_rows
    kind_rows = jnp.zeros((devices, col_count), jnp.float32)
    for block in range(row_count // block_rows):
        kind_rows = jnp.where(owner == block, kind_ref[block].astype(jnp.float32), kind_rows)
    stage[pl.ds(planes, devices, stride=planes + 1), :] = kind_rows
    loads[1].wait()
    for part in range(parts):
        for spot in range(share):
            stage[pl.ds(part * share + spot, devices, stride=planes + 1), :] = final[
                part, pl.ds(spot, devices, stride=share), :
            ]
    pl.semaphore_wait(barrier, devices - 1)

    def exchange(source, target, phase):
        width = source.shape[0] // devices
        mine = pl.ds(me * width, width)
        for other, where in others:
            pltpu.make_async_remote_copy(
                src_ref=source.at[pl.ds(other * width, width)],
                dst_ref=target.at[mine],
                send_sem=send_sem.at[phase],
                recv_sem=recv_sem.at[phase],
                device_id=where,
                device_id_type=MESH,
            ).start()
        own = pltpu.make_async_copy(source.at[mine], target.at[mine], local_sem.at[phase])
        own.start()
        return own

    def finish(source, target, phase, own):
        own.wait()
        foreign = pl.ds(0, source.shape[0] // devices * (devices - 1))
        sent = source.at[foreign]
        pltpu.make_async_copy(sent, sent, send_sem.at[phase]).wait()
        came = target.at[foreign]
        pltpu.make_async_copy(came, came, recv_sem.at[phase]).wait()

    own = exchange(stage, held, 0)
    for load in loads[2:]:
        load.wait()

    def split(kind, carry):
        rows = pl.ds(pl.multiple_of(kind * col_count, col_count), col_count)
        for part in range(2):
            columns = slice(part * col_count, (part + 1) * col_count)
            full = table[part, kind]
            high = full.astype(jnp.bfloat16)
            weight_high[rows, columns] = high
            weight_low[rows, columns] = (full - high.astype(jnp.float32)).astype(jnp.bfloat16)
        return carry

    lax.fori_loop(0, kinds, split, 0)

    row = lax.broadcasted_iota(jnp.int32, (row_count, col_count), 0)
    column = lax.broadcasted_iota(jnp.int32, (row_count, col_count), 1)
    diag = jnp.zeros((row_count, col_count), jnp.float32)
    shuffles = []
    for spin in range(lead):
        target = bond_ref[spin]
        shuffles.append(jnp.bitwise_xor(column, jnp.left_shift(jnp.int32(1), target)))
        parity = jnp.bitwise_xor(
            jnp.right_shift(row % devices, spin), jnp.right_shift(column, target)
        )
        sign = (1 - 2 * jnp.bitwise_and(parity, 1)).astype(jnp.float32)
        diag = diag + strength_ref[spin] * sign
    diagonal[...] = diag

    finish(stage, held, 0, own)
    kind_now = held[pl.ds(planes, devices, stride=planes + 1), :]
    kind_now = jnp.concatenate([kind_now] * share, 0)
    for kind in range(kinds):
        masks[kind] = (kind_now == float(kind)).astype(jnp.float32).astype(jnp.bfloat16)
    for part in range(parts):
        for spot in range(share):
            came = held[pl.ds(part * share + spot, devices, stride=planes + 1), :]
            rows = slice(spot * devices, (spot + 1) * devices)
            psi[part, rows] = came
            field[part, rows] = came
    total[...] = jnp.zeros_like(total)

    def section(now):
        both = jnp.concatenate([field[0], field[1]], 0)
        high = both.astype(jnp.bfloat16)
        low = (both - high.astype(jnp.float32)).astype(jnp.bfloat16)
        high_parts = []
        low_parts = []
        for kind in range(kinds):
            mask = jnp.concatenate([masks[kind], masks[kind]], 0)
            high_parts.append(high * mask)
            low_parts.append(low * mask)
        high_all = jnp.concatenate(high_parts, 1)
        low_all = jnp.concatenate(low_parts, 1)
        main = jnp.dot(
            jnp.concatenate([high_all, low_all], 0),
            weight_high[...],
            preferred_element_type=jnp.float32,
        )
        rest = jnp.dot(high_all, weight_low[...], preferred_element_type=jnp.float32)
        product = main[: 2 * row_count] + (main[2 * row_count :] + rest)
        from_real, from_imag = product[:row_count], product[row_count:]
        column_real = from_imag[:, :col_count] - from_real[:, col_count:]
        column_imag = -from_real[:, :col_count] - from_imag[:, col_count:]
        leads = []
        for part in range(2):
            here = field[part]
            other = diagonal[...] * here
            for spin in range(lead):
                there = flipped(here, 1 << spin)
                moved = jnp.take_along_axis(
                    there, shuffles[spin], axis=1, mode="promise_in_bounds"
                )
                other = other + strength_ref[spin] * moved + drive_ref[now, spin] * there
            leads.append(other)
        slope = (column_real + leads[1], column_imag - leads[0])
        weight = 1.0 if now in (0, sections - 1) else 2.0
        step = STEP_SIZE if now == sections - 2 else 0.5 * STEP_SIZE
        for part in range(2):
            total[part] = total[part] + weight * slope[part]
            field[part] = psi[part] + step * slope[part]

    for now in range(sections):
        section(now)
    final[...] = psi[...] + (STEP_SIZE / 6.0) * total[...]
    for part in range(parts):
        for spot in range(share):
            back[pl.ds(part * share + spot, devices, stride=planes), :] = final[
                part, spot * devices : (spot + 1) * devices
            ]
    own = exchange(back, landed, 1)
    finish(back, landed, 1, own)
    for part in range(parts):
        for spot in range(share):
            out_ref[part, pl.ds(spot, devices, stride=share), :] = landed[
                pl.ds(part * share + spot, devices, stride=planes), :
            ]


def body_by_rows(
    sizes, amplitudes, couplings, block_index, bond_map, bond_strength, drive_amplitude
):
    parts, row_count, col_count = amplitudes.shape
    kinds = couplings.shape[1]
    block_rows = row_count // block_index.shape[0]
    half = (parts, row_count, col_count)
    weight = pltpu.VMEM((kinds * col_count, 2 * col_count), jnp.bfloat16)
    homeward = pltpu.VMEM((parts * row_count, col_count), jnp.float32)
    outward = pltpu.VMEM((parts * row_count + sizes[0] * sizes[1], col_count), jnp.float32)
    return pl.pallas_call(
        functools.partial(step_kernel, (*sizes, block_rows)),
        out_shape=pltpu.VMEM(half, jnp.float32),
        in_specs=[pl.BlockSpec(memory_space=pltpu.HBM)] * 6,
        out_specs=pl.BlockSpec(memory_space=pltpu.VMEM),
        scratch_shapes=[
            pltpu.SMEM(block_index.shape, jnp.int32),
            pltpu.SMEM(bond_map.shape, jnp.int32),
            pltpu.SMEM(bond_strength.shape, jnp.float32),
            pltpu.SMEM(drive_amplitude.shape, jnp.float32),
            outward,
            outward,
            pltpu.VMEM(couplings.shape, jnp.float32),
            weight,
            weight,
            pltpu.VMEM((kinds, row_count, col_count), jnp.bfloat16),
            pltpu.VMEM((row_count, col_count), jnp.float32),
            pltpu.VMEM(half, jnp.float32),
            pltpu.VMEM(half, jnp.float32),
            pltpu.VMEM(half, jnp.float32),
            pltpu.VMEM(half, jnp.float32),
            homeward,
            homeward,
            pltpu.SemaphoreType.DMA((9,)),
            pltpu.SemaphoreType.DMA((2,)),
            pltpu.SemaphoreType.DMA((2,)),
        ],
        compiler_params=pltpu.CompilerParams(
            collective_id=0, has_side_effects=True, vmem_limit_bytes=VMEM_GRANT
        ),
    )(block_index, bond_map, bond_strength, drive_amplitude, amplitudes, couplings)


def chosen_body(sizes, amplitudes, couplings, block_index, *rest):
    row_count = amplitudes.shape[1]
    devices = sizes[0] * sizes[1]
    block_rows = row_count // block_index.shape[0]
    if row_count % devices == 0 and block_rows % (row_count // devices) == 0:
        return body_by_rows(sizes, amplitudes, couplings, block_index, *rest)
    return body(amplitudes, couplings, block_index, *rest)


def solution(mesh):
    in_specs = (P(None, ("grp", "dev"), None), P(), P(("grp", "dev")), P(), P(), P())
    out_specs = P(None, ("grp", "dev"), None)
    sizes = (mesh.shape["grp"], mesh.shape["dev"])
    return jax.shard_map(
        functools.partial(chosen_body, sizes),
        mesh=mesh,
        in_specs=in_specs,
        out_specs=out_specs,
        check_vma=False,
    )
```

```python
import functools

import jax
import jax.numpy as jnp
from jax import lax
from jax.experimental import pallas as pl
from jax.experimental.pallas import tpu as pltpu
from jax.sharding import PartitionSpec as P

BROWS = 16


STEP_SIZE = 0.5
HIGHEST = lax.Precision.HIGHEST


def swapped(shard, axis, distance):
    return lax.ppermute(shard, axis, [(i, i ^ 1 << distance) for i in range(lax.axis_size(axis))])


def spin_count(number):
    return number.bit_length() - 1


def flip_group(real_part, imag_part, bit_now):
    return swapped((real_part, imag_part), "grp", bit_now)


def coupled(real_part, imag_part, table, row_kind, kinds):
    row_count, col_count = real_part.shape
    product = jnp.dot(
        jnp.concatenate([real_part, imag_part], 0),
        table,
        precision=HIGHEST,
        preferred_element_type=jnp.float32,
    )
    extent = kinds * col_count
    left_part = product[:, :extent]
    right_part = product[:, extent:]
    all_real = left_part[:row_count] - right_part[row_count:]
    all_imag = left_part[row_count:] + right_part[:row_count]
    select = (row_kind[:, None] == jnp.arange(kinds, dtype=jnp.int32)[None, :]).astype(jnp.float32)[
        :, :, None
    ]
    out_real = jnp.sum(all_real.reshape(row_count, kinds, col_count) * select, axis=1)
    out_imag = jnp.sum(all_imag.reshape(row_count, kinds, col_count) * select, axis=1)
    return (out_real, out_imag)


def evaluate_field(
    real_part, imag_part, table, row_kind, kinds, bond_map, bond_strength, drive_row
):
    out_real, out_imag = coupled(real_part, imag_part, table, row_kind, kinds)
    row_count, col_count = real_part.shape
    dev_bits = spin_count(lax.axis_size("dev"))
    grp_bits = spin_count(lax.axis_size("grp"))
    columns = jnp.arange(col_count, dtype=jnp.int32)
    for lead_spin in range(dev_bits + grp_bits):
        target = bond_map[lead_spin]
        shuffle = jnp.bitwise_xor(columns, jnp.left_shift(jnp.int32(1), target))
        sign_col = (1 - 2 * jnp.bitwise_and(jnp.right_shift(columns, target), 1)).astype(
            jnp.float32
        )[None, :]
        if lead_spin < dev_bits:
            part_real, part_imag = swapped((real_part, imag_part), "dev", lead_spin)
            sign_lead = (
                1 - 2 * jnp.bitwise_and(jnp.right_shift(lax.axis_index("dev"), lead_spin), 1)
            ).astype(jnp.float32)
        else:
            part_real, part_imag = flip_group(real_part, imag_part, lead_spin - dev_bits)
            sign_lead = (
                1
                - 2
                * jnp.bitwise_and(jnp.right_shift(lax.axis_index("grp"), lead_spin - dev_bits), 1)
            ).astype(jnp.float32)
        strength = bond_strength[lead_spin]
        drive_now = drive_row[lead_spin]
        out_real = (
            out_real
            + strength * (sign_lead * sign_col * real_part + jnp.take(part_real, shuffle, axis=1))
            + drive_now * part_real
        )
        out_imag = (
            out_imag
            + strength * (sign_lead * sign_col * imag_part + jnp.take(part_imag, shuffle, axis=1))
            + drive_now * part_imag
        )
    return (out_imag, -out_real)


def runge_kutta(real_part, imag_part, evaluate):
    half_step = 0.5 * STEP_SIZE
    slope_one = evaluate(0, real_part, imag_part)
    slope_two = evaluate(
        1, real_part + half_step * slope_one[0], imag_part + half_step * slope_one[1]
    )
    slope_three = evaluate(
        2, real_part + half_step * slope_two[0], imag_part + half_step * slope_two[1]
    )
    slope_four = evaluate(
        3, real_part + STEP_SIZE * slope_three[0], imag_part + STEP_SIZE * slope_three[1]
    )
    factor = STEP_SIZE / 6.0
    new_real = real_part + factor * (
        slope_one[0] + 2.0 * slope_two[0] + 2.0 * slope_three[0] + slope_four[0]
    )
    new_imag = imag_part + factor * (
        slope_one[1] + 2.0 * slope_two[1] + 2.0 * slope_three[1] + slope_four[1]
    )
    return (new_real, new_imag)


def body(amplitudes, couplings, block_index, bond_map, bond_strength, drive_amplitude):
    kinds = couplings.shape[1]
    col_count = couplings.shape[2]
    table_real = jnp.transpose(couplings[0], (2, 0, 1)).reshape(col_count, kinds * col_count)
    table_imag = jnp.transpose(couplings[1], (2, 0, 1)).reshape(col_count, kinds * col_count)
    table = jnp.concatenate([table_real, table_imag], 1)
    real_part = amplitudes[0]
    imag_part = amplitudes[1]
    row_count = real_part.shape[0]
    row_kind = jnp.repeat(block_index, BROWS, total_repeat_length=row_count)

    def evaluate(section, first, second):
        return evaluate_field(
            first, second, table, row_kind, kinds, bond_map, bond_strength, drive_amplitude[section]
        )

    new_real, new_imag = runge_kutta(real_part, imag_part, evaluate)
    return jnp.stack([new_real, new_imag])


SUBLANES = 8
VMEM_GRANT = 64 * 2**20 - 2**18
MESH = pl.DeviceIdType.MESH


def flipped(field, stride):
    row_count, col_count = field.shape
    if stride >= SUBLANES:
        folded = field.reshape(row_count // (2 * stride), 2, stride, col_count)
        return jnp.concatenate([folded[:, 1:], folded[:, :1]], 1).reshape(row_count, col_count)
    tiles = field.reshape(row_count // SUBLANES, SUBLANES, col_count)
    down = pltpu.roll(tiles, stride, 1)
    if 2 * stride < SUBLANES:
        row = lax.broadcasted_iota(jnp.int32, tiles.shape, 1)
        up = pltpu.roll(tiles, SUBLANES - stride, 1)
        down = jnp.where(row // stride % 2 == 1, down, up)
    return down.reshape(row_count, col_count)


def mixed_order(count):
    order = [0]
    while len(order) < count:
        order = [2 * place for place in order] + [2 * place + 1 for place in order]
    return order


def step_kernel(
    sizes,
    kind_hbm,
    bond_hbm,
    strength_hbm,
    drive_hbm,
    amp_ref,
    coup_ref,
    out_ref,
    kind_ref,
    bond_ref,
    strength_ref,
    drive_ref,
    stage,
    held,
    table,
    weight_high,
    weight_low,
    masks,
    diagonal,
    field,
    total,
    final,
    psi,
    back,
    landed,
    local_sem,
    send_sem,
    recv_sem,
):
    grp_size, dev_size, block_rows = sizes
    devices = grp_size * dev_size
    lead = spin_count(devices)
    parts, row_count, col_count = amp_ref.shape
    kinds = coup_ref.shape[1]
    sections = drive_ref.shape[0]
    share = row_count // devices
    planes = parts * share
    grp, dev = lax.axis_index("grp"), lax.axis_index("dev")
    me = grp * dev_size + dev
    devs = [dev] + [lax.rem(dev + hop, dev_size) for hop in range(1, dev_size)]

    def for_others(action):
        def visit(there, skipped):
            for dev_hop in mixed_order(dev_size):
                if dev_hop >= skipped:
                    where = (there, devs[dev_hop])
                    action(where[0] * dev_size + where[1], where)

        def visit_group(hop, carry):
            visit(lax.rem(grp + hop, grp_size), 0)
            return carry

        lax.fori_loop(1, grp_size, visit_group, 0)
        visit(grp, 1)

    loads = [
        pltpu.make_async_copy(source, target, local_sem.at[3 + index])
        for index, (source, target) in enumerate(
            (
                (kind_hbm, kind_ref),
                (amp_ref, final),
                (coup_ref, table),
                (bond_hbm, bond_ref),
                (strength_hbm, strength_ref),
                (drive_hbm, drive_ref),
            )
        )
    ]
    for load in loads[:2]:
        load.start()
    barrier = pltpu.get_barrier_semaphore()

    for_others(
        lambda _, where: pl.semaphore_signal(
            barrier, inc=1, device_id=where, device_id_type=MESH
        )
    )
    for load in loads[2:]:
        load.start()
    loads[0].wait()
    owner = lax.broadcasted_iota(jnp.int32, (devices, col_count), 0) * share // block_rows
    kind_rows = jnp.zeros((devices, col_count), jnp.float32)
    for block in range(row_count // block_rows):
        kind_rows = jnp.where(owner == block, kind_ref[block].astype(jnp.float32), kind_rows)
    stage[pl.ds(planes, devices, stride=planes + 1), :] = kind_rows
    loads[1].wait()
    for part in range(parts):
        for spot in range(share):
            stage[pl.ds(part * share + spot, devices, stride=planes + 1), :] = final[
                part, pl.ds(spot, devices, stride=share), :
            ]
    pl.semaphore_wait(barrier, devices - 1)

    def exchange(source, target, phase):
        width = source.shape[0] // devices
        mine = pl.ds(me * width, width)

        def send(other, where):
            pltpu.make_async_remote_copy(
                src_ref=source.at[pl.ds(other * width, width)],
                dst_ref=target.at[mine],
                send_sem=send_sem.at[phase],
                recv_sem=recv_sem.at[phase],
                device_id=where,
                device_id_type=MESH,
            ).start()

        for_others(send)
        own = pltpu.make_async_copy(source.at[mine], target.at[mine], local_sem.at[phase])
        own.start()
        return own

    def finish(source, target, phase, own):
        own.wait()
        foreign = pl.ds(0, source.shape[0] // devices * (devices - 1))
        sent = source.at[foreign]
        pltpu.make_async_copy(sent, sent, send_sem.at[phase]).wait()
        came = target.at[foreign]
        pltpu.make_async_copy(came, came, recv_sem.at[phase]).wait()

    own = exchange(stage, held, 0)
    for load in loads[2:]:
        load.wait()

    def split(kind, carry):
        rows = pl.ds(pl.multiple_of(kind * col_count, col_count), col_count)
        for part in range(2):
            columns = slice(part * col_count, (part + 1) * col_count)
            full = table[part, kind]
            high = full.astype(jnp.bfloat16)
            weight_high[rows, columns] = high
            weight_low[rows, columns] = (full - high.astype(jnp.float32)).astype(jnp.bfloat16)
        return carry

    lax.fori_loop(0, kinds, split, 0)

    row = lax.broadcasted_iota(jnp.int32, (row_count, col_count), 0)
    column = lax.broadcasted_iota(jnp.int32, (row_count, col_count), 1)
    diag = jnp.zeros((row_count, col_count), jnp.float32)
    shuffles = []
    for spin in range(lead):
        target = bond_ref[spin]
        shuffles.append(jnp.bitwise_xor(column, jnp.left_shift(jnp.int32(1), target)))
        parity = jnp.bitwise_xor(
            jnp.right_shift(row % devices, spin), jnp.right_shift(column, target)
        )
        sign = (1 - 2 * jnp.bitwise_and(parity, 1)).astype(jnp.float32)
        diag = diag + strength_ref[spin] * sign
    diagonal[...] = diag

    finish(stage, held, 0, own)
    kind_now = held[pl.ds(planes, devices, stride=planes + 1), :]
    kind_now = jnp.concatenate([kind_now] * share, 0)
    for kind in range(kinds):
        masks[kind] = (kind_now == float(kind)).astype(jnp.float32).astype(jnp.bfloat16)
    for part in range(parts):
        for spot in range(share):
            came = held[pl.ds(part * share + spot, devices, stride=planes + 1), :]
            rows = slice(spot * devices, (spot + 1) * devices)
            psi[part, rows] = came
            field[part, rows] = came
    total[...] = jnp.zeros_like(total)

    def section(now, carry):
        both = jnp.concatenate([field[0], field[1]], 0)
        high = both.astype(jnp.bfloat16)
        low = (both - high.astype(jnp.float32)).astype(jnp.bfloat16)
        high_parts = []
        low_parts = []
        for kind in range(kinds):
            mask = jnp.concatenate([masks[kind], masks[kind]], 0)
            high_parts.append(high * mask)
            low_parts.append(low * mask)
        high_all = jnp.concatenate(high_parts, 1)
        low_all = jnp.concatenate(low_parts, 1)
        main = jnp.dot(
            jnp.concatenate([high_all, low_all], 0),
            weight_high[...],
            preferred_element_type=jnp.float32,
        )
        rest = jnp.dot(high_all, weight_low[...], preferred_element_type=jnp.float32)
        product = main[: 2 * row_count] + (main[2 * row_count :] + rest)
        from_real, from_imag = product[:row_count], product[row_count:]
        column_real = from_imag[:, :col_count] - from_real[:, col_count:]
        column_imag = -from_real[:, :col_count] - from_imag[:, col_count:]
        leads = []
        for part in range(2):
            here = field[part]
            other = diagonal[...] * here
            for spin in range(lead):
                there = flipped(here, 1 << spin)
                moved = jnp.take_along_axis(
                    there, shuffles[spin], axis=1, mode="promise_in_bounds"
                )
                other = other + strength_ref[spin] * moved + drive_ref[now, spin] * there
            leads.append(other)
        slope = (column_real + leads[1], column_imag - leads[0])
        edge = (now == 0) | (now == sections - 1)
        weight = jnp.where(edge, 1.0, 2.0)
        step = jnp.where(now == sections - 2, STEP_SIZE, 0.5 * STEP_SIZE)
        for part in range(2):
            total[part] = total[part] + weight * slope[part]
            field[part] = psi[part] + step * slope[part]
        return carry

    lax.fori_loop(0, sections, section, 0)
    final[...] = psi[...] + (STEP_SIZE / 6.0) * total[...]
    for part in range(parts):
        for spot in range(share):
            back[pl.ds(part * share + spot, devices, stride=planes), :] = final[
                part, spot * devices : (spot + 1) * devices
            ]
    own = exchange(back, landed, 1)
    finish(back, landed, 1, own)
    for part in range(parts):
        for spot in range(share):
            out_ref[part, pl.ds(spot, devices, stride=share), :] = landed[
                pl.ds(part * share + spot, devices, stride=planes), :
            ]


def body_by_rows(
    sizes, amplitudes, couplings, block_index, bond_map, bond_strength, drive_amplitude
):
    parts, row_count, col_count = amplitudes.shape
    kinds = couplings.shape[1]
    block_rows = row_count // block_index.shape[0]
    half = (parts, row_count, col_count)
    weight = pltpu.VMEM((kinds * col_count, 2 * col_count), jnp.bfloat16)
    homeward = pltpu.VMEM((parts * row_count, col_count), jnp.float32)
    outward = pltpu.VMEM((parts * row_count + sizes[0] * sizes[1], col_count), jnp.float32)
    return pl.pallas_call(
        functools.partial(step_kernel, (*sizes, block_rows)),
        out_shape=pltpu.VMEM(half, jnp.float32),
        in_specs=[pl.BlockSpec(memory_space=pltpu.HBM)] * 6,
        out_specs=pl.BlockSpec(memory_space=pltpu.VMEM),
        scratch_shapes=[
            pltpu.SMEM(block_index.shape, jnp.int32),
            pltpu.SMEM(bond_map.shape, jnp.int32),
            pltpu.SMEM(bond_strength.shape, jnp.float32),
            pltpu.SMEM(drive_amplitude.shape, jnp.float32),
            outward,
            outward,
            pltpu.VMEM(couplings.shape, jnp.float32),
            weight,
            weight,
            pltpu.VMEM((kinds, row_count, col_count), jnp.bfloat16),
            pltpu.VMEM((row_count, col_count), jnp.float32),
            pltpu.VMEM(half, jnp.float32),
            pltpu.VMEM(half, jnp.float32),
            pltpu.VMEM(half, jnp.float32),
            pltpu.VMEM(half, jnp.float32),
            homeward,
            homeward,
            pltpu.SemaphoreType.DMA((9,)),
            pltpu.SemaphoreType.DMA((2,)),
            pltpu.SemaphoreType.DMA((2,)),
        ],
        compiler_params=pltpu.CompilerParams(
            collective_id=0, has_side_effects=True, vmem_limit_bytes=VMEM_GRANT
        ),
    )(block_index, bond_map, bond_strength, drive_amplitude, amplitudes, couplings)


def chosen_body(sizes, amplitudes, couplings, block_index, *rest):
    row_count = amplitudes.shape[1]
    devices = sizes[0] * sizes[1]
    block_rows = row_count // block_index.shape[0]
    if row_count % devices == 0 and block_rows % (row_count // devices) == 0:
        return body_by_rows(sizes, amplitudes, couplings, block_index, *rest)
    return body(amplitudes, couplings, block_index, *rest)


def solution(mesh):
    in_specs = (P(None, ("grp", "dev"), None), P(), P(("grp", "dev")), P(), P(), P())
    out_specs = P(None, ("grp", "dev"), None)
    sizes = (mesh.shape["grp"], mesh.shape["dev"])
    return jax.shard_map(
        functools.partial(chosen_body, sizes),
        mesh=mesh,
        in_specs=in_specs,
        out_specs=out_specs,
        check_vma=False,
    )
```
